256 devices in a mesh: slab: 16 (over y, z_lo), row: 2 (over core), col: 8 (over x, z_hi).
Axes of the slice: x: 4, y: 4, z: 8 (z_hi: 2, z_lo: 4; z = z_hi * 4 + z_lo), core: 2. Of those that a mesh axis runs over, the one named last changes fastest.
Arguments:
- pressure: float32 [64, 256, 1024], P('slab', 'row', 'col'), may hold values from -6 to 6
- velocity: float32 [3, 64, 256, 1024], P(None, 'slab', 'row', 'col'), may hold values from -6 to 6
- kappa: float32 [64, 256, 1024], P('slab', 'row', 'col'), may hold values from 0.5 to 2
- drive: float32 [64, 256, 1024], P('slab', 'row', 'col'), may hold values from -6 to 6
- adj_pressure_in: float32 [64, 256, 1024], P('slab', 'row', 'col'), may hold values from -6 to 6
- adj_velocity_in: float32 [3, 64, 256, 1024], P(None, 'slab', 'row', 'col'), may hold values from -6 to 6
- wall_mask: int32 [64, 256, 1024], P('slab', 'row', 'col'), may hold values 0 or 1
- wall_cells: int32 [16, 2, 8, 512], P('slab', 'row', 'col'), may hold values from 0 to 65535
- wall_rows: int32 [16, 2, 8, 512], P('slab', 'row', 'col'), may hold values from 0 to 2047
- slot_angle: float32 [16, 2, 8, 512], P('slab', 'row', 'col'), may hold values from 0 to 64
- wall_count: int32 [16, 2, 8], P('slab', 'row', 'col'), may hold values from 1 to 512, as said below
- step: int32 [1], replicated, may hold values from 0 to 4095
Outputs:
- adj_pressure: float32 [64, 256, 1024], P('slab', 'row', 'col')
- adj_velocity: float32 [3, 64, 256, 1024], P(None, 'slab', 'row', 'col')
- shape_grad: float32 [2048, 64], P(('slab', 'row', 'col'))
The draws below stay inside these ranges and needn't reach their ends.
Inputs may be any that keep to these rules, and one draw needn't show every extreme that they name: `wall_count`: some device has all 512 slots live in every draw.
All inputs are finite; a program needn't handle non-finite values. No bound on the sum of `wall_mask` on one device may be relied on, other than what follows from the above.
Results may differ from the reference program's by a relative error of at most 0.00002.
Values sent between devices are 32-bit elements; how exact they have to be, the bound alone decides.
A program may use at most 64 MiB of HBM per device.

```python
import math
import jax
import jax.numpy as jnp
from jax import lax

CX = 4
CY = 128
CZ = 128
WALL = 512
NROWS = 2048
ANG = 64
NX = 64
NY = 256
NZ = 1024
N_SLAB = 16
N_ROW = 2
N_COL = 8


def draw_wall_count(key, part):
    base = jax.random.randint(jax.random.fold_in(key, 1), (N_SLAB, N_ROW, N_COL), 0, WALL, dtype=jnp.int32)
    slab_ids = jnp.arange(N_SLAB, dtype=jnp.int32)[:, None, None] + 1
    counts = 1 + base * slab_ids // N_SLAB
    picked = jax.random.randint(jax.random.fold_in(key, 2), (), 0, N_SLAB * N_ROW * N_COL, dtype=jnp.int32)
    flat = counts.reshape(-1)
    flat = jnp.where(jnp.arange(flat.shape[0], dtype=jnp.int32) == picked, WALL, flat)
    return flat.reshape((N_SLAB, N_ROW, N_COL))


def set_ends(array, key, smallest, top_value):
    longest = array.shape.index(max(array.shape))
    spots = []
    for shift in (0, 1):
        where = [jax.random.randint(jax.random.fold_in(key, axis), (), 0, length) for axis, length in enumerate(array.shape)]
        where[longest] = (where[longest] + shift) % array.shape[longest]
        spots.append(tuple(where))
    return array.at[spots[0]].set(smallest).at[spots[1]].set(top_value)


def level_of(own_key, dims, cuts, smallest, high):
    def one(axis_at, blocks):
        steps = jax.random.uniform(jax.random.fold_in(jax.random.fold_in(own_key, 6), axis_at), (blocks,), jnp.float32, smallest / len(cuts), high / len(cuts))
        return jnp.repeat(jnp.exp(steps), dims[axis_at] // blocks).reshape((-1,) + (1,) * (len(dims) - axis_at - 1))

    factor_of = one(*cuts[0])
    for cut in cuts[1:]:
        factor_of = factor_of * one(*cut)
    return factor_of


def noise(rng, extent, scale, most, cuts=(), held_as=jnp.bfloat16):
    drawn = jax.random.normal(rng, extent, jnp.float32) * scale
    if len(cuts) > 0:
        drawn = level_of(rng, extent, cuts, -0.22, 0.18) * drawn
    return jnp.clip(drawn, min=-most, max=most).astype(held_as)


def setup_inputs(seed: int = 0) -> dict:
    key_list = jax.random.split(jax.random.key(seed), 13)
    pressure = noise(key_list[0], (NX, NY, NZ), 1.0, 6.0, ((0, 16), (1, 2), (2, 8)), jnp.float32)
    velocity = noise(key_list[1], (3, NX, NY, NZ), 1.0, 6.0, ((1, 16), (2, 2), (3, 8)), jnp.float32)
    kappa = jnp.clip(jnp.exp(math.log(2.0) - 1.3862944 * jax.random.uniform(key_list[2], (NX, NY, NZ), jnp.float32) ** level_of(key_list[2], (NX, NY, NZ), ((0, 16), (1, 2), (2, 8)), -0.2, 0.2)), 0.5, 2.0)
    drive = noise(key_list[3], (NX, NY, NZ), 1.0, 6.0, ((0, 16), (1, 2), (2, 8)), jnp.float32)
    adj_pressure_in = noise(key_list[4], (NX, NY, NZ), 1.0, 6.0, ((0, 16), (1, 2), (2, 8)), jnp.float32)
    adj_velocity_in = noise(key_list[5], (3, NX, NY, NZ), 1.0, 6.0, ((1, 16), (2, 2), (3, 8)), jnp.float32)
    wall_mask = set_ends((jax.random.randint(key_list[6], (NX, NY, NZ), 0, 8) < 1).astype(jnp.int32), jax.random.fold_in(key_list[6], 1), 0, 1)
    wall_cells = set_ends(jax.random.randint(key_list[7], (N_SLAB, N_ROW, N_COL, WALL), 0, CX * CY * CZ), jax.random.fold_in(key_list[7], 1), 0, (CX * CY * CZ) - 1).astype(jnp.int32)
    wall_rows = set_ends(jax.random.randint(key_list[8], (N_SLAB, N_ROW, N_COL, WALL), 0, NROWS), jax.random.fold_in(key_list[8], 1), 0, NROWS - 1).astype(jnp.int32)
    slot_angle = jnp.clip(64.0 * jax.random.uniform(key_list[9], (N_SLAB, N_ROW, N_COL, WALL), jnp.float32) ** level_of(key_list[9], (N_SLAB, N_ROW, N_COL, WALL), ((0, 16), (1, 2), (2, 8)), -0.2, 0.2), 0.0, 64.0)
    wall_count = draw_wall_count(jax.random.fold_in(key_list[12], 71), 0)
    step = jax.random.randint(key_list[11], (1,), 0, 4096).astype(jnp.int32)
    return {"pressure": pressure, "velocity": velocity, "kappa": kappa, "drive": drive, "adj_pressure_in": adj_pressure_in, "adj_velocity_in": adj_velocity_in, "wall_mask": wall_mask, "wall_cells": wall_cells, "wall_rows": wall_rows, "slot_angle": slot_angle, "wall_count": wall_count, "step": step}


def centered(field, axis):
    widths = [(0, 0), (0, 0), (0, 0)]
    widths[axis] = (1, 1)
    padded = jnp.pad(field, widths)
    size = padded.shape[axis]
    upper = lax.slice_in_dim(padded, 2, size, axis=axis)
    lower = lax.slice_in_dim(padded, 0, size - 2, axis=axis)
    return (upper - lower) * 0.5


def spline_weights(angle):
    knots = jnp.arange(ANG, dtype=jnp.float32)
    dist = jnp.abs(angle[..., None] - knots)
    dist = jnp.minimum(dist, ANG - dist)
    outer = jnp.maximum(2.0 - dist, 0.0)
    inner = jnp.maximum(1.0 - dist, 0.0)
    return (outer * outer * outer - 4.0 * inner * inner * inner) / 6.0


def reference(pressure, velocity, kappa, drive, adj_pressure_in, adj_velocity_in, wall_mask, wall_cells, wall_rows, slot_angle, wall_count, step):
    open_cells = 1.0 - wall_mask.astype(jnp.float32)
    phase = jnp.cos(0.5 * (step[0] % 97).astype(jnp.float32))
    moved = []
    for comp in range(3):
        value = velocity[comp] - 0.3 * centered(pressure, comp)
        if comp == 0:
            value = value + drive * phase
        moved.append(value)
    scaled = kappa * adj_pressure_in
    total = [adj_velocity_in[comp] + centered(scaled, comp) for comp in range(3)]
    lam_u = [open_cells * total[comp] for comp in range(3)]
    divergence = centered(lam_u[0], 0) + centered(lam_u[1], 1) + centered(lam_u[2], 2)
    adj_pressure = adj_pressure_in + 0.3 * divergence
    sens = -(total[0] * moved[0] + total[1] * moved[1] + total[2] * moved[2])
    slab_ids = jnp.arange(N_SLAB, dtype=jnp.int32)[:, None, None, None]
    row_ids = jnp.arange(N_ROW, dtype=jnp.int32)[None, :, None, None]
    col_ids = jnp.arange(N_COL, dtype=jnp.int32)[None, None, :, None]
    glob_x = slab_ids * CX + wall_cells // (CY * CZ)
    glob_y = row_ids * CY + (wall_cells // CZ) % CY
    glob_z = col_ids * CZ + wall_cells % CZ
    values = sens[glob_x, glob_y, glob_z]
    live = jnp.arange(WALL, dtype=jnp.int32) < wall_count[..., None]
    values = jnp.where(live, values, 0.0)
    contrib = values[..., None] * spline_weights(slot_angle)
    shape_grad = jnp.zeros((NROWS, ANG), jnp.float32).at[wall_rows.reshape(-1)].add(contrib.reshape(-1, ANG))
    return adj_pressure, jnp.stack(lam_u), shape_grad
```

```python
import functools

import jax
import jax.numpy as jnp
from jax import lax
from jax.experimental import pallas as pl
from jax.experimental.pallas import tpu as pltpu
from jax.sharding import PartitionSpec as P

ANG = 64
CX = 4
CY = 128
CZ = 128
WALL = 512
OWN = 8
MESH = pl.DeviceIdType.MESH
F32 = jnp.float32
BF16 = jnp.bfloat16


def pieces(value):
    high = value.astype(BF16)
    rest = value - high.astype(F32)
    mid = rest.astype(BF16)
    low = (rest - mid.astype(F32)).astype(BF16)
    return high, mid, low


def kernel(
    ns, nr, nc,
    p_in, v_in, kap_in, drv_in, ap_in, av_in, mask_in, cells_ref, rows_ref, angle_ref, count_ref, step_ref,
    ap_out, av_out, grad_out,
    pp, qq, kap, drv, ap, vel, avel, mask,
    lam0, lam1, lam2, apo,
    zsend, zrecv, lsend, lrecv,
    slots, vals, hot, weight, where_hot, sens_t, dense, parts,
    load_sem, store_sem, halo_send, halo_recv, lam_send, lam_recv,
    slot_send, slot_recv, val_send, val_recv, part_send, part_recv,
):
    nb = nr * nc
    s = lax.axis_index("slab")
    r = lax.axis_index("row")
    c = lax.axis_index("col")
    b = r * nc + c

    def slab_peer(k):
        return (lax.rem(s + k, ns), r, c)

    def block_peer(k):
        other = lax.rem(b + k, nb)
        return (s, lax.div(other, nc), lax.rem(other, nc))

    loads = [
        pltpu.make_async_copy(kap_in, kap, load_sem.at[0]),
        pltpu.make_async_copy(ap_in, ap, load_sem.at[1]),
        pltpu.make_async_copy(p_in, pp.at[pl.ds(1, CX), pl.ds(8, CY)], load_sem.at[2]),
        pltpu.make_async_copy(av_in, avel, load_sem.at[3]),
        pltpu.make_async_copy(mask_in, mask, load_sem.at[4]),
        pltpu.make_async_copy(v_in, vel, load_sem.at[5]),
        pltpu.make_async_copy(drv_in, drv, load_sem.at[6]),
    ]
    for copy in loads:
        copy.start()

    plane = jnp.zeros((CY, CZ), F32)
    for ref in (pp, qq):
        ref[0, pl.ds(8, CY)] = plane
        ref[CX + 1, pl.ds(8, CY)] = plane
        for x in range(CX):
            ref[x + 1, pl.ds(0, 8)] = jnp.zeros((8, CZ), F32)
            ref[x + 1, pl.ds(CY + 8, 8)] = jnp.zeros((8, CZ), F32)
    lam0[0] = plane
    lam0[CX + 1] = plane
    for x in range(CX):
        lam1[x, pl.ds(0, 8)] = jnp.zeros((8, CZ), F32)
        lam1[x, pl.ds(CY + 8, 8)] = jnp.zeros((8, CZ), F32)
    zrecv[...] = jnp.zeros_like(zrecv)
    lrecv[...] = jnp.zeros_like(lrecv)

    barrier = pltpu.get_barrier_semaphore()

    def greet_slab(k, _):
        pl.semaphore_signal(barrier, inc=1, device_id=slab_peer(k), device_id_type=MESH)
        return 0

    def greet_block(k, _):
        pl.semaphore_signal(barrier, inc=1, device_id=block_peer(k), device_id_type=MESH)
        return 0

    lax.fori_loop(1, ns, greet_slab, 0)
    lax.fori_loop(1, nb, greet_block, 0)

    lane = lax.broadcasted_iota(jnp.int32, (1, WALL), 1)
    own_rows = rows_ref[0, 0]
    live = lane < count_ref[0, 0, 0]
    slots[ns - 1, 0:1] = jnp.where(live, own_rows.astype(F32), -1.0)
    slots[ns - 1, 1:2] = angle_ref[0, 0]

    pl.semaphore_wait(barrier, ns - 1 + nb - 1)

    def slot_copy(k):
        return pltpu.make_async_remote_copy(
            src_ref=slots.at[ns - 1], dst_ref=slots.at[k - 1],
            send_sem=slot_send, recv_sem=slot_recv,
            device_id=slab_peer(k), device_id_type=MESH,
        )

    def send_slots(k, _):
        slot_copy(k).start()
        return 0

    def halo(src, dst, sem_at, send_sem, recv_sem, device):
        return pltpu.make_async_remote_copy(
            src_ref=src, dst_ref=dst, send_sem=send_sem.at[sem_at], recv_sem=recv_sem.at[sem_at],
            device_id=device, device_id_type=MESH,
        )

    rows_of = pl.ds(8, CY)
    s_up, s_down = jnp.minimum(s + 1, ns - 1), jnp.maximum(s - 1, 0)
    r_up, r_down = jnp.minimum(r + 1, nr - 1), jnp.maximum(r - 1, 0)
    c_up, c_down = jnp.minimum(c + 1, nc - 1), jnp.maximum(c - 1, 0)
    has = {
        "xu": s < ns - 1, "xd": s > 0, "yu": r < nr - 1, "yd": r > 0, "zu": c < nc - 1, "zd": c > 0,
    }

    def field_x(ref, base):
        return {
            "xu": halo(ref.at[CX, rows_of], ref.at[0, rows_of], base, halo_send, halo_recv, (s_up, r, c)),
            "xd": halo(ref.at[1, rows_of], ref.at[CX + 1, rows_of], base + 1, halo_send, halo_recv, (s_down, r, c)),
        }

    def field_y(ref, base):
        inner = pl.ds(1, CX)
        return {
            "yu": halo(ref.at[inner, pl.ds(CY, 8)], ref.at[inner, pl.ds(0, 8)], base, halo_send, halo_recv, (s, r_up, c)),
            "yd": halo(ref.at[inner, pl.ds(8, 8)], ref.at[inner, pl.ds(CY + 8, 8)], base + 1, halo_send, halo_recv, (s, r_down, c)),
        }

    q_x = field_x(qq, 0)
    p_x = field_x(pp, 2)
    q_y = field_y(qq, 4)
    p_y = field_y(pp, 6)
    pq_z = {
        "zu": halo(zsend.at[pl.ds(8, 8)], zrecv.at[pl.ds(0, 8)], 8, halo_send, halo_recv, (s, r, c_up)),
        "zd": halo(zsend.at[pl.ds(0, 8)], zrecv.at[pl.ds(8, 8)], 9, halo_send, halo_recv, (s, r, c_down)),
    }
    inner = pl.ds(0, CX)
    lam_x = {
        "xu": halo(lam0.at[CX], lam0.at[0], 0, lam_send, lam_recv, (s_up, r, c)),
        "xd": halo(lam0.at[1], lam0.at[CX + 1], 1, lam_send, lam_recv, (s_down, r, c)),
    }
    lam_y = {
        "yu": halo(lam1.at[inner, pl.ds(CY, 8)], lam1.at[inner, pl.ds(0, 8)], 2, lam_send, lam_recv, (s, r_up, c)),
        "yd": halo(lam1.at[inner, pl.ds(8, 8)], lam1.at[inner, pl.ds(CY + 8, 8)], 3, lam_send, lam_recv, (s, r_down, c)),
    }
    lam_z = {
        "zu": halo(lsend.at[pl.ds(8, 8)], lrecv.at[pl.ds(0, 8)], 4, lam_send, lam_recv, (s, r, c_up)),
        "zd": halo(lsend.at[pl.ds(0, 8)], lrecv.at[pl.ds(8, 8)], 5, lam_send, lam_recv, (s, r, c_down)),
    }

    def start(group):
        for side, copy in group.items():
            pl.when(has[side])(copy.start)

    opposite = {"xu": "xd", "xd": "xu", "yu": "yd", "yd": "yu", "zu": "zd", "zd": "zu"}

    def arrive(group):
        for side, copy in group.items():
            pl.when(has[opposite[side]])(copy.wait_recv)

    def sent(group):
        for side, copy in group.items():
            pl.when(has[side])(copy.wait_send)

    lax.fori_loop(1, ns, send_slots, 0)

    loads[0].wait()
    loads[1].wait()
    for x in (0, CX - 1):
        qq[x + 1, rows_of] = kap[x] * ap[x]
    start(q_x)
    for x in range(1, CX - 1):
        qq[x + 1, rows_of] = kap[x] * ap[x]
    start(q_y)
    loads[2].wait()
    start(p_x)
    start(p_y)
    for ref, at in ((pp, 0), (qq, CX)):
        for x in range(CX):
            turned = ref[x + 1, rows_of].T
            zsend[at + x:at + x + 1] = turned[0:1]
            zsend[8 + at + x:8 + at + x + 1] = turned[CZ - 1:CZ]
    start(pq_z)

    own_cells = cells_ref[0, 0]
    own_xy = own_cells >> 7
    own_z = own_cells & (CZ - 1)
    xy = lax.broadcasted_iota(jnp.int32, (CY, WALL), 0)
    for x in range(CX):
        where_hot[x * CY:(x + 1) * CY] = jnp.where(xy + x * CY == own_xy, 1.0, 0.0).astype(BF16)

    pltpu.make_async_copy(slots.at[pl.ds(0, ns - 1)], slots.at[pl.ds(0, ns - 1)], slot_recv).wait()
    width = nb * OWN
    first = (s * width).astype(F32)
    row_at = lax.broadcasted_iota(jnp.int32, (width, WALL), 0).astype(F32) + first
    knots = lax.broadcasted_iota(jnp.int32, (ANG, WALL), 0).astype(F32)

    def prepare(g, _):
        hot[g] = jnp.where(slots[g, 0:1] == row_at, 1.0, 0.0).astype(BF16)
        dist = jnp.abs(slots[g, 1:2] - knots)
        dist = jnp.minimum(dist, ANG - dist)
        outer = jnp.maximum(2.0 - dist, 0.0)
        near = jnp.maximum(1.0 - dist, 0.0)
        weight[g] = (outer * outer * outer - 4.0 * near * near * near) * (1.0 / 6.0)
        return 0

    lax.fori_loop(0, ns, prepare, 0)

    phase = jnp.cos(0.5 * jnp.full((1, CZ), lax.rem(step_ref[0], 97).astype(F32), F32))
    for copy in loads[3:]:
        copy.wait()
    for group in (q_x, q_y, p_x, p_y, pq_z):
        arrive(group)
    edge_t = jnp.concatenate([zrecv[...], jnp.zeros((CZ - 16, CZ), F32)], axis=0).T
    at_z = lax.broadcasted_iota(jnp.int32, (CY, CZ), 1)

    def along_z(field, low, high):
        upper = jnp.where(at_z == CZ - 1, high, pltpu.roll(field, CZ - 1, 1))
        lower = jnp.where(at_z == 0, low, pltpu.roll(field, 1, 1))
        return (upper - lower) * 0.5

    def slopes(ref, x, at):
        mid = ref[x + 1, rows_of]
        return (
            (ref[x + 2, rows_of] - ref[x, rows_of]) * 0.5,
            (ref[x + 1, pl.ds(9, CY)] - ref[x + 1, pl.ds(7, CY)]) * 0.5,
            along_z(mid, edge_t[:, at + x:at + x + 1], edge_t[:, 8 + at + x:8 + at + x + 1]),
        )

    for x in range(CX):
        dp = slopes(pp, x, 0)
        dq = slopes(qq, x, CX)
        free = 1.0 - mask[x].astype(F32)
        total = [avel[k, x] + dq[k] for k in range(3)]
        lam0[x + 1] = free * total[0]
        lam1[x, rows_of] = free * total[1]
        lam2[x] = free * total[2]
        sens = -(
            total[0] * (vel[0, x] - 0.3 * dp[0] + drv[x] * phase)
            + total[1] * (vel[1, x] - 0.3 * dp[1])
            + total[2] * (vel[2, x] - 0.3 * dp[2])
        )
        for i, piece in enumerate(pieces(sens.T)):
            sens_t[i * CZ:(i + 1) * CZ, x * CY:(x + 1) * CY] = piece

    picked = jnp.dot(sens_t[...], where_hot[...], preferred_element_type=F32)
    picked = picked[0:CZ] + picked[CZ:2 * CZ] + picked[2 * CZ:3 * CZ]
    z_at = lax.broadcasted_iota(jnp.int32, (CZ, WALL), 0)
    vals[ns - 1] = jnp.sum(jnp.where(z_at == own_z, picked, 0.0), axis=0, keepdims=True)

    def send_vals(k, _):
        pltpu.make_async_remote_copy(
            src_ref=vals.at[ns - 1], dst_ref=vals.at[k - 1], send_sem=val_send, recv_sem=val_recv,
            device_id=slab_peer(k), device_id_type=MESH,
        ).start()
        return 0

    lax.fori_loop(1, ns, send_vals, 0)

    start(lam_x)
    start(lam_y)
    for x in range(CX):
        turned = lam2[x].T
        lsend[x:x + 1] = turned[0:1]
        lsend[8 + x:9 + x] = turned[CZ - 1:CZ]
    start(lam_z)
    stores = [
        pltpu.make_async_copy(lam0.at[pl.ds(1, CX)], av_out.at[0], store_sem.at[0]),
        pltpu.make_async_copy(lam1.at[pl.ds(0, CX), rows_of], av_out.at[1], store_sem.at[1]),
        pltpu.make_async_copy(lam2, av_out.at[2], store_sem.at[2]),
    ]
    for copy in stores:
        copy.start()

    pltpu.make_async_copy(vals.at[pl.ds(0, ns - 1)], vals.at[pl.ds(0, ns - 1)], val_recv).wait()

    def add_up(g, total):
        scaled = jnp.concatenate(pieces(weight[g] * vals[g]), axis=0)
        return total + lax.dot_general(
            hot[g], scaled, (((1,), (1,)), ((), ())), preferred_element_type=F32
        )

    summed = lax.fori_loop(0, ns, add_up, jnp.zeros((width, 3 * ANG), F32))
    summed = summed[:, 0:ANG] + summed[:, ANG:2 * ANG] + summed[:, 2 * ANG:3 * ANG]
    dense[...] = jnp.concatenate([summed, jnp.zeros_like(summed)], axis=1).reshape(nb, OWN, 2 * ANG)

    def send_part(k, _):
        other = lax.rem(b + k, nb)
        pltpu.make_async_remote_copy(
            src_ref=dense.at[other], dst_ref=parts.at[k - 1], send_sem=part_send, recv_sem=part_recv,
            device_id=block_peer(k), device_id_type=MESH,
        ).start()
        return 0

    lax.fori_loop(1, nb, send_part, 0)

    for group in (lam_x, lam_y, lam_z):
        arrive(group)
    edge_l = jnp.concatenate([lrecv[...], jnp.zeros((CZ - 16, CZ), F32)], axis=0).T
    for x in range(CX):
        div = (
            (lam0[x + 2] - lam0[x]) * 0.5
            + (lam1[x, pl.ds(9, CY)] - lam1[x, pl.ds(7, CY)]) * 0.5
            + along_z(lam2[x], edge_l[:, x:x + 1], edge_l[:, 8 + x:9 + x])
        )
        apo[x] = ap[x] + 0.3 * div
    last = pltpu.make_async_copy(apo, ap_out, store_sem.at[3])
    last.start()

    pltpu.make_async_copy(parts, parts, part_recv).wait()
    grad_out[...] = (dense[b] + jnp.sum(parts[...], axis=0))[:, 0:ANG]

    for group in (q_x, q_y, p_x, p_y, pq_z, lam_x, lam_y, lam_z):
        sent(group)
    pltpu.make_async_copy(slots.at[pl.ds(0, ns - 1)], slots.at[pl.ds(0, ns - 1)], slot_send).wait()
    pltpu.make_async_copy(vals.at[pl.ds(0, ns - 1)], vals.at[pl.ds(0, ns - 1)], val_send).wait()
    pltpu.make_async_copy(parts, parts, part_send).wait()
    for copy in stores + [last]:
        copy.wait()


def local(ns, nr, nc, *args):
    nb = nr * nc
    anyspace = pl.BlockSpec(memory_space=pl.ANY)
    vmem = pl.BlockSpec(memory_space=pltpu.VMEM)
    smem = pl.BlockSpec(memory_space=pltpu.SMEM)
    block = (CX, CY, CZ)
    dma = pltpu.SemaphoreType.DMA
    return pl.pallas_call(
        functools.partial(kernel, ns, nr, nc),
        out_shape=(
            jax.ShapeDtypeStruct(block, F32),
            jax.ShapeDtypeStruct((3,) + block, F32),
            jax.ShapeDtypeStruct((OWN, ANG), F32),
        ),
        in_specs=[anyspace] * 7 + [vmem] * 3 + [smem] * 2,
        out_specs=(anyspace, anyspace, vmem),
        scratch_shapes=[
            pltpu.VMEM((CX + 2, CY + 16, CZ), F32),
            pltpu.VMEM((CX + 2, CY + 16, CZ), F32),
            pltpu.VMEM(block, F32),
            pltpu.VMEM(block, F32),
            pltpu.VMEM(block, F32),
            pltpu.VMEM((3,) + block, F32),
            pltpu.VMEM((3,) + block, F32),
            pltpu.VMEM(block, jnp.int32),
            pltpu.VMEM((CX + 2, CY, CZ), F32),
            pltpu.VMEM((CX, CY + 16, CZ), F32),
            pltpu.VMEM(block, F32),
            pltpu.VMEM(block, F32),
            pltpu.VMEM((16, CY), F32),
            pltpu.VMEM((16, CY), F32),
            pltpu.VMEM((16, CY), F32),
            pltpu.VMEM((16, CY), F32),
            pltpu.VMEM((ns, 2, WALL), F32),
            pltpu.VMEM((ns, 1, WALL), F32),
            pltpu.VMEM((ns, nb * OWN, WALL), BF16),
            pltpu.VMEM((ns, ANG, WALL), F32),
            pltpu.VMEM((CX * CY, WALL), BF16),
            pltpu.VMEM((3 * CZ, CX * CY), BF16),
            pltpu.VMEM((nb, OWN, 2 * ANG), F32),
            pltpu.VMEM((nb - 1, OWN, 2 * ANG), F32),
            dma((7,)), dma((4,)), dma((10,)), dma((10,)), dma((6,)), dma((6,)),
            dma, dma, dma, dma, dma, dma,
        ],
        compiler_params=pltpu.CompilerParams(
            collective_id=0, has_side_effects=True, vmem_limit_bytes=48 * 1024 * 1024
        ),
        cost_estimate=pl.CostEstimate(flops=10**9, bytes_accessed=4 * 10**6, transcendentals=0),
    )(*args)


def solution(mesh):
    names = ("slab", "row", "col")
    sizes = tuple(mesh.shape[name] for name in names)
    cells = P(*names)
    vector = P(None, *names)
    slot = P(*names, None)
    in_specs = (cells, vector, cells, cells, cells, vector, cells, slot, slot, slot, cells, P())
    out_specs = (cells, vector, P(names, None))
    return jax.shard_map(
        functools.partial(local, *sizes), mesh=mesh, in_specs=in_specs, out_specs=out_specs, check_vma=False
    )
```

```python
import functools

import jax
import jax.numpy as jnp
from jax import lax
from jax.experimental import pallas as pl
from jax.experimental.pallas import tpu as pltpu
from jax.sharding import PartitionSpec as P

ANG = 64
CX = 4
CY = 128
CZ = 128
WALL = 512
OWN = 8
NXC = 4
NYC = 4
ZL = 4
ZH = 2
NA = NXC * NYC
NB = 2 * ZL * ZH
WIDTH = NB * OWN
MESH = pl.DeviceIdType.MESH
PLANE = sorted(
    ((dy, dx) for dy in range(NYC) for dx in range(NXC)),
    key=lambda d: (min(d[0], NYC - d[0]) + min(d[1], NXC - d[1]), d),
)
F32 = jnp.float32
BF16 = jnp.bfloat16


def pieces(value):
    high = value.astype(BF16)
    rest = value - high.astype(F32)
    mid = rest.astype(BF16)
    low = (rest - mid.astype(F32)).astype(BF16)
    return high, mid, low


def kernel(
    ns, nr, nc,
    p_in, v_in, kap_in, drv_in, ap_in, av_in, mask_in, cells_in, rows_in, angle_in, count_in, step_in,
    ap_out, av_out, grad_out,
    cells_ref, rows_ref, angle_ref, count_ref, step_ref,
    pp, qq, kap, drv, ap, vel, avel, mask,
    lam0, lam1, lam2, apo,
    zsend, zrecv, lsend, lrecv,
    slots, vals, hot, weight, where_hot, sens_t, dense, parts,
    small_sem, load_sem, store_sem, halo_send, halo_recv, lam_send, lam_recv,
    slot_send, slot_recv, val_send, val_recv, part_send, part_recv,
):
    s = lax.axis_index("slab")
    r = lax.axis_index("row")
    c = lax.axis_index("col")
    y, zl = lax.div(s, ZL), lax.rem(s, ZL)
    x_at, zh = lax.div(c, ZH), lax.rem(c, ZH)
    group = y * NXC + x_at
    b = (zl * 2 + r) * ZH + zh

    def plane_peer(k):
        dy, dx = PLANE[k]
        return (lax.rem(y + dy, NYC) * ZL + zl, r, lax.rem(x_at + dx, NXC) * ZH + zh)

    def line_peer(k):
        other_zl = lax.rem(zl + lax.div(k, 2 * ZH), ZL)
        other_r = lax.rem(r + lax.rem(lax.div(k, ZH), 2), 2)
        other_zh = lax.rem(zh + lax.rem(k, ZH), ZH)
        return (y * ZL + other_zl, other_r, x_at * ZH + other_zh)

    loads = [
        pltpu.make_async_copy(kap_in, kap, load_sem.at[0]),
        pltpu.make_async_copy(ap_in, ap, load_sem.at[1]),
        pltpu.make_async_copy(p_in, pp.at[pl.ds(1, CX), pl.ds(8, CY)], load_sem.at[2]),
        pltpu.make_async_copy(av_in, avel, load_sem.at[3]),
        pltpu.make_async_copy(mask_in, mask, load_sem.at[4]),
        pltpu.make_async_copy(v_in, vel, load_sem.at[5]),
        pltpu.make_async_copy(drv_in, drv, load_sem.at[6]),
    ]
    small = [
        pltpu.make_async_copy(rows_in, rows_ref, small_sem.at[0]),
        pltpu.make_async_copy(angle_in, angle_ref, small_sem.at[1]),
        pltpu.make_async_copy(count_in, count_ref, small_sem.at[2]),
        pltpu.make_async_copy(cells_in, cells_ref, small_sem.at[3]),
        pltpu.make_async_copy(step_in, step_ref, small_sem.at[4]),
    ]
    for copy in small + loads:
        copy.start()

    plane = jnp.zeros((CY, CZ), F32)
    for ref in (pp, qq):
        ref[0, pl.ds(8, CY)] = plane
        ref[CX + 1, pl.ds(8, CY)] = plane
        for x in range(CX):
            ref[x + 1, pl.ds(0, 8)] = jnp.zeros((8, CZ), F32)
            ref[x + 1, pl.ds(CY + 8, 8)] = jnp.zeros((8, CZ), F32)
    lam0[0] = plane
    lam0[CX + 1] = plane
    for x in range(CX):
        lam1[x, pl.ds(0, 8)] = jnp.zeros((8, CZ), F32)
        lam1[x, pl.ds(CY + 8, 8)] = jnp.zeros((8, CZ), F32)
    zrecv[...] = jnp.zeros_like(zrecv)
    lrecv[...] = jnp.zeros_like(lrecv)

    barrier = pltpu.get_barrier_semaphore()

    def greet(device):
        pl.semaphore_signal(barrier, inc=1, device_id=device, device_id_type=MESH)

    def greet_line(k, _):
        greet(line_peer(k))
        return 0

    s_up, s_down = jnp.minimum(s + 1, ns - 1), jnp.maximum(s - 1, 0)
    r_up, r_down = jnp.minimum(r + 1, nr - 1), jnp.maximum(r - 1, 0)
    c_up, c_down = jnp.minimum(c + 1, nc - 1), jnp.maximum(c - 1, 0)
    has = {
        "xu": s < ns - 1, "xd": s > 0, "yu": r < nr - 1, "yd": r > 0, "zu": c < nc - 1, "zd": c > 0,
    }
    beyond = (
        (jnp.logical_and(zh == ZH - 1, has["zu"]), (s, r, c_up)),
        (jnp.logical_and(zh == 0, has["zd"]), (s, r, c_down)),
        (jnp.logical_and(zl == ZL - 1, has["xu"]), (s_up, r, c)),
        (jnp.logical_and(zl == 0, has["xd"]), (s_down, r, c)),
    )
    partners = NA - 1 + NB - 1
    for here, device in beyond:
        pl.when(here)(functools.partial(greet, device))
        partners = partners + here.astype(jnp.int32)
    for k in range(1, NA):
        greet(plane_peer(k))
    lax.fori_loop(1, NB, greet_line, 0)

    lane = lax.broadcasted_iota(jnp.int32, (1, WALL), 1)
    for copy in small:
        copy.wait()
    own_rows = rows_ref[0, 0]
    live = lane < count_ref[0, 0, 0]
    bits = own_rows >> 3
    owner_group = ((bits >> 6) << 2) + ((bits >> 1) & 3)
    owner_line = (((bits >> 4) & 3) << 2) + (((bits >> 3) & 1) << 1) + (bits & 1)
    code = owner_group * WIDTH + owner_line * OWN + (own_rows & (OWN - 1))
    slots[0, 0:1] = jnp.where(live, code.astype(F32), -1.0)
    slots[0, 1:2] = angle_ref[0, 0]
    row_at = (lax.broadcasted_iota(jnp.int32, (WIDTH, WALL), 0) + group * WIDTH).astype(F32)
    knots = lax.broadcasted_iota(jnp.int32, (ANG, WALL), 0).astype(F32)

    def prepare(k):
        hot[k] = jnp.where(slots[k, 0:1] == row_at, 1.0, 0.0).astype(BF16)
        dist = jnp.abs(slots[k, 1:2] - knots)
        dist = jnp.minimum(dist, ANG - dist)
        outer = jnp.maximum(2.0 - dist, 0.0)
        near = jnp.maximum(1.0 - dist, 0.0)
        weight[k] = (outer * outer * outer - 4.0 * near * near * near) * (1.0 / 6.0)

    prepare(0)

    own_cells = cells_ref[0, 0]
    own_xy = own_cells >> 7
    own_z = own_cells & (CZ - 1)
    xy = lax.broadcasted_iota(jnp.int32, (CY, WALL), 0)
    for x in range(CX):
        where_hot[x * CY:(x + 1) * CY] = jnp.where(xy + x * CY == own_xy, 1.0, 0.0).astype(BF16)

    loads[0].wait()
    loads[1].wait()
    rows_of = pl.ds(8, CY)
    for x in range(CX):
        qq[x + 1, rows_of] = kap[x] * ap[x]
    loads[2].wait()
    for ref, at in ((pp, 0), (qq, CX)):
        for x in range(CX):
            turned = ref[x + 1, rows_of].T
            zsend[at + x:at + x + 1] = turned[0:1]
            zsend[8 + at + x:8 + at + x + 1] = turned[CZ - 1:CZ]

    pl.semaphore_wait(barrier, partners)

    def slot_copy(k):
        return pltpu.make_async_remote_copy(
            src_ref=slots.at[0], dst_ref=slots.at[k],
            send_sem=slot_send, recv_sem=slot_recv.at[k],
            device_id=plane_peer(k), device_id_type=MESH,
        )

    def halo(src, dst, sem_at, send_sem, recv_sem, device):
        return pltpu.make_async_remote_copy(
            src_ref=src, dst_ref=dst, send_sem=send_sem.at[sem_at], recv_sem=recv_sem.at[sem_at],
            device_id=device, device_id_type=MESH,
        )


    def field_x(ref, base):
        return {
            "xu": halo(ref.at[CX, rows_of], ref.at[0, rows_of], base, halo_send, halo_recv, (s_up, r, c)),
            "xd": halo(ref.at[1, rows_of], ref.at[CX + 1, rows_of], base + 1, halo_send, halo_recv, (s_down, r, c)),
        }

    def field_y(ref, base):
        inner = pl.ds(1, CX)
        return {
            "yu": halo(ref.at[inner, pl.ds(CY, 8)], ref.at[inner, pl.ds(0, 8)], base, halo_send, halo_recv, (s, r_up, c)),
            "yd": halo(ref.at[inner, pl.ds(8, 8)], ref.at[inner, pl.ds(CY + 8, 8)], base + 1, halo_send, halo_recv, (s, r_down, c)),
        }

    q_x = field_x(qq, 0)
    p_x = field_x(pp, 2)
    q_y = field_y(qq, 4)
    p_y = field_y(pp, 6)
    pq_z = {
        "zu": halo(zsend.at[pl.ds(8, 8)], zrecv.at[pl.ds(0, 8)], 8, halo_send, halo_recv, (s, r, c_up)),
        "zd": halo(zsend.at[pl.ds(0, 8)], zrecv.at[pl.ds(8, 8)], 9, halo_send, halo_recv, (s, r, c_down)),
    }
    inner = pl.ds(0, CX)
    lam_x = {
        "xu": halo(lam0.at[CX], lam0.at[0], 0, lam_send, lam_recv, (s_up, r, c)),
        "xd": halo(lam0.at[1], lam0.at[CX + 1], 1, lam_send, lam_recv, (s_down, r, c)),
    }
    lam_y = {
        "yu": halo(lam1.at[inner, pl.ds(CY, 8)], lam1.at[inner, pl.ds(0, 8)], 2, lam_send, lam_recv, (s, r_up, c)),
        "yd": halo(lam1.at[inner, pl.ds(8, 8)], lam1.at[inner, pl.ds(CY + 8, 8)], 3, lam_send, lam_recv, (s, r_down, c)),
    }
    lam_z = {
        "zu": halo(lsend.at[pl.ds(8, 8)], lrecv.at[pl.ds(0, 8)], 4, lam_send, lam_recv, (s, r, c_up)),
        "zd": halo(lsend.at[pl.ds(0, 8)], lrecv.at[pl.ds(8, 8)], 5, lam_send, lam_recv, (s, r, c_down)),
    }

    def start(faces):
        for side, copy in faces.items():
            pl.when(has[side])(copy.start)

    opposite = {"xu": "xd", "xd": "xu", "yu": "yd", "yd": "yu", "zu": "zd", "zd": "zu"}

    def arrive(faces):
        for side, copy in faces.items():
            pl.when(has[opposite[side]])(copy.wait_recv)

    def sent(faces):
        for side, copy in faces.items():
            pl.when(has[side])(copy.wait_send)

    start(pq_z)
    for k in range(NA - 1, 0, -1):
        slot_copy(k).start()
    start(q_x)
    start(p_x)
    start(q_y)
    start(p_y)
    halos = [q_x, q_y, p_x, p_y, pq_z]

    def slots_of(k, _):
        pltpu.make_async_copy(slots.at[k], slots.at[k], slot_recv.at[k]).wait()
        prepare(k)
        return 0

    lax.fori_loop(1, NA, slots_of, 0)
    rest = slots.at[pl.ds(1, NA - 1)]

    phase = jnp.cos(0.5 * jnp.full((1, CZ), lax.rem(step_ref[0], 97).astype(F32), F32))
    for copy in loads[3:]:
        copy.wait()
    for faces in (q_x, q_y, p_x, p_y, pq_z):
        arrive(faces)
    edge_t = jnp.concatenate([zrecv[...], jnp.zeros((CZ - 16, CZ), F32)], axis=0).T
    at_z = lax.broadcasted_iota(jnp.int32, (CY, CZ), 1)

    def along_z(field, low, high):
        upper = jnp.where(at_z == CZ - 1, high, pltpu.roll(field, CZ - 1, 1))
        lower = jnp.where(at_z == 0, low, pltpu.roll(field, 1, 1))
        return (upper - lower) * 0.5

    def slopes(ref, x, at):
        mid = ref[x + 1, rows_of]
        return (
            (ref[x + 2, rows_of] - ref[x, rows_of]) * 0.5,
            (ref[x + 1, pl.ds(9, CY)] - ref[x + 1, pl.ds(7, CY)]) * 0.5,
            along_z(mid, edge_t[:, at + x:at + x + 1], edge_t[:, 8 + at + x:8 + at + x + 1]),
        )

    for x in range(CX):
        dp = slopes(pp, x, 0)
        dq = slopes(qq, x, CX)
        free = 1.0 - mask[x].astype(F32)
        total = [avel[k, x] + dq[k] for k in range(3)]
        lam0[x + 1] = free * total[0]
        lam1[x, rows_of] = free * total[1]
        lam2[x] = free * total[2]
        sens = -(
            total[0] * (vel[0, x] - 0.3 * dp[0] + drv[x] * phase)
            + total[1] * (vel[1, x] - 0.3 * dp[1])
            + total[2] * (vel[2, x] - 0.3 * dp[2])
        )
        for i, piece in enumerate(pieces(sens.T)):
            sens_t[i * CZ:(i + 1) * CZ, x * CY:(x + 1) * CY] = piece

    picked = jnp.dot(sens_t[...], where_hot[...], preferred_element_type=F32)
    picked = picked[0:CZ] + picked[CZ:2 * CZ] + picked[2 * CZ:3 * CZ]
    z_at = lax.broadcasted_iota(jnp.int32, (CZ, WALL), 0)
    vals[0] = jnp.sum(jnp.where(z_at == own_z, picked, 0.0), axis=0, keepdims=True)

    for k in range(NA - 1, 0, -1):
        pltpu.make_async_remote_copy(
            src_ref=vals.at[0], dst_ref=vals.at[k], send_sem=val_send, recv_sem=val_recv.at[k],
            device_id=plane_peer(k), device_id_type=MESH,
        ).start()

    start(lam_x)
    start(lam_y)
    for x in range(CX):
        turned = lam2[x].T
        lsend[x:x + 1] = turned[0:1]
        lsend[8 + x:9 + x] = turned[CZ - 1:CZ]
    start(lam_z)
    stores = [
        pltpu.make_async_copy(lam0.at[pl.ds(1, CX)], av_out.at[0], store_sem.at[0]),
        pltpu.make_async_copy(lam1.at[pl.ds(0, CX), rows_of], av_out.at[1], store_sem.at[1]),
        pltpu.make_async_copy(lam2, av_out.at[2], store_sem.at[2]),
    ]
    for copy in stores:
        copy.start()

    def product(k):
        scaled = jnp.concatenate(pieces(weight[k] * vals[k]), axis=0)
        return lax.dot_general(hot[k], scaled, (((1,), (1,)), ((), ())), preferred_element_type=F32)

    def add_up(k, total):
        pltpu.make_async_copy(vals.at[k], vals.at[k], val_recv.at[k]).wait()
        return total + product(k)

    rest_vals = vals.at[pl.ds(1, NA - 1)]
    summed = lax.fori_loop(1, NA, add_up, product(0))
    summed = summed[:, 0:ANG] + summed[:, ANG:2 * ANG] + summed[:, 2 * ANG:3 * ANG]
    dense[...] = jnp.concatenate([summed, jnp.zeros_like(summed)], axis=1).reshape(NB, OWN, 2 * ANG)

    def send_part(k, _):
        peer = line_peer(k)
        other = (lax.rem(peer[0], ZL) * 2 + peer[1]) * ZH + lax.rem(peer[2], ZH)
        pltpu.make_async_remote_copy(
            src_ref=dense.at[other], dst_ref=parts.at[k - 1], send_sem=part_send, recv_sem=part_recv,
            device_id=peer, device_id_type=MESH,
        ).start()
        return 0

    lax.fori_loop(1, NB, send_part, 0)

    for faces in (lam_x, lam_y, lam_z):
        arrive(faces)
    edge_l = jnp.concatenate([lrecv[...], jnp.zeros((CZ - 16, CZ), F32)], axis=0).T
    for x in range(CX):
        div = (
            (lam0[x + 2] - lam0[x]) * 0.5
            + (lam1[x, pl.ds(9, CY)] - lam1[x, pl.ds(7, CY)]) * 0.5
            + along_z(lam2[x], edge_l[:, x:x + 1], edge_l[:, 8 + x:9 + x])
        )
        apo[x] = ap[x] + 0.3 * div
    last = pltpu.make_async_copy(apo, ap_out, store_sem.at[3])
    last.start()

    pltpu.make_async_copy(parts, parts, part_recv).wait()
    grad_out[...] = (dense[b] + jnp.sum(parts[...], axis=0))[:, 0:ANG]

    for faces in (q_x, q_y, p_x, p_y, pq_z, lam_x, lam_y, lam_z):
        sent(faces)
    pltpu.make_async_copy(rest, rest, slot_send).wait()
    pltpu.make_async_copy(rest_vals, rest_vals, val_send).wait()
    pltpu.make_async_copy(parts, parts, part_send).wait()
    for copy in stores + [last]:
        copy.wait()


def local(ns, nr, nc, *args):
    hbm = pl.BlockSpec(memory_space=pltpu.HBM)
    vmem = pl.BlockSpec(memory_space=pltpu.VMEM)
    block = (CX, CY, CZ)
    dma = pltpu.SemaphoreType.DMA
    return pl.pallas_call(
        functools.partial(kernel, ns, nr, nc),
        out_shape=(
            jax.ShapeDtypeStruct(block, F32),
            jax.ShapeDtypeStruct((3,) + block, F32),
            jax.ShapeDtypeStruct((OWN, ANG), F32),
        ),
        in_specs=[hbm] * 12,
        out_specs=(pl.BlockSpec(memory_space=pl.ANY), pl.BlockSpec(memory_space=pl.ANY), vmem),
        scratch_shapes=[
            pltpu.VMEM((1, 1, 1, WALL), jnp.int32),
            pltpu.VMEM((1, 1, 1, WALL), jnp.int32),
            pltpu.VMEM((1, 1, 1, WALL), F32),
            pltpu.SMEM((1, 1, 1), jnp.int32),
            pltpu.SMEM((1,), jnp.int32),
            pltpu.VMEM((CX + 2, CY + 16, CZ), F32),
            pltpu.VMEM((CX + 2, CY + 16, CZ), F32),
            pltpu.VMEM(block, F32),
            pltpu.VMEM(block, F32),
            pltpu.VMEM(block, F32),
            pltpu.VMEM((3,) + block, F32),
            pltpu.VMEM((3,) + block, F32),
            pltpu.VMEM(block, jnp.int32),
            pltpu.VMEM((CX + 2, CY, CZ), F32),
            pltpu.VMEM((CX, CY + 16, CZ), F32),
            pltpu.VMEM(block, F32),
            pltpu.VMEM(block, F32),
            pltpu.VMEM((16, CY), F32),
            pltpu.VMEM((16, CY), F32),
            pltpu.VMEM((16, CY), F32),
            pltpu.VMEM((16, CY), F32),
            pltpu.VMEM((NA, 2, WALL), F32),
            pltpu.VMEM((NA, 1, WALL), F32),
            pltpu.VMEM((NA, WIDTH, WALL), BF16),
            pltpu.VMEM((NA, ANG, WALL), F32),
            pltpu.VMEM((CX * CY, WALL), BF16),
            pltpu.VMEM((3 * CZ, CX * CY), BF16),
            pltpu.VMEM((NB, OWN, 2 * ANG), F32),
            pltpu.VMEM((NB - 1, OWN, 2 * ANG), F32),
            dma((5,)), dma((7,)), dma((4,)), dma((10,)), dma((10,)), dma((6,)), dma((6,)),
            dma, dma((NA,)), dma, dma((NA,)), dma, dma,
        ],
        compiler_params=pltpu.CompilerParams(
            collective_id=0, has_side_effects=True, vmem_limit_bytes=60 * 1024 * 1024
        ),
        cost_estimate=pl.CostEstimate(flops=10**9, bytes_accessed=4 * 10**6, transcendentals=0),
    )(*args)


def solution(mesh):
    names = ("slab", "row", "col")
    sizes = tuple(mesh.shape[name] for name in names)
    cells = P(*names)
    vector = P(None, *names)
    slot = P(*names, None)
    in_specs = (cells, vector, cells, cells, cells, vector, cells, slot, slot, slot, cells, P())
    out_specs = (cells, vector, P(names, None))
    return jax.shard_map(
        functools.partial(local, *sizes), mesh=mesh, in_specs=in_specs, out_specs=out_specs, check_vma=False
    )
```

```python
import functools

import jax
import jax.numpy as jnp
from jax import lax
from jax.experimental import pallas as pl
from jax.experimental.pallas import tpu as pltpu
from jax.sharding import PartitionSpec as P

ANG = 64
CX = 4
CY = 128
CZ = 128
WALL = 512
OWN = 8
NXC = 4
NYC = 4
ZL = 4
ZH = 2
NA = NXC * NYC
NB = 2 * ZL * ZH
WIDTH = NB * OWN
MESH = pl.DeviceIdType.MESH
PLANE = sorted(
    ((dy, dx) for dy in range(NYC) for dx in range(NXC)),
    key=lambda d: (min(d[0], NYC - d[0]) + min(d[1], NXC - d[1]), d),
)
F32 = jnp.float32
BF16 = jnp.bfloat16


def pieces(value):
    high = value.astype(BF16)
    rest = value - high.astype(F32)
    mid = rest.astype(BF16)
    low = (rest - mid.astype(F32)).astype(BF16)
    return high, mid, low


def kernel(
    ns, nr, nc,
    p_in, v_in, kap_in, drv_in, ap_in, av_in, mask_in, cells_in, rows_in, angle_in, count_in, step_in,
    ap_out, av_out, grad_out,
    cells_ref, rows_ref, angle_ref, count_ref, step_ref,
    pp, qq, kap, drv, ap, vel, avel, mask,
    lam0, lam1, lam2, apo,
    zsend, zrecv, lsend, lrecv,
    slots, vals, hot, weight, where_hot, sens_t, dense, parts,
    small_sem, load_sem, store_sem, halo_send, halo_recv, lam_send, lam_recv,
    slot_send, slot_recv, val_send, val_recv, part_send, part_recv,
):
    s = lax.axis_index("slab")
    r = lax.axis_index("row")
    c = lax.axis_index("col")
    y, zl = lax.div(s, ZL), lax.rem(s, ZL)
    x_at, zh = lax.div(c, ZH), lax.rem(c, ZH)
    group = y * NXC + x_at
    b = (zl * 2 + r) * ZH + zh

    def plane_peer(k):
        dy, dx = PLANE[k]
        return (lax.rem(y + dy, NYC) * ZL + zl, r, lax.rem(x_at + dx, NXC) * ZH + zh)

    def line_peer(k):
        other_zl = lax.rem(zl + lax.div(k, 2 * ZH), ZL)
        other_r = lax.rem(r + lax.rem(lax.div(k, ZH), 2), 2)
        other_zh = lax.rem(zh + lax.rem(k, ZH), ZH)
        return (y * ZL + other_zl, other_r, x_at * ZH + other_zh)

    loads = [
        pltpu.make_async_copy(kap_in, kap, load_sem.at[0]),
        pltpu.make_async_copy(ap_in, ap, load_sem.at[1]),
        pltpu.make_async_copy(p_in, pp.at[pl.ds(1, CX), pl.ds(8, CY)], load_sem.at[2]),
        pltpu.make_async_copy(av_in, avel, load_sem.at[3]),
        pltpu.make_async_copy(mask_in, mask, load_sem.at[4]),
        pltpu.make_async_copy(v_in, vel, load_sem.at[5]),
        pltpu.make_async_copy(drv_in, drv, load_sem.at[6]),
    ]
    small = [
        pltpu.make_async_copy(rows_in, rows_ref, small_sem.at[0]),
        pltpu.make_async_copy(angle_in, angle_ref, small_sem.at[1]),
        pltpu.make_async_copy(count_in, count_ref, small_sem.at[2]),
        pltpu.make_async_copy(cells_in, cells_ref, small_sem.at[3]),
        pltpu.make_async_copy(step_in, step_ref, small_sem.at[4]),
    ]
    for copy in small + loads:
        copy.start()

    plane = jnp.zeros((CY, CZ), F32)
    for ref in (pp, qq):
        ref[0, pl.ds(8, CY)] = plane
        ref[CX + 1, pl.ds(8, CY)] = plane
        for x in range(CX):
            ref[x + 1, pl.ds(0, 8)] = jnp.zeros((8, CZ), F32)
            ref[x + 1, pl.ds(CY + 8, 8)] = jnp.zeros((8, CZ), F32)
    lam0[0] = plane
    lam0[CX + 1] = plane
    for x in range(CX):
        lam1[x, pl.ds(0, 8)] = jnp.zeros((8, CZ), F32)
        lam1[x, pl.ds(CY + 8, 8)] = jnp.zeros((8, CZ), F32)
    zrecv[...] = jnp.zeros_like(zrecv)
    lrecv[...] = jnp.zeros_like(lrecv)

    barrier = pltpu.get_barrier_semaphore()

    def greet(device):
        pl.semaphore_signal(barrier, inc=1, device_id=device, device_id_type=MESH)

    def greet_line(k, _):
        greet(line_peer(k))
        return 0

    s_up, s_down = jnp.minimum(s + 1, ns - 1), jnp.maximum(s - 1, 0)
    r_up, r_down = jnp.minimum(r + 1, nr - 1), jnp.maximum(r - 1, 0)
    c_up, c_down = jnp.minimum(c + 1, nc - 1), jnp.maximum(c - 1, 0)
    has = {
        "xu": s < ns - 1, "xd": s > 0, "yu": r < nr - 1, "yd": r > 0, "zu": c < nc - 1, "zd": c > 0,
    }
    beyond = (
        (jnp.logical_and(zh == ZH - 1, has["zu"]), (s, r, c_up)),
        (jnp.logical_and(zh == 0, has["zd"]), (s, r, c_down)),
        (jnp.logical_and(zl == ZL - 1, has["xu"]), (s_up, r, c)),
        (jnp.logical_and(zl == 0, has["xd"]), (s_down, r, c)),
    )
    partners = NA - 1 + NB - 1
    for here, device in beyond:
        pl.when(here)(functools.partial(greet, device))
        partners = partners + here.astype(jnp.int32)
    for k in range(1, NA):
        greet(plane_peer(k))
    lax.fori_loop(1, NB, greet_line, 0)

    lane = lax.broadcasted_iota(jnp.int32, (1, WALL), 1)
    for copy in small:
        copy.wait()
    own_rows = rows_ref[0, 0]
    live = lane < count_ref[0, 0, 0]
    bits = own_rows >> 3
    owner_group = ((bits >> 6) << 2) + ((bits >> 1) & 3)
    owner_line = (((bits >> 4) & 3) << 2) + (((bits >> 3) & 1) << 1) + (bits & 1)
    code = owner_group * WIDTH + owner_line * OWN + (own_rows & (OWN - 1))
    slots[0, 0:1] = jnp.where(live, code.astype(F32), -1.0)
    slots[0, 1:2] = angle_ref[0, 0]
    row_at = (lax.broadcasted_iota(jnp.int32, (WIDTH, WALL), 0) + group * WIDTH).astype(F32)
    knots = lax.broadcasted_iota(jnp.int32, (ANG, WALL), 0).astype(F32)

    def prepare(k):
        hot[k] = jnp.where(slots[k, 0:1] == row_at, 1.0, 0.0).astype(BF16)
        dist = jnp.abs(slots[k, 1:2] - knots)
        dist = jnp.minimum(dist, ANG - dist)
        outer = jnp.maximum(2.0 - dist, 0.0)
        near = jnp.maximum(1.0 - dist, 0.0)
        weight[k] = (outer * outer * outer - 4.0 * near * near * near) * (1.0 / 6.0)

    prepare(0)

    own_cells = cells_ref[0, 0]
    own_xy = own_cells >> 7
    own_z = own_cells & (CZ - 1)
    xy = lax.broadcasted_iota(jnp.int32, (CY, WALL), 0)
    for x in range(CX):
        where_hot[x * CY:(x + 1) * CY] = jnp.where(xy + x * CY == own_xy, 1.0, 0.0).astype(BF16)

    loads[0].wait()
    loads[1].wait()
    rows_of = pl.ds(8, CY)
    for x in range(CX):
        qq[x + 1, rows_of] = kap[x] * ap[x]
    loads[2].wait()
    for ref, at in ((pp, 0), (qq, CX)):
        for x in range(CX):
            turned = ref[x + 1, rows_of].T
            zsend[at + x:at + x + 1] = turned[0:1]
            zsend[8 + at + x:8 + at + x + 1] = turned[CZ - 1:CZ]

    pl.semaphore_wait(barrier, partners)

    def slot_copy(k):
        return pltpu.make_async_remote_copy(
            src_ref=slots.at[0], dst_ref=slots.at[k],
            send_sem=slot_send, recv_sem=slot_recv.at[k],
            device_id=plane_peer(k), device_id_type=MESH,
        )

    def halo(src, dst, sem_at, send_sem, recv_sem, device):
        return pltpu.make_async_remote_copy(
            src_ref=src, dst_ref=dst, send_sem=send_sem.at[sem_at], recv_sem=recv_sem.at[sem_at],
            device_id=device, device_id_type=MESH,
        )


    def field_x(ref, base):
        return {
            "xu": halo(ref.at[CX, rows_of], ref.at[0, rows_of], base, halo_send, halo_recv, (s_up, r, c)),
            "xd": halo(ref.at[1, rows_of], ref.at[CX + 1, rows_of], base + 1, halo_send, halo_recv, (s_down, r, c)),
        }

    def field_y(ref, base):
        inner = pl.ds(1, CX)
        return {
            "yu": halo(ref.at[inner, pl.ds(CY, 8)], ref.at[inner, pl.ds(0, 8)], base, halo_send, halo_recv, (s, r_up, c)),
            "yd": halo(ref.at[inner, pl.ds(8, 8)], ref.at[inner, pl.ds(CY + 8, 8)], base + 1, halo_send, halo_recv, (s, r_down, c)),
        }

    q_x = field_x(qq, 0)
    p_x = field_x(pp, 2)
    q_y = field_y(qq, 4)
    p_y = field_y(pp, 6)
    pq_z = {
        "zu": halo(zsend.at[pl.ds(8, 8)], zrecv.at[pl.ds(0, 8)], 8, halo_send, halo_recv, (s, r, c_up)),
        "zd": halo(zsend.at[pl.ds(0, 8)], zrecv.at[pl.ds(8, 8)], 9, halo_send, halo_recv, (s, r, c_down)),
    }
    inner = pl.ds(0, CX)
    lam_x = {
        "xu": halo(lam0.at[CX], lam0.at[0], 0, lam_send, lam_recv, (s_up, r, c)),
        "xd": halo(lam0.at[1], lam0.at[CX + 1], 1, lam_send, lam_recv, (s_down, r, c)),
    }
    lam_y = {
        "yu": halo(lam1.at[inner, pl.ds(CY, 8)], lam1.at[inner, pl.ds(0, 8)], 2, lam_send, lam_recv, (s, r_up, c)),
        "yd": halo(lam1.at[inner, pl.ds(8, 8)], lam1.at[inner, pl.ds(CY + 8, 8)], 3, lam_send, lam_recv, (s, r_down, c)),
    }
    lam_z = {
        "zu": halo(lsend.at[pl.ds(8, 8)], lrecv.at[pl.ds(0, 8)], 4, lam_send, lam_recv, (s, r, c_up)),
        "zd": halo(lsend.at[pl.ds(0, 8)], lrecv.at[pl.ds(8, 8)], 5, lam_send, lam_recv, (s, r, c_down)),
    }

    def start(faces):
        for side, copy in faces.items():
            pl.when(has[side])(copy.start)

    opposite = {"xu": "xd", "xd": "xu", "yu": "yd", "yd": "yu", "zu": "zd", "zd": "zu"}

    def arrive(faces):
        for side, copy in faces.items():
            pl.when(has[opposite[side]])(copy.wait_recv)

    def sent(faces):
        for side, copy in faces.items():
            pl.when(has[side])(copy.wait_send)

    start(pq_z)
    for k in range(NA - 1, 0, -1):
        slot_copy(k).start()
    start(q_x)
    start(p_x)
    start(q_y)
    start(p_y)
    halos = [q_x, q_y, p_x, p_y, pq_z]

    def slots_of(k, _):
        pltpu.make_async_copy(slots.at[k], slots.at[k], slot_recv.at[k]).wait()
        prepare(k)
        return 0

    lax.fori_loop(1, NA, slots_of, 0)
    rest = slots.at[pl.ds(1, NA - 1)]

    phase = jnp.cos(0.5 * jnp.full((1, CZ), lax.rem(step_ref[0], 97).astype(F32), F32))
    for copy in loads[3:]:
        copy.wait()
    for faces in (q_x, q_y, p_x, p_y, pq_z):
        arrive(faces)
    edge_t = jnp.concatenate([zrecv[...], jnp.zeros((CZ - 16, CZ), F32)], axis=0).T
    at_z = lax.broadcasted_iota(jnp.int32, (CY, CZ), 1)

    def along_z(field, low, high):
        upper = jnp.where(at_z == CZ - 1, high, pltpu.roll(field, CZ - 1, 1))
        lower = jnp.where(at_z == 0, low, pltpu.roll(field, 1, 1))
        return (upper - lower) * 0.5

    def slopes(ref, x, at):
        mid = ref[x + 1, rows_of]
        return (
            (ref[x + 2, rows_of] - ref[x, rows_of]) * 0.5,
            (ref[x + 1, pl.ds(9, CY)] - ref[x + 1, pl.ds(7, CY)]) * 0.5,
            along_z(mid, edge_t[:, at + x:at + x + 1], edge_t[:, 8 + at + x:8 + at + x + 1]),
        )

    for x in range(CX):
        dp = slopes(pp, x, 0)
        dq = slopes(qq, x, CX)
        free = 1.0 - mask[x].astype(F32)
        total = [avel[k, x] + dq[k] for k in range(3)]
        lam0[x + 1] = free * total[0]
        lam1[x, rows_of] = free * total[1]
        lam2[x] = free * total[2]
        sens = -(
            total[0] * (vel[0, x] - 0.3 * dp[0] + drv[x] * phase)
            + total[1] * (vel[1, x] - 0.3 * dp[1])
            + total[2] * (vel[2, x] - 0.3 * dp[2])
        )
        for i, piece in enumerate(pieces(sens.T)):
            sens_t[i * CZ:(i + 1) * CZ, x * CY:(x + 1) * CY] = piece

    picked = jnp.dot(sens_t[...], where_hot[...], preferred_element_type=F32)
    picked = picked[0:CZ] + picked[CZ:2 * CZ] + picked[2 * CZ:3 * CZ]
    z_at = lax.broadcasted_iota(jnp.int32, (CZ, WALL), 0)
    vals[0] = jnp.sum(jnp.where(z_at == own_z, picked, 0.0), axis=0, keepdims=True)

    for k in range(NA - 1, 0, -1):
        pltpu.make_async_remote_copy(
            src_ref=vals.at[0], dst_ref=vals.at[k], send_sem=val_send, recv_sem=val_recv.at[k],
            device_id=plane_peer(k), device_id_type=MESH,
        ).start()

    start(lam_x)
    start(lam_y)
    for x in range(CX):
        turned = lam2[x].T
        lsend[x:x + 1] = turned[0:1]
        lsend[8 + x:9 + x] = turned[CZ - 1:CZ]
    start(lam_z)
    stores = [
        pltpu.make_async_copy(lam0.at[pl.ds(1, CX)], av_out.at[0], store_sem.at[0]),
        pltpu.make_async_copy(lam1.at[pl.ds(0, CX), rows_of], av_out.at[1], store_sem.at[1]),
        pltpu.make_async_copy(lam2, av_out.at[2], store_sem.at[2]),
    ]
    for copy in stores:
        copy.start()

    def product(k):
        scaled = jnp.concatenate(pieces(weight[k] * vals[k]), axis=0)
        return lax.dot_general(hot[k], scaled, (((1,), (1,)), ((), ())), preferred_element_type=F32)

    def add_up(k, total):
        pltpu.make_async_copy(vals.at[k], vals.at[k], val_recv.at[k]).wait()
        return total + product(k)

    rest_vals = vals.at[pl.ds(1, NA - 1)]
    summed = lax.fori_loop(1, NA, add_up, product(0))
    summed = summed[:, 0:ANG] + summed[:, ANG:2 * ANG] + summed[:, 2 * ANG:3 * ANG]
    dense[...] = jnp.concatenate([summed, jnp.zeros_like(summed)], axis=1).reshape(NB, OWN, 2 * ANG)

    def send_part(k, _):
        peer = line_peer(k)
        other = (lax.rem(peer[0], ZL) * 2 + peer[1]) * ZH + lax.rem(peer[2], ZH)
        pltpu.make_async_remote_copy(
            src_ref=dense.at[other], dst_ref=parts.at[k - 1], send_sem=part_send, recv_sem=part_recv,
            device_id=peer, device_id_type=MESH,
        ).start()
        return 0

    lax.fori_loop(1, NB, send_part, 0)

    for faces in (lam_x, lam_y, lam_z):
        arrive(faces)
    edge_l = jnp.concatenate([lrecv[...], jnp.zeros((CZ - 16, CZ), F32)], axis=0).T
    for x in range(CX):
        div = (
            (lam0[x + 2] - lam0[x]) * 0.5
            + (lam1[x, pl.ds(9, CY)] - lam1[x, pl.ds(7, CY)]) * 0.5
            + along_z(lam2[x], edge_l[:, x:x + 1], edge_l[:, 8 + x:9 + x])
        )
        apo[x] = ap[x] + 0.3 * div
    last = pltpu.make_async_copy(apo, ap_out, store_sem.at[3])
    last.start()

    pltpu.make_async_copy(parts, parts, part_recv).wait()
    grad_out[...] = (dense[b] + jnp.sum(parts[...], axis=0))[:, 0:ANG]

    for faces in (q_x, q_y, p_x, p_y, pq_z, lam_x, lam_y, lam_z):
        sent(faces)
    pltpu.make_async_copy(rest, rest, slot_send).wait()
    pltpu.make_async_copy(rest_vals, rest_vals, val_send).wait()
    pltpu.make_async_copy(parts, parts, part_send).wait()
    for copy in stores + [last]:
        copy.wait()


def written(outs):
    anyspace = pl.BlockSpec(memory_space=pl.ANY)
    return pl.pallas_call(
        hand3,
        out_shape=tuple(jax.ShapeDtypeStruct(o.shape, o.dtype) for o in outs),
        in_specs=[anyspace] * 3,
        out_specs=(anyspace,) * 3,
        scratch_shapes=[pltpu.SemaphoreType.DMA((3,))],
        compiler_params=pltpu.CompilerParams(vmem_limit_bytes=1024 * 1024),
    )(*outs)


def hand3(a, b, c, d, e, f, sem):
    copies = [pltpu.make_async_copy(x, y, sem.at[i]) for i, (x, y) in enumerate(((a, d), (b, e), (c, f)))]
    for copy in copies:
        copy.start()
    for copy in copies:
        copy.wait()


def local(ns, nr, nc, *args):
    hbm = pl.BlockSpec(memory_space=pltpu.HBM)
    vmem = pl.BlockSpec(memory_space=pltpu.VMEM)
    block = (CX, CY, CZ)
    dma = pltpu.SemaphoreType.DMA
    return written(pl.pallas_call(
        functools.partial(kernel, ns, nr, nc),
        out_shape=(
            pltpu.VMEM(block, F32),
            pltpu.VMEM((3,) + block, F32),
            pltpu.VMEM((OWN, ANG), F32),
        ),
        in_specs=[hbm] * 12,
        out_specs=(pl.BlockSpec(memory_space=pl.ANY), pl.BlockSpec(memory_space=pl.ANY), vmem),
        scratch_shapes=[
            pltpu.VMEM((1, 1, 1, WALL), jnp.int32),
            pltpu.VMEM((1, 1, 1, WALL), jnp.int32),
            pltpu.VMEM((1, 1, 1, WALL), F32),
            pltpu.SMEM((1, 1, 1), jnp.int32),
            pltpu.SMEM((1,), jnp.int32),
            pltpu.VMEM((CX + 2, CY + 16, CZ), F32),
            pltpu.VMEM((CX + 2, CY + 16, CZ), F32),
            pltpu.VMEM(block, F32),
            pltpu.VMEM(block, F32),
            pltpu.VMEM(block, F32),
            pltpu.VMEM((3,) + block, F32),
            pltpu.VMEM((3,) + block, F32),
            pltpu.VMEM(block, jnp.int32),
            pltpu.VMEM((CX + 2, CY, CZ), F32),
            pltpu.VMEM((CX, CY + 16, CZ), F32),
            pltpu.VMEM(block, F32),
            pltpu.VMEM(block, F32),
            pltpu.VMEM((16, CY), F32),
            pltpu.VMEM((16, CY), F32),
            pltpu.VMEM((16, CY), F32),
            pltpu.VMEM((16, CY), F32),
            pltpu.VMEM((NA, 2, WALL), F32),
            pltpu.VMEM((NA, 1, WALL), F32),
            pltpu.VMEM((NA, WIDTH, WALL), BF16),
            pltpu.VMEM((NA, ANG, WALL), F32),
            pltpu.VMEM((CX * CY, WALL), BF16),
            pltpu.VMEM((3 * CZ, CX * CY), BF16),
            pltpu.VMEM((NB, OWN, 2 * ANG), F32),
            pltpu.VMEM((NB - 1, OWN, 2 * ANG), F32),
            dma((5,)), dma((7,)), dma((4,)), dma((10,)), dma((10,)), dma((6,)), dma((6,)),
            dma, dma((NA,)), dma, dma((NA,)), dma, dma,
        ],
        compiler_params=pltpu.CompilerParams(
            collective_id=0, has_side_effects=True, vmem_limit_bytes=62 * 1024 * 1024 + 512 * 1024
        ),
        cost_estimate=pl.CostEstimate(flops=10**9, bytes_accessed=4 * 10**6, transcendentals=0),
    )(*args))


def solution(mesh):
    names = ("slab", "row", "col")
    sizes = tuple(mesh.shape[name] for name in names)
    cells = P(*names)
    vector = P(None, *names)
    slot = P(*names, None)
    in_specs = (cells, vector, cells, cells, cells, vector, cells, slot, slot, slot, cells, P())
    out_specs = (cells, vector, P(names, None))
    return jax.shard_map(
        functools.partial(local, *sizes), mesh=mesh, in_specs=in_specs, out_specs=out_specs, check_vma=False
    )
```

```python
import functools

import jax
import jax.numpy as jnp
from jax import lax
from jax.experimental import pallas as pl
from jax.experimental.pallas import tpu as pltpu
from jax.sharding import PartitionSpec as P

ANG = 64
CX = 4
CY = 128
CZ = 128
WALL = 512
OWN = 8
NXC = 4
NYC = 4
ZL = 4
ZH = 2
NA = NXC * NYC
NB = 2 * ZL * ZH
WIDTH = NB * OWN
BATCHES = (0, 5, 11, 16)
MESH = pl.DeviceIdType.MESH
PLANE = sorted(
    ((dy, dx) for dy in range(NYC) for dx in range(NXC)),
    key=lambda d: (min(d[0], NYC - d[0]) + min(d[1], NXC - d[1]), d),
)
F32 = jnp.float32
BF16 = jnp.bfloat16


def pieces(value):
    high = value.astype(BF16)
    rest = value - high.astype(F32)
    mid = rest.astype(BF16)
    low = (rest - mid.astype(F32)).astype(BF16)
    return high, mid, low


def kernel(
    ns, nr, nc,
    p_in, v_in, kap_in, drv_in, ap_in, av_in, mask_in, cells_in, rows_in, angle_in, count_in, step_in,
    ap_out, av_out, grad_out,
    cells_ref, rows_ref, angle_ref, count_ref, step_ref,
    pp, qq, kap, drv, ap, vel, total, mask,
    lam0, lam1, lam2, apo, sums, q_near,
    zsend, zrecv, lsend, lrecv,
    turned_face, turned_wrap, face_parts, wrap_parts, slot_parts,
    cells_buf, answer, answered,
    slots, vals, hot, weight, where_hot, sens_t, dense, parts,
    small_sem, load_sem, store_sem, halo_send, halo_recv, lam_send, lam_recv,
    wrap_send, wrap_recv, cell_send, cell_recv, answer_send, answer_recv,
    slot_send, slot_recv, val_send, val_recv, part_send, part_recv,
):
    s = lax.axis_index("slab")
    r = lax.axis_index("row")
    c = lax.axis_index("col")
    y, zl = lax.div(s, ZL), lax.rem(s, ZL)
    x_at, zh = lax.div(c, ZH), lax.rem(c, ZH)
    group = y * NXC + x_at
    b = (zl * 2 + r) * ZH + zh

    def plane_peer(k):
        dy, dx = PLANE[k]
        return (lax.rem(y + dy, NYC) * ZL + zl, r, lax.rem(x_at + dx, NXC) * ZH + zh)

    def line_peer(k):
        other_zl = lax.rem(zl + lax.div(k, 2 * ZH), ZL)
        other_r = lax.rem(r + lax.rem(lax.div(k, ZH), 2), 2)
        other_zh = lax.rem(zh + lax.rem(k, ZH), ZH)
        return (y * ZL + other_zl, other_r, x_at * ZH + other_zh)

    loads = [
        pltpu.make_async_copy(kap_in, kap, load_sem.at[0]),
        pltpu.make_async_copy(ap_in, ap, load_sem.at[1]),
        pltpu.make_async_copy(p_in, pp.at[pl.ds(0, CX), pl.ds(8, CY)], load_sem.at[2]),
        pltpu.make_async_copy(av_in, total, load_sem.at[3]),
        pltpu.make_async_copy(mask_in, mask, load_sem.at[4]),
        pltpu.make_async_copy(v_in, vel, load_sem.at[5]),
        pltpu.make_async_copy(drv_in, drv, load_sem.at[6]),
    ]
    small = [
        pltpu.make_async_copy(rows_in, rows_ref, small_sem.at[0]),
        pltpu.make_async_copy(angle_in, angle_ref, small_sem.at[1]),
        pltpu.make_async_copy(count_in, count_ref, small_sem.at[2]),
        pltpu.make_async_copy(cells_in, cells_ref, small_sem.at[3]),
        pltpu.make_async_copy(step_in, step_ref, small_sem.at[4]),
    ]
    for copy in small + loads:
        copy.start()

    plane = jnp.zeros((CY, CZ), F32)
    strip = jnp.zeros((8, CZ), F32)
    for ref in (pp, qq, lam1):
        for x in range(CX):
            ref[x, pl.ds(0, 8)] = strip
            ref[x, pl.ds(CY + 8, 8)] = strip
    for ref in (q_near, ):
        ref[0] = plane
        ref[1] = plane
    lam0[0] = plane
    lam0[CX + 1] = plane
    zrecv[...] = jnp.zeros_like(zrecv)
    lrecv[...] = jnp.zeros_like(lrecv)
    answered[...] = jnp.zeros_like(answered)

    barrier = pltpu.get_barrier_semaphore()

    def greet(device):
        pl.semaphore_signal(barrier, inc=1, device_id=device, device_id_type=MESH)

    def greet_line(k, _):
        greet(line_peer(k))
        return 0

    s_up, s_down = jnp.minimum(s + 1, ns - 1), jnp.maximum(s - 1, 0)
    r_up, r_down = jnp.minimum(r + 1, nr - 1), jnp.maximum(r - 1, 0)
    c_up, c_down = jnp.minimum(c + 1, nc - 1), jnp.maximum(c - 1, 0)
    has = {
        "xu": s < ns - 1, "xd": s > 0, "yu": r < nr - 1, "yd": r > 0, "zu": c < nc - 1, "zd": c > 0,
    }
    wrap_up = jnp.logical_and(zl == ZL - 1, has["xu"])
    wrap_down = jnp.logical_and(zl == 0, has["xd"])
    near_up = zl < ZL - 1
    near_down = zl > 0
    beyond = (
        (jnp.logical_and(zh == ZH - 1, has["zu"]), (s, r, c_up)),
        (jnp.logical_and(zh == 0, has["zd"]), (s, r, c_down)),
        (wrap_up, (s_up, r, c)),
        (wrap_down, (s_down, r, c)),
    )
    partners = NA - 1 + NB - 1
    for here, device in beyond:
        pl.when(here)(functools.partial(greet, device))
        partners = partners + here.astype(jnp.int32)
    for k in range(1, NA):
        greet(plane_peer(k))
    lax.fori_loop(1, NB, greet_line, 0)

    lane = lax.broadcasted_iota(jnp.int32, (1, WALL), 1)
    for copy in small:
        copy.wait()
    own_rows = rows_ref[0, 0]
    live = lane < count_ref[0, 0, 0]
    bits = own_rows >> 3
    owner_group = ((bits >> 6) << 2) + ((bits >> 1) & 3)
    owner_line = (((bits >> 4) & 3) << 2) + (((bits >> 3) & 1) << 1) + (bits & 1)
    code = owner_group * WIDTH + owner_line * OWN + (own_rows & (OWN - 1))
    slots[0, 0:1] = jnp.where(live, code.astype(F32), -1.0)
    slots[0, 1:2] = angle_ref[0, 0]
    row_at = (lax.broadcasted_iota(jnp.int32, (WIDTH, WALL), 0) + group * WIDTH).astype(F32)
    knots = lax.broadcasted_iota(jnp.int32, (ANG, WALL), 0).astype(F32)

    def at_slots(k):
        return pl.ds(pl.multiple_of(k * WALL, WALL), WALL)

    def prepare(k):
        hot[:, at_slots(k)] = jnp.where(slots[k, 0:1] == row_at, 1.0, 0.0).astype(BF16)
        dist = jnp.abs(slots[k, 1:2] - knots)
        dist = jnp.minimum(dist, ANG - dist)
        outer = jnp.maximum(2.0 - dist, 0.0)
        near = jnp.maximum(1.0 - dist, 0.0)
        weight[k] = (outer * outer * outer - 4.0 * near * near * near) * (1.0 / 6.0)

    prepare(0)

    own_cells = cells_ref[0, 0]
    cells_buf[0] = own_cells
    own_xy = own_cells >> 7
    own_x = own_cells >> 14
    own_z = own_cells & (CZ - 1)
    y_at = lax.broadcasted_iota(jnp.int32, (CY, WALL), 0)
    for x in range(CX):
        where_hot[x * CY:(x + 1) * CY] = jnp.where(y_at + x * CY == own_xy, 1.0, 0.0).astype(BF16)

    loads[0].wait()
    loads[1].wait()
    rows_of = pl.ds(8, CY)
    for x in range(CX):
        qq[x, rows_of] = kap[x] * ap[x]
    loads[2].wait()
    for i, (ref, at) in enumerate(((pp, 0), (qq, CX))):
        for x in range(CX):
            turned = ref[x, rows_of].T
            zsend[at + x:at + x + 1] = turned[0:1]
            zsend[8 + at + x:8 + at + x + 1] = turned[CZ - 1:CZ]
            if x in (0, CX - 1):
                turned_face[x // (CX - 1), i] = turned

    def split_into(ref, first, second):
        for i, field in enumerate((first, second)):
            for j, piece in enumerate(pieces(field)):
                ref[(3 * i + j) * CZ:(3 * i + j + 1) * CZ] = piece

    for side in range(2):
        split_into(face_parts.at[side], turned_face[side, 0], turned_face[side, 1])

    def pick(ref, hot_y, at_z):
        got = jnp.dot(ref[...], hot_y, preferred_element_type=F32)
        out = []
        for i in range(2):
            field = got[3 * i * CZ:(3 * i + 1) * CZ]
            field = field + got[(3 * i + 1) * CZ:(3 * i + 2) * CZ] + got[(3 * i + 2) * CZ:(3 * i + 3) * CZ]
            out.append(jnp.sum(jnp.where(y_at == at_z, field, 0.0), axis=0, keepdims=True))
        return out

    def hot_y_of(cells):
        return jnp.where(y_at == ((cells >> 7) & (CY - 1)), 1.0, 0.0).astype(BF16)

    pl.semaphore_wait(barrier, partners)

    def slot_copy(k):
        return pltpu.make_async_remote_copy(
            src_ref=slots.at[0], dst_ref=slots.at[k],
            send_sem=slot_send, recv_sem=slot_recv.at[k],
            device_id=plane_peer(k), device_id_type=MESH,
        )

    def halo(src, dst, sem_at, send_sem, recv_sem, device):
        return pltpu.make_async_remote_copy(
            src_ref=src, dst_ref=dst, send_sem=send_sem.at[sem_at], recv_sem=recv_sem.at[sem_at],
            device_id=device, device_id_type=MESH,
        )


    inner = pl.ds(0, CX)
    q_x = {
        "xu": halo(qq.at[CX - 1, rows_of], q_near.at[0], 0, halo_send, halo_recv, (s_up, r, c)),
        "xd": halo(qq.at[0, rows_of], q_near.at[1], 1, halo_send, halo_recv, (s_down, r, c)),
    }

    def field_y(ref, base):
        return {
            "yu": halo(ref.at[inner, pl.ds(CY, 8)], ref.at[inner, pl.ds(0, 8)], base, halo_send, halo_recv, (s, r_up, c)),
            "yd": halo(ref.at[inner, pl.ds(8, 8)], ref.at[inner, pl.ds(CY + 8, 8)], base + 1, halo_send, halo_recv, (s, r_down, c)),
        }

    q_y = field_y(qq, 4)
    p_y = field_y(pp, 6)
    wrap = {
        "xu": halo(turned_face.at[1], turned_wrap, 0, wrap_send, wrap_recv, (s_up, r, c)),
        "xd": halo(turned_face.at[0], turned_wrap, 1, wrap_send, wrap_recv, (s_down, r, c)),
    }
    ask = {
        "xu": halo(cells_buf.at[0], cells_buf.at[1], 0, cell_send, cell_recv, (s_up, r, c)),
        "xd": halo(cells_buf.at[0], cells_buf.at[2], 1, cell_send, cell_recv, (s_down, r, c)),
    }
    reply = {
        "xu": halo(answer.at[1], answered.at[0], 0, answer_send, answer_recv, (s_up, r, c)),
        "xd": halo(answer.at[0], answered.at[1], 1, answer_send, answer_recv, (s_down, r, c)),
    }
    pq_z = {
        "zu": halo(zsend.at[pl.ds(8, 8)], zrecv.at[pl.ds(0, 8)], 8, halo_send, halo_recv, (s, r, c_up)),
        "zd": halo(zsend.at[pl.ds(0, 8)], zrecv.at[pl.ds(8, 8)], 9, halo_send, halo_recv, (s, r, c_down)),
    }
    lam_x = {
        "xu": halo(lam0.at[CX], lam0.at[0], 0, lam_send, lam_recv, (s_up, r, c)),
        "xd": halo(lam0.at[1], lam0.at[CX + 1], 1, lam_send, lam_recv, (s_down, r, c)),
    }
    lam_y = {
        "yu": halo(lam1.at[inner, pl.ds(CY, 8)], lam1.at[inner, pl.ds(0, 8)], 2, lam_send, lam_recv, (s, r_up, c)),
        "yd": halo(lam1.at[inner, pl.ds(8, 8)], lam1.at[inner, pl.ds(CY + 8, 8)], 3, lam_send, lam_recv, (s, r_down, c)),
    }
    lam_z = {
        "zu": halo(lsend.at[pl.ds(8, 8)], lrecv.at[pl.ds(0, 8)], 4, lam_send, lam_recv, (s, r, c_up)),
        "zd": halo(lsend.at[pl.ds(0, 8)], lrecv.at[pl.ds(8, 8)], 5, lam_send, lam_recv, (s, r, c_down)),
    }

    def start(faces):
        for side, copy in faces.items():
            pl.when(has[side])(copy.start)

    opposite = {"xu": "xd", "xd": "xu", "yu": "yd", "yd": "yu", "zu": "zd", "zd": "zu"}

    def arrive(faces):
        for side, copy in faces.items():
            pl.when(has[opposite[side]])(copy.wait_recv)

    def sent(faces):
        for side, copy in faces.items():
            pl.when(has[side])(copy.wait_send)

    pl.when(wrap_up)(wrap["xu"].start)
    pl.when(wrap_down)(wrap["xd"].start)
    start(pq_z)
    pl.when(near_up)(ask["xu"].start)
    pl.when(near_down)(ask["xd"].start)
    start(q_y)
    start(p_y)
    for k in range(NA - 1, 0, -1):
        slot_copy(k).start()

    phase = jnp.cos(0.5 * jnp.full((1, CZ), lax.rem(step_ref[0], 97).astype(F32), F32))
    for copy in loads[3:]:
        copy.wait()
    arrive(q_y)
    arrive(p_y)

    def along_x(ref, x):
        if x == 0:
            return ref[1, rows_of] * 0.5
        if x == CX - 1:
            return ref[CX - 2, rows_of] * -0.5
        return (ref[x + 1, rows_of] - ref[x - 1, rows_of]) * 0.5

    def along_y(ref, x):
        return (ref[x, pl.ds(9, CY)] - ref[x, pl.ds(7, CY)]) * 0.5

    for x in range(CX):
        total_0 = total[0, x] + along_x(qq, x)
        total_1 = total[1, x] + along_y(qq, x)
        total[0, x] = total_0
        total[1, x] = total_1
        moved_0 = vel[0, x] - 0.3 * along_x(pp, x) + drv[x] * phase
        sums[x] = total_0 * moved_0 + total_1 * (vel[1, x] - 0.3 * along_y(pp, x))
        if x in (0, CX - 1):
            split_into(slot_parts.at[x // (CX - 1)], total_0.T, moved_0.T)

    def serve(side, at):
        cells = cells_buf[at]
        p_at, q_at = pick(face_parts.at[side], hot_y_of(cells), cells & (CZ - 1))
        answer[side, 0:1] = p_at
        answer[side, 1:2] = q_at

    @pl.when(near_up)
    def _():
        ask["xd"].wait_recv()
        serve(1, 2)
        reply["xu"].start()

    @pl.when(near_down)
    def _():
        ask["xu"].wait_recv()
        serve(0, 1)
        reply["xd"].start()

    pl.when(near_up)(q_x["xu"].start)
    pl.when(near_down)(q_x["xd"].start)

    on_face = [
        pick(slot_parts.at[side], where_hot[side * (CX - 1) * CY:(side * (CX - 1) + 1) * CY], own_z)
        for side in range(2)
    ]

    def slots_of(k, _):
        pltpu.make_async_copy(slots.at[k], slots.at[k], slot_recv.at[k]).wait()
        prepare(k)
        return 0

    lax.fori_loop(1, BATCHES[1], slots_of, 0)
    rest = slots.at[pl.ds(1, NA - 1)]

    arrive(pq_z)
    edge_t = jnp.concatenate([zrecv[...], jnp.zeros((CZ - 16, CZ), F32)], axis=0).T
    at_z = lax.broadcasted_iota(jnp.int32, (CY, CZ), 1)

    def along_z(field, low, high):
        upper = jnp.where(at_z == CZ - 1, high, pltpu.roll(field, CZ - 1, 1))
        lower = jnp.where(at_z == 0, low, pltpu.roll(field, 1, 1))
        return (upper - lower) * 0.5

    for x in range(CX):
        dp = along_z(pp[x, rows_of], edge_t[:, x:x + 1], edge_t[:, 8 + x:9 + x])
        dq = along_z(qq[x, rows_of], edge_t[:, CX + x:CX + x + 1], edge_t[:, 8 + CX + x:9 + CX + x])
        total_2 = total[2, x] + dq
        total[2, x] = total_2
        sens = -(sums[x] + total_2 * (vel[2, x] - 0.3 * dp))
        for i, piece in enumerate(pieces(sens.T)):
            sens_t[i * CZ:(i + 1) * CZ, x * CY:(x + 1) * CY] = piece

    picked = jnp.dot(sens_t[...], where_hot[...], preferred_element_type=F32)
    picked = picked[0:CZ] + picked[CZ:2 * CZ] + picked[2 * CZ:3 * CZ]
    picked = jnp.sum(jnp.where(y_at == own_z, picked, 0.0), axis=0, keepdims=True)

    pl.when(near_down)(reply["xu"].wait_recv)
    pl.when(near_up)(reply["xd"].wait_recv)

    def own_answer(side):
        split_into(wrap_parts, turned_wrap[0], turned_wrap[1])
        p_at, q_at = pick(wrap_parts, hot_y_of(cells_buf[0]), cells_buf[0] & (CZ - 1))
        answered[side, 0:1] = p_at
        answered[side, 1:2] = q_at

    @pl.when(wrap_down)
    def _():
        wrap["xu"].wait_recv()
        own_answer(0)

    @pl.when(wrap_up)
    def _():
        wrap["xd"].wait_recv()
        own_answer(1)

    for side, (total_at, moved_at) in enumerate(on_face):
        sign = 2.0 * side - 1.0
        here = own_x == side * (CX - 1)
        more_total = jnp.where(here, answered[side, 1:2], 0.0) * (0.5 * sign)
        more_moved = jnp.where(here, answered[side, 0:1], 0.0) * (-0.15 * sign)
        picked = picked - (more_total * (moved_at + more_moved) + total_at * more_moved)
    vals[0] = picked

    for k in range(NA - 1, 0, -1):
        pltpu.make_async_remote_copy(
            src_ref=vals.at[0], dst_ref=vals.at[k], send_sem=val_send, recv_sem=val_recv.at[k],
            device_id=plane_peer(k), device_id_type=MESH,
        ).start()

    pl.when(near_down)(q_x["xu"].wait_recv)
    pl.when(near_up)(q_x["xd"].wait_recv)

    @pl.when(wrap_down)
    def _():
        q_near[0] = turned_wrap[1].T

    @pl.when(wrap_up)
    def _():
        q_near[1] = turned_wrap[1].T

    for x in range(CX):
        free = 1.0 - mask[x].astype(F32)
        total_0 = total[0, x]
        if x == 0:
            total_0 = total_0 - q_near[0] * 0.5
        if x == CX - 1:
            total_0 = total_0 + q_near[1] * 0.5
        lam0[x + 1] = free * total_0
        lam1[x, rows_of] = free * total[1, x]
        lam2[x] = free * total[2, x]

    start(lam_x)
    start(lam_y)
    for x in range(CX):
        turned = lam2[x].T
        lsend[x:x + 1] = turned[0:1]
        lsend[8 + x:9 + x] = turned[CZ - 1:CZ]
    start(lam_z)
    stores = [
        pltpu.make_async_copy(lam0.at[pl.ds(1, CX)], av_out.at[0], store_sem.at[0]),
        pltpu.make_async_copy(lam1.at[pl.ds(0, CX), rows_of], av_out.at[1], store_sem.at[1]),
        pltpu.make_async_copy(lam2, av_out.at[2], store_sem.at[2]),
    ]
    for copy in stores:
        copy.start()

    lax.fori_loop(BATCHES[1], NA, slots_of, 0)

    rest_vals = vals.at[pl.ds(1, NA - 1)]
    summed = None
    for low, high in zip(BATCHES[:-1], BATCHES[1:]):
        for k in range(max(low, 1), high):
            pltpu.make_async_copy(vals.at[k], vals.at[k], val_recv.at[k]).wait()
        split = [pieces(weight[k] * vals[k]) for k in range(low, high)]
        scaled = jnp.concatenate(
            [jnp.concatenate([one[i] for one in split], axis=1) for i in range(3)], axis=0
        )
        product = lax.dot_general(
            hot[:, low * WALL:high * WALL], scaled, (((1,), (1,)), ((), ())), preferred_element_type=F32
        )
        summed = product if summed is None else summed + product
    summed = summed[:, 0:ANG] + summed[:, ANG:2 * ANG] + summed[:, 2 * ANG:3 * ANG]
    dense[...] = jnp.concatenate([summed, jnp.zeros_like(summed)], axis=1).reshape(NB, OWN, 2 * ANG)

    def send_part(k, _):
        peer = line_peer(k)
        other = (lax.rem(peer[0], ZL) * 2 + peer[1]) * ZH + lax.rem(peer[2], ZH)
        pltpu.make_async_remote_copy(
            src_ref=dense.at[other], dst_ref=parts.at[k - 1], send_sem=part_send, recv_sem=part_recv,
            device_id=peer, device_id_type=MESH,
        ).start()
        return 0

    lax.fori_loop(1, NB, send_part, 0)

    for faces in (lam_x, lam_y, lam_z):
        arrive(faces)
    edge_l = jnp.concatenate([lrecv[...], jnp.zeros((CZ - 16, CZ), F32)], axis=0).T
    for x in range(CX):
        div = (
            (lam0[x + 2] - lam0[x]) * 0.5
            + (lam1[x, pl.ds(9, CY)] - lam1[x, pl.ds(7, CY)]) * 0.5
            + along_z(lam2[x], edge_l[:, x:x + 1], edge_l[:, 8 + x:9 + x])
        )
        apo[x] = ap[x] + 0.3 * div
    last = pltpu.make_async_copy(apo, ap_out, store_sem.at[3])
    last.start()

    pltpu.make_async_copy(parts, parts, part_recv).wait()
    grad_out[...] = (dense[b] + jnp.sum(parts[...], axis=0))[:, 0:ANG]

    for faces in (q_y, p_y, pq_z, lam_x, lam_y, lam_z):
        sent(faces)
    pl.when(wrap_up)(wrap["xu"].wait_send)
    pl.when(wrap_down)(wrap["xd"].wait_send)
    for faces in (ask, reply, q_x):
        pl.when(near_up)(faces["xu"].wait_send)
        pl.when(near_down)(faces["xd"].wait_send)
    pltpu.make_async_copy(rest, rest, slot_send).wait()
    pltpu.make_async_copy(rest_vals, rest_vals, val_send).wait()
    pltpu.make_async_copy(parts, parts, part_send).wait()
    for copy in stores + [last]:
        copy.wait()


def written(outs):
    anyspace = pl.BlockSpec(memory_space=pl.ANY)
    return pl.pallas_call(
        hand3,
        out_shape=tuple(jax.ShapeDtypeStruct(o.shape, o.dtype) for o in outs),
        in_specs=[anyspace] * 3,
        out_specs=(anyspace,) * 3,
        scratch_shapes=[pltpu.SemaphoreType.DMA((3,))],
        compiler_params=pltpu.CompilerParams(vmem_limit_bytes=1024 * 1024),
    )(*outs)


def hand3(a, b, c, d, e, f, sem):
    copies = [pltpu.make_async_copy(x, y, sem.at[i]) for i, (x, y) in enumerate(((a, d), (b, e), (c, f)))]
    for copy in copies:
        copy.start()
    for copy in copies:
        copy.wait()


def local(ns, nr, nc, *args):
    hbm = pl.BlockSpec(memory_space=pltpu.HBM)
    vmem = pl.BlockSpec(memory_space=pltpu.VMEM)
    block = (CX, CY, CZ)
    dma = pltpu.SemaphoreType.DMA
    return written(pl.pallas_call(
        functools.partial(kernel, ns, nr, nc),
        out_shape=(
            pltpu.VMEM(block, F32),
            pltpu.VMEM((3,) + block, F32),
            pltpu.VMEM((OWN, ANG), F32),
        ),
        in_specs=[hbm] * 12,
        out_specs=(pl.BlockSpec(memory_space=pl.ANY), pl.BlockSpec(memory_space=pl.ANY), vmem),
        scratch_shapes=[
            pltpu.VMEM((1, 1, 1, WALL), jnp.int32),
            pltpu.VMEM((1, 1, 1, WALL), jnp.int32),
            pltpu.VMEM((1, 1, 1, WALL), F32),
            pltpu.SMEM((1, 1, 1), jnp.int32),
            pltpu.SMEM((1,), jnp.int32),
            pltpu.VMEM((CX, CY + 16, CZ), F32),
            pltpu.VMEM((CX, CY + 16, CZ), F32),
            pltpu.VMEM(block, F32),
            pltpu.VMEM(block, F32),
            pltpu.VMEM(block, F32),
            pltpu.VMEM((3,) + block, F32),
            pltpu.VMEM((3,) + block, F32),
            pltpu.VMEM(block, jnp.int32),
            pltpu.VMEM((CX + 2, CY, CZ), F32),
            pltpu.VMEM((CX, CY + 16, CZ), F32),
            pltpu.VMEM(block, F32),
            pltpu.VMEM(block, F32),
            pltpu.VMEM(block, F32),
            pltpu.VMEM((2, CY, CZ), F32),
            pltpu.VMEM((16, CY), F32),
            pltpu.VMEM((16, CY), F32),
            pltpu.VMEM((16, CY), F32),
            pltpu.VMEM((16, CY), F32),
            pltpu.VMEM((2, 2, CZ, CY), F32),
            pltpu.VMEM((2, CZ, CY), F32),
            pltpu.VMEM((2, 6 * CZ, CY), BF16),
            pltpu.VMEM((6 * CZ, CY), BF16),
            pltpu.VMEM((2, 6 * CZ, CY), BF16),
            pltpu.VMEM((3, 1, WALL), jnp.int32),
            pltpu.VMEM((2, 2, WALL), F32),
            pltpu.VMEM((2, 2, WALL), F32),
            pltpu.VMEM((NA, 2, WALL), F32),
            pltpu.VMEM((NA, 1, WALL), F32),
            pltpu.VMEM((WIDTH, NA * WALL), BF16),
            pltpu.VMEM((NA, ANG, WALL), F32),
            pltpu.VMEM((CX * CY, WALL), BF16),
            pltpu.VMEM((3 * CZ, CX * CY), BF16),
            pltpu.VMEM((NB, OWN, 2 * ANG), F32),
            pltpu.VMEM((NB - 1, OWN, 2 * ANG), F32),
            dma((5,)), dma((7,)), dma((4,)), dma((10,)), dma((10,)), dma((6,)), dma((6,)),
            dma((2,)), dma((2,)), dma((2,)), dma((2,)), dma((2,)), dma((2,)),
            dma, dma((NA,)), dma, dma((NA,)), dma, dma,
        ],
        compiler_params=pltpu.CompilerParams(
            collective_id=0, has_side_effects=True, vmem_limit_bytes=62 * 1024 * 1024 + 512 * 1024
        ),
        cost_estimate=pl.CostEstimate(flops=10**9, bytes_accessed=4 * 10**6, transcendentals=0),
    )(*args))


def solution(mesh):
    names = ("slab", "row", "col")
    sizes = tuple(mesh.shape[name] for name in names)
    cells = P(*names)
    vector = P(None, *names)
    slot = P(*names, None)
    in_specs = (cells, vector, cells, cells, cells, vector, cells, slot, slot, slot, cells, P())
    out_specs = (cells, vector, P(names, None))
    return jax.shard_map(
        functools.partial(local, *sizes), mesh=mesh, in_specs=in_specs, out_specs=out_specs, check_vma=False
    )
```

```python
import functools

import jax
import jax.numpy as jnp
from jax import lax
from jax.experimental import pallas as pl
from jax.experimental.pallas import tpu as pltpu
from jax.sharding import PartitionSpec as P

ANG = 64
CX = 4
CY = 128
CZ = 128
WALL = 512
OWN = 8
NXC = 4
NYC = 4
ZL = 4
ZH = 2
NA = NXC * NYC
NB = 2 * ZL * ZH
WIDTH = NB * OWN
BATCHES = (0, 5, 11, 16)
MESH = pl.DeviceIdType.MESH
PLANE = sorted(
    ((dy, dx) for dy in range(NYC) for dx in range(NXC)),
    key=lambda d: (min(d[0], NYC - d[0]) + min(d[1], NXC - d[1]), d),
)
F32 = jnp.float32
BF16 = jnp.bfloat16


def pieces(value):
    high = value.astype(BF16)
    rest = value - high.astype(F32)
    mid = rest.astype(BF16)
    low = (rest - mid.astype(F32)).astype(BF16)
    return high, mid, low


def kernel(
    ns, nr, nc,
    p_in, v_in, kap_in, drv_in, ap_in, av_in, mask_in, cells_in, rows_in, angle_in, count_in, step_in,
    ap_out, av_out, grad_out,
    cells_ref, rows_ref, angle_ref, count_ref, step_ref,
    pp, qq, kap, drv, ap, vel, total, mask,
    lam0, lam1, lam2, apo, q_near,
    zsend, zrecv, lsend, lrecv,
    turned_face, turned_wrap, face_parts, wrap_parts, slot_parts,
    cells_buf, answer, answered,
    ends, own_hot_y,
    slots, vals, hot, weight, where_hot, sens_t, dense, parts,
    small_sem, load_sem, store_sem, halo_send, halo_recv, lam_send, lam_recv,
    wrap_send, wrap_recv, cell_send, cell_recv, answer_send, answer_recv,
    slot_send, slot_recv, val_send, val_recv, part_send, part_recv,
):
    s = lax.axis_index("slab")
    r = lax.axis_index("row")
    c = lax.axis_index("col")
    y, zl = lax.div(s, ZL), lax.rem(s, ZL)
    x_at, zh = lax.div(c, ZH), lax.rem(c, ZH)
    group = y * NXC + x_at
    b = (zl * 2 + r) * ZH + zh

    def plane_peer(k):
        dy, dx = PLANE[k]
        return (lax.rem(y + dy, NYC) * ZL + zl, r, lax.rem(x_at + dx, NXC) * ZH + zh)

    def line_peer(k):
        other_zl = lax.rem(zl + lax.div(k, 2 * ZH), ZL)
        other_r = lax.rem(r + lax.rem(lax.div(k, ZH), 2), 2)
        other_zh = lax.rem(zh + lax.rem(k, ZH), ZH)
        return (y * ZL + other_zl, other_r, x_at * ZH + other_zh)

    loads = [
        pltpu.make_async_copy(kap_in, kap, load_sem.at[0]),
        pltpu.make_async_copy(ap_in, ap, load_sem.at[1]),
        pltpu.make_async_copy(p_in, pp.at[pl.ds(0, CX), pl.ds(8, CY)], load_sem.at[2]),
        pltpu.make_async_copy(av_in, total, load_sem.at[3]),
        pltpu.make_async_copy(mask_in, mask, load_sem.at[4]),
        pltpu.make_async_copy(v_in, vel, load_sem.at[5]),
        pltpu.make_async_copy(drv_in, drv, load_sem.at[6]),
    ]
    small = [
        pltpu.make_async_copy(rows_in, rows_ref, small_sem.at[0]),
        pltpu.make_async_copy(angle_in, angle_ref, small_sem.at[1]),
        pltpu.make_async_copy(count_in, count_ref, small_sem.at[2]),
        pltpu.make_async_copy(cells_in, cells_ref, small_sem.at[3]),
        pltpu.make_async_copy(step_in, step_ref, small_sem.at[4]),
    ]
    for copy in small + loads:
        copy.start()

    plane = jnp.zeros((CY, CZ), F32)
    strip = jnp.zeros((8, CZ), F32)
    for ref in (pp, qq, lam1):
        for x in range(CX):
            ref[x, pl.ds(0, 8)] = strip
            ref[x, pl.ds(CY + 8, 8)] = strip
    for ref in (q_near, ):
        ref[0] = plane
        ref[1] = plane
    lam0[0] = plane
    lam0[CX + 1] = plane
    zrecv[...] = jnp.zeros_like(zrecv)
    lrecv[...] = jnp.zeros_like(lrecv)
    answered[...] = jnp.zeros_like(answered)

    barrier = pltpu.get_barrier_semaphore()

    def greet(device):
        pl.semaphore_signal(barrier, inc=1, device_id=device, device_id_type=MESH)

    def greet_line(k, _):
        greet(line_peer(k))
        return 0

    s_up, s_down = jnp.minimum(s + 1, ns - 1), jnp.maximum(s - 1, 0)
    r_up, r_down = jnp.minimum(r + 1, nr - 1), jnp.maximum(r - 1, 0)
    c_up, c_down = jnp.minimum(c + 1, nc - 1), jnp.maximum(c - 1, 0)
    has = {
        "xu": s < ns - 1, "xd": s > 0, "yu": r < nr - 1, "yd": r > 0, "zu": c < nc - 1, "zd": c > 0,
    }
    wrap_up = jnp.logical_and(zl == ZL - 1, has["xu"])
    wrap_down = jnp.logical_and(zl == 0, has["xd"])
    near_up = zl < ZL - 1
    near_down = zl > 0
    beyond = (
        (jnp.logical_and(zh == ZH - 1, has["zu"]), (s, r, c_up)),
        (jnp.logical_and(zh == 0, has["zd"]), (s, r, c_down)),
        (wrap_up, (s_up, r, c)),
        (wrap_down, (s_down, r, c)),
    )
    partners = NA - 1 + NB - 1
    for here, device in beyond:
        pl.when(here)(functools.partial(greet, device))
        partners = partners + here.astype(jnp.int32)
    for k in range(1, NA):
        greet(plane_peer(k))
    lax.fori_loop(1, NB, greet_line, 0)

    lane = lax.broadcasted_iota(jnp.int32, (1, WALL), 1)
    for copy in small:
        copy.wait()
    own_rows = rows_ref[0, 0]
    live = lane < count_ref[0, 0, 0]
    bits = own_rows >> 3
    owner_group = ((bits >> 6) << 2) + ((bits >> 1) & 3)
    owner_line = (((bits >> 4) & 3) << 2) + (((bits >> 3) & 1) << 1) + (bits & 1)
    code = owner_group * WIDTH + owner_line * OWN + (own_rows & (OWN - 1))
    slots[0, 0:1] = jnp.where(live, code.astype(F32), -1.0)
    slots[0, 1:2] = angle_ref[0, 0]
    row_at = (lax.broadcasted_iota(jnp.int32, (WIDTH, WALL), 0) + group * WIDTH).astype(F32)
    knots = lax.broadcasted_iota(jnp.int32, (ANG, WALL), 0).astype(F32)

    def at_slots(k):
        return pl.ds(pl.multiple_of(k * WALL, WALL), WALL)

    def prepare(k):
        hot[:, at_slots(k)] = jnp.where(slots[k, 0:1] == row_at, 1.0, 0.0).astype(BF16)
        dist = jnp.abs(slots[k, 1:2] - knots)
        dist = jnp.minimum(dist, ANG - dist)
        outer = jnp.maximum(2.0 - dist, 0.0)
        near = jnp.maximum(1.0 - dist, 0.0)
        weight[k] = (outer * outer * outer - 4.0 * near * near * near) * (1.0 / 6.0)

    prepare(0)

    own_cells = cells_ref[0, 0]
    cells_buf[0] = own_cells
    own_xy = own_cells >> 7
    own_x = own_cells >> 14
    own_z = own_cells & (CZ - 1)
    y_at = lax.broadcasted_iota(jnp.int32, (CY, WALL), 0)
    for x in range(CX):
        where_hot[x * CY:(x + 1) * CY] = jnp.where(y_at + x * CY == own_xy, 1.0, 0.0).astype(BF16)

    loads[0].wait()
    loads[1].wait()
    rows_of = pl.ds(8, CY)
    for x in range(CX):
        qq[x, rows_of] = kap[x] * ap[x]
    loads[2].wait()
    for i, (ref, at) in enumerate(((pp, 0), (qq, CX))):
        for x in range(CX):
            turned = ref[x, rows_of].T
            zsend[at + x:at + x + 1] = turned[0:1]
            zsend[8 + at + x:8 + at + x + 1] = turned[CZ - 1:CZ]
            if x in (0, CX - 1):
                turned_face[x // (CX - 1), i] = turned

    def split_into(ref, first, second):
        for i, field in enumerate((first, second)):
            for j, piece in enumerate(pieces(field)):
                ref[(3 * i + j) * CZ:(3 * i + j + 1) * CZ] = piece

    for side in range(2):
        split_into(face_parts.at[side], turned_face[side, 0], turned_face[side, 1])

    def pick(ref, hot_y, at_z):
        got = jnp.dot(ref[...], hot_y, preferred_element_type=F32)
        out = []
        for i in range(2):
            field = got[3 * i * CZ:(3 * i + 1) * CZ]
            field = field + got[(3 * i + 1) * CZ:(3 * i + 2) * CZ] + got[(3 * i + 2) * CZ:(3 * i + 3) * CZ]
            out.append(jnp.sum(jnp.where(y_at == at_z, field, 0.0), axis=0, keepdims=True))
        return out

    def hot_y_of(cells):
        return jnp.where(y_at == ((cells >> 7) & (CY - 1)), 1.0, 0.0).astype(BF16)

    own_hot_y[...] = hot_y_of(own_cells)

    pl.semaphore_wait(barrier, partners)

    def slot_copy(k):
        return pltpu.make_async_remote_copy(
            src_ref=slots.at[0], dst_ref=slots.at[k],
            send_sem=slot_send, recv_sem=slot_recv.at[k],
            device_id=plane_peer(k), device_id_type=MESH,
        )

    def halo(src, dst, sem_at, send_sem, recv_sem, device):
        return pltpu.make_async_remote_copy(
            src_ref=src, dst_ref=dst, send_sem=send_sem.at[sem_at], recv_sem=recv_sem.at[sem_at],
            device_id=device, device_id_type=MESH,
        )


    inner = pl.ds(0, CX)
    q_x = {
        "xu": halo(qq.at[CX - 1, rows_of], q_near.at[0], 0, halo_send, halo_recv, (s_up, r, c)),
        "xd": halo(qq.at[0, rows_of], q_near.at[1], 1, halo_send, halo_recv, (s_down, r, c)),
    }

    def field_y(ref, base):
        return {
            "yu": halo(ref.at[inner, pl.ds(CY, 8)], ref.at[inner, pl.ds(0, 8)], base, halo_send, halo_recv, (s, r_up, c)),
            "yd": halo(ref.at[inner, pl.ds(8, 8)], ref.at[inner, pl.ds(CY + 8, 8)], base + 1, halo_send, halo_recv, (s, r_down, c)),
        }

    q_y = field_y(qq, 4)
    p_y = field_y(pp, 6)
    wrap = {
        "xu": halo(turned_face.at[1], turned_wrap, 0, wrap_send, wrap_recv, (s_up, r, c)),
        "xd": halo(turned_face.at[0], turned_wrap, 1, wrap_send, wrap_recv, (s_down, r, c)),
    }
    ask = {
        "xu": halo(cells_buf.at[0], cells_buf.at[1], 0, cell_send, cell_recv, (s_up, r, c)),
        "xd": halo(cells_buf.at[0], cells_buf.at[2], 1, cell_send, cell_recv, (s_down, r, c)),
    }
    reply = {
        "xu": halo(answer.at[1], answered.at[0], 0, answer_send, answer_recv, (s_up, r, c)),
        "xd": halo(answer.at[0], answered.at[1], 1, answer_send, answer_recv, (s_down, r, c)),
    }
    pq_z = {
        "zu": halo(zsend.at[pl.ds(8, 8)], zrecv.at[pl.ds(0, 8)], 8, halo_send, halo_recv, (s, r, c_up)),
        "zd": halo(zsend.at[pl.ds(0, 8)], zrecv.at[pl.ds(8, 8)], 9, halo_send, halo_recv, (s, r, c_down)),
    }
    lam_x = {
        "xu": halo(lam0.at[CX], lam0.at[0], 0, lam_send, lam_recv, (s_up, r, c)),
        "xd": halo(lam0.at[1], lam0.at[CX + 1], 1, lam_send, lam_recv, (s_down, r, c)),
    }
    lam_y = {
        "yu": halo(lam1.at[inner, pl.ds(CY, 8)], lam1.at[inner, pl.ds(0, 8)], 2, lam_send, lam_recv, (s, r_up, c)),
        "yd": halo(lam1.at[inner, pl.ds(8, 8)], lam1.at[inner, pl.ds(CY + 8, 8)], 3, lam_send, lam_recv, (s, r_down, c)),
    }
    lam_z = {
        "zu": halo(lsend.at[pl.ds(8, 8)], lrecv.at[pl.ds(0, 8)], 4, lam_send, lam_recv, (s, r, c_up)),
        "zd": halo(lsend.at[pl.ds(0, 8)], lrecv.at[pl.ds(8, 8)], 5, lam_send, lam_recv, (s, r, c_down)),
    }

    def start(faces):
        for side, copy in faces.items():
            pl.when(has[side])(copy.start)

    opposite = {"xu": "xd", "xd": "xu", "yu": "yd", "yd": "yu", "zu": "zd", "zd": "zu"}

    def arrive(faces):
        for side, copy in faces.items():
            pl.when(has[opposite[side]])(copy.wait_recv)

    def sent(faces):
        for side, copy in faces.items():
            pl.when(has[side])(copy.wait_send)

    start(pq_z)
    start(q_y)
    start(p_y)
    pl.when(near_up)(ask["xu"].start)
    pl.when(near_down)(ask["xd"].start)
    pl.when(wrap_up)(wrap["xu"].start)
    pl.when(wrap_down)(wrap["xd"].start)
    for k in range(NA - 1, 0, -1):
        slot_copy(k).start()

    phase = jnp.cos(0.5 * jnp.full((1, CZ), lax.rem(step_ref[0], 97).astype(F32), F32))
    for copy in loads[3:]:
        copy.wait()
    arrive(q_y)
    arrive(p_y)

    def along_x(ref, x):
        if x == 0:
            return ref[1, rows_of] * 0.5
        if x == CX - 1:
            return ref[CX - 2, rows_of] * -0.5
        return (ref[x + 1, rows_of] - ref[x - 1, rows_of]) * 0.5

    def along_y(ref, x):
        return (ref[x, pl.ds(9, CY)] - ref[x, pl.ds(7, CY)]) * 0.5

    at_z = lax.broadcasted_iota(jnp.int32, (CY, CZ), 1)

    def along_z(field):
        upper = jnp.where(at_z == CZ - 1, 0.0, pltpu.roll(field, CZ - 1, 1))
        lower = jnp.where(at_z == 0, 0.0, pltpu.roll(field, 1, 1))
        return (upper - lower) * 0.5

    for x in range(CX):
        here = slice(x * CY, (x + 1) * CY)
        total_0 = total[0, x] + along_x(qq, x)
        total_1 = total[1, x] + along_y(qq, x)
        total_2 = total[2, x] + along_z(qq[x, rows_of])
        total[0, x] = total_0
        total[1, x] = total_1
        total[2, x] = total_2
        moved_0 = vel[0, x] - 0.3 * along_x(pp, x) + drv[x] * phase
        moved_2 = vel[2, x] - 0.3 * along_z(pp[x, rows_of])
        sens = -(
            total_0 * moved_0 + total_1 * (vel[1, x] - 0.3 * along_y(pp, x)) + total_2 * moved_2
        )
        for i, piece in enumerate(pieces(sens.T)):
            sens_t[i * CZ:(i + 1) * CZ, here] = piece
        if x in (0, CX - 1):
            split_into(slot_parts.at[x // (CX - 1)], total_0.T, moved_0.T)
        for i, field in enumerate((total_2.T, moved_2.T)):
            ends[i:i + 1, here] = field[0:1]
            ends[2 + i:3 + i, here] = field[CZ - 1:CZ]

    def serve(side, at):
        cells = cells_buf[at]
        p_at, q_at = pick(face_parts.at[side], hot_y_of(cells), cells & (CZ - 1))
        answer[side, 0:1] = p_at
        answer[side, 1:2] = q_at

    @pl.when(near_up)
    def _():
        ask["xd"].wait_recv()
        serve(1, 2)
        reply["xu"].start()

    @pl.when(near_down)
    def _():
        ask["xu"].wait_recv()
        serve(0, 1)
        reply["xd"].start()

    pl.when(near_up)(q_x["xu"].start)
    pl.when(near_down)(q_x["xd"].start)

    on_face = [
        pick(slot_parts.at[side], where_hot[side * (CX - 1) * CY:(side * (CX - 1) + 1) * CY], own_z)
        for side in range(2)
    ]

    edge_parts = jnp.concatenate(pieces(ends[...]), axis=0)
    edge = jnp.dot(edge_parts, where_hot[...], preferred_element_type=F32)
    edge = edge[0:4] + edge[4:8] + edge[8:12]

    picked = jnp.dot(sens_t[...], where_hot[...], preferred_element_type=F32)
    picked = picked[0:CZ] + picked[CZ:2 * CZ] + picked[2 * CZ:3 * CZ]
    picked = jnp.sum(jnp.where(y_at == own_z, picked, 0.0), axis=0, keepdims=True)

    def corrected(value, side, here, total_at, moved_at, p_at, q_at):
        sign = 2.0 * side - 1.0
        more_total = jnp.where(here, q_at, 0.0) * (0.5 * sign)
        more_moved = jnp.where(here, p_at, 0.0) * (-0.15 * sign)
        return value - (more_total * (moved_at + more_moved) + total_at * more_moved)

    arrive(pq_z)
    z_parts = jnp.concatenate(pieces(zrecv[...]), axis=0)
    faces_z = jnp.dot(z_parts, own_hot_y[...], preferred_element_type=F32)
    faces_z = faces_z[0:16] + faces_z[16:32] + faces_z[32:48]
    row_x = lax.broadcasted_iota(jnp.int32, (16, WALL), 0) & (CX - 1)
    faces_z = jnp.where(row_x == own_x, faces_z, 0.0)
    for side in range(2):
        p_at = jnp.sum(faces_z[8 * side:8 * side + 4], axis=0, keepdims=True)
        q_at = jnp.sum(faces_z[8 * side + 4:8 * side + 8], axis=0, keepdims=True)
        here = own_z == side * (CZ - 1)
        picked = corrected(picked, side, here, edge[2 * side:2 * side + 1], edge[2 * side + 1:2 * side + 2], p_at, q_at)

    pl.when(near_down)(reply["xu"].wait_recv)
    pl.when(near_up)(reply["xd"].wait_recv)

    def own_answer(side):
        split_into(wrap_parts, turned_wrap[0], turned_wrap[1])
        p_at, q_at = pick(wrap_parts, own_hot_y[...], cells_buf[0] & (CZ - 1))
        answered[side, 0:1] = p_at
        answered[side, 1:2] = q_at

    @pl.when(wrap_down)
    def _():
        wrap["xu"].wait_recv()
        own_answer(0)

    @pl.when(wrap_up)
    def _():
        wrap["xd"].wait_recv()
        own_answer(1)

    for side, (total_at, moved_at) in enumerate(on_face):
        here = own_x == side * (CX - 1)
        picked = corrected(picked, side, here, total_at, moved_at, answered[side, 0:1], answered[side, 1:2])
    vals[0] = picked

    for k in range(NA - 1, 0, -1):
        pltpu.make_async_remote_copy(
            src_ref=vals.at[0], dst_ref=vals.at[k], send_sem=val_send, recv_sem=val_recv.at[k],
            device_id=plane_peer(k), device_id_type=MESH,
        ).start()

    pl.when(near_down)(q_x["xu"].wait_recv)
    pl.when(near_up)(q_x["xd"].wait_recv)

    @pl.when(wrap_down)
    def _():
        q_near[0] = turned_wrap[1].T

    @pl.when(wrap_up)
    def _():
        q_near[1] = turned_wrap[1].T

    edge_t = jnp.concatenate([zrecv[...], jnp.zeros((CZ - 16, CZ), F32)], axis=0).T

    def with_edges(field, low, high):
        field = jnp.where(at_z == CZ - 1, field + high * 0.5, field)
        return jnp.where(at_z == 0, field - low * 0.5, field)

    for x in range(CX):
        free = 1.0 - mask[x].astype(F32)
        total_0 = total[0, x]
        if x == 0:
            total_0 = total_0 - q_near[0] * 0.5
        if x == CX - 1:
            total_0 = total_0 + q_near[1] * 0.5
        lam0[x + 1] = free * total_0
        lam1[x, rows_of] = free * total[1, x]
        low, high = (edge_t[:, 8 * i + CX + x:8 * i + CX + x + 1] for i in range(2))
        lam2[x] = free * with_edges(total[2, x], low, high)

    start(lam_x)
    start(lam_y)
    for x in range(CX):
        turned = lam2[x].T
        lsend[x:x + 1] = turned[0:1]
        lsend[8 + x:9 + x] = turned[CZ - 1:CZ]
    start(lam_z)
    stores = [
        pltpu.make_async_copy(lam0.at[pl.ds(1, CX)], av_out.at[0], store_sem.at[0]),
        pltpu.make_async_copy(lam1.at[pl.ds(0, CX), rows_of], av_out.at[1], store_sem.at[1]),
        pltpu.make_async_copy(lam2, av_out.at[2], store_sem.at[2]),
    ]
    for copy in stores:
        copy.start()

    def slots_of(k, _):
        pltpu.make_async_copy(slots.at[k], slots.at[k], slot_recv.at[k]).wait()
        prepare(k)
        return 0

    rest = slots.at[pl.ds(1, NA - 1)]
    lax.fori_loop(1, NA, slots_of, 0)

    rest_vals = vals.at[pl.ds(1, NA - 1)]
    summed = None
    for low, high in zip(BATCHES[:-1], BATCHES[1:]):
        for k in range(max(low, 1), high):
            pltpu.make_async_copy(vals.at[k], vals.at[k], val_recv.at[k]).wait()
        split = [pieces(weight[k] * vals[k]) for k in range(low, high)]
        scaled = jnp.concatenate(
            [jnp.concatenate([one[i] for one in split], axis=1) for i in range(3)], axis=0
        )
        product = lax.dot_general(
            hot[:, low * WALL:high * WALL], scaled, (((1,), (1,)), ((), ())), preferred_element_type=F32
        )
        summed = product if summed is None else summed + product
    summed = summed[:, 0:ANG] + summed[:, ANG:2 * ANG] + summed[:, 2 * ANG:3 * ANG]
    dense[...] = jnp.concatenate([summed, jnp.zeros_like(summed)], axis=1).reshape(NB, OWN, 2 * ANG)

    def send_part(k, _):
        peer = line_peer(k)
        other = (lax.rem(peer[0], ZL) * 2 + peer[1]) * ZH + lax.rem(peer[2], ZH)
        pltpu.make_async_remote_copy(
            src_ref=dense.at[other], dst_ref=parts.at[k - 1], send_sem=part_send, recv_sem=part_recv,
            device_id=peer, device_id_type=MESH,
        ).start()
        return 0

    lax.fori_loop(1, NB, send_part, 0)

    for faces in (lam_x, lam_y, lam_z):
        arrive(faces)
    edge_l = jnp.concatenate([lrecv[...], jnp.zeros((CZ - 16, CZ), F32)], axis=0).T
    for x in range(CX):
        div = (
            (lam0[x + 2] - lam0[x]) * 0.5
            + (lam1[x, pl.ds(9, CY)] - lam1[x, pl.ds(7, CY)]) * 0.5
            + with_edges(along_z(lam2[x]), edge_l[:, x:x + 1], edge_l[:, 8 + x:9 + x])
        )
        apo[x] = ap[x] + 0.3 * div
    last = pltpu.make_async_copy(apo, ap_out, store_sem.at[3])
    last.start()

    pltpu.make_async_copy(parts, parts, part_recv).wait()
    grad_out[...] = (dense[b] + jnp.sum(parts[...], axis=0))[:, 0:ANG]

    for faces in (q_y, p_y, pq_z, lam_x, lam_y, lam_z):
        sent(faces)
    pl.when(wrap_up)(wrap["xu"].wait_send)
    pl.when(wrap_down)(wrap["xd"].wait_send)
    for faces in (ask, reply, q_x):
        pl.when(near_up)(faces["xu"].wait_send)
        pl.when(near_down)(faces["xd"].wait_send)
    pltpu.make_async_copy(rest, rest, slot_send).wait()
    pltpu.make_async_copy(rest_vals, rest_vals, val_send).wait()
    pltpu.make_async_copy(parts, parts, part_send).wait()
    for copy in stores + [last]:
        copy.wait()


def written(outs):
    anyspace = pl.BlockSpec(memory_space=pl.ANY)
    return pl.pallas_call(
        hand3,
        out_shape=tuple(jax.ShapeDtypeStruct(o.shape, o.dtype) for o in outs),
        in_specs=[anyspace] * 3,
        out_specs=(anyspace,) * 3,
        scratch_shapes=[pltpu.SemaphoreType.DMA((3,))],
        compiler_params=pltpu.CompilerParams(vmem_limit_bytes=1024 * 1024),
    )(*outs)


def hand3(a, b, c, d, e, f, sem):
    copies = [pltpu.make_async_copy(x, y, sem.at[i]) for i, (x, y) in enumerate(((a, d), (b, e), (c, f)))]
    for copy in copies:
        copy.start()
    for copy in copies:
        copy.wait()


def local(ns, nr, nc, *args):
    hbm = pl.BlockSpec(memory_space=pltpu.HBM)
    vmem = pl.BlockSpec(memory_space=pltpu.VMEM)
    block = (CX, CY, CZ)
    dma = pltpu.SemaphoreType.DMA
    return written(pl.pallas_call(
        functools.partial(kernel, ns, nr, nc),
        out_shape=(
            pltpu.VMEM(block, F32),
            pltpu.VMEM((3,) + block, F32),
            pltpu.VMEM((OWN, ANG), F32),
        ),
        in_specs=[hbm] * 12,
        out_specs=(pl.BlockSpec(memory_space=pl.ANY), pl.BlockSpec(memory_space=pl.ANY), vmem),
        scratch_shapes=[
            pltpu.VMEM((1, 1, 1, WALL), jnp.int32),
            pltpu.VMEM((1, 1, 1, WALL), jnp.int32),
            pltpu.VMEM((1, 1, 1, WALL), F32),
            pltpu.SMEM((1, 1, 1), jnp.int32),
            pltpu.SMEM((1,), jnp.int32),
            pltpu.VMEM((CX, CY + 16, CZ), F32),
            pltpu.VMEM((CX, CY + 16, CZ), F32),
            pltpu.VMEM(block, F32),
            pltpu.VMEM(block, F32),
            pltpu.VMEM(block, F32),
            pltpu.VMEM((3,) + block, F32),
            pltpu.VMEM((3,) + block, F32),
            pltpu.VMEM(block, jnp.int32),
            pltpu.VMEM((CX + 2, CY, CZ), F32),
            pltpu.VMEM((CX, CY + 16, CZ), F32),
            pltpu.VMEM(block, F32),
            pltpu.VMEM(block, F32),
            pltpu.VMEM((2, CY, CZ), F32),
            pltpu.VMEM((16, CY), F32),
            pltpu.VMEM((16, CY), F32),
            pltpu.VMEM((16, CY), F32),
            pltpu.VMEM((16, CY), F32),
            pltpu.VMEM((2, 2, CZ, CY), F32),
            pltpu.VMEM((2, CZ, CY), F32),
            pltpu.VMEM((2, 6 * CZ, CY), BF16),
            pltpu.VMEM((6 * CZ, CY), BF16),
            pltpu.VMEM((2, 6 * CZ, CY), BF16),
            pltpu.VMEM((3, 1, WALL), jnp.int32),
            pltpu.VMEM((2, 2, WALL), F32),
            pltpu.VMEM((2, 2, WALL), F32),
            pltpu.VMEM((4, CX * CY), F32),
            pltpu.VMEM((CY, WALL), BF16),
            pltpu.VMEM((NA, 2, WALL), F32),
            pltpu.VMEM((NA, 1, WALL), F32),
            pltpu.VMEM((WIDTH, NA * WALL), BF16),
            pltpu.VMEM((NA, ANG, WALL), F32),
            pltpu.VMEM((CX * CY, WALL), BF16),
            pltpu.VMEM((3 * CZ, CX * CY), BF16),
            pltpu.VMEM((NB, OWN, 2 * ANG), F32),
            pltpu.VMEM((NB - 1, OWN, 2 * ANG), F32),
            dma((5,)), dma((7,)), dma((4,)), dma((10,)), dma((10,)), dma((6,)), dma((6,)),
            dma((2,)), dma((2,)), dma((2,)), dma((2,)), dma((2,)), dma((2,)),
            dma, dma((NA,)), dma, dma((NA,)), dma, dma,
        ],
        compiler_params=pltpu.CompilerParams(
            collective_id=0, has_side_effects=True, vmem_limit_bytes=62 * 1024 * 1024 + 512 * 1024
        ),
        cost_estimate=pl.CostEstimate(flops=10**9, bytes_accessed=4 * 10**6, transcendentals=0),
    )(*args))


def solution(mesh):
    names = ("slab", "row", "col")
    sizes = tuple(mesh.shape[name] for name in names)
    cells = P(*names)
    vector = P(None, *names)
    slot = P(*names, None)
    in_specs = (cells, vector, cells, cells, cells, vector, cells, slot, slot, slot, cells, P())
    out_specs = (cells, vector, P(names, None))
    return jax.shard_map(
        functools.partial(local, *sizes), mesh=mesh, in_specs=in_specs, out_specs=out_specs, check_vma=False
    )
```

```python
import functools

import jax
import jax.numpy as jnp
from jax import lax
from jax.experimental import pallas as pl
from jax.experimental.pallas import tpu as pltpu
from jax.sharding import PartitionSpec as P

ANG = 64
CX = 4
CY = 128
CZ = 128
WALL = 512
OWN = 8
NXC = 4
NYC = 4
ZL = 4
ZH = 2
NA = NXC * NYC
NB = 2 * ZL * ZH
WIDTH = NB * OWN
BATCHES = (0, 5, 11, 16)
MESH = pl.DeviceIdType.MESH
PLANE = sorted(
    ((dy, dx) for dy in range(NYC) for dx in range(NXC)),
    key=lambda d: (min(d[0], NYC - d[0]) + min(d[1], NXC - d[1]), d),
)
F32 = jnp.float32
BF16 = jnp.bfloat16


def pieces(value):
    high = value.astype(BF16)
    rest = value - high.astype(F32)
    mid = rest.astype(BF16)
    low = (rest - mid.astype(F32)).astype(BF16)
    return high, mid, low


def kernel(
    ns, nr, nc,
    p_in, v_in, kap_in, drv_in, ap_in, av_in, mask_in, cells_in, rows_in, angle_in, count_in, step_in,
    ap_out, av_out, grad_out,
    cells_ref, rows_ref, angle_ref, count_ref, step_ref,
    pp, qq, kap, drv, ap, vel, total, mask,
    lam0, lam1, lam2, apo, q_near,
    zsend, zrecv, lsend, lrecv,
    turned_face, turned_wrap, face_parts, wrap_parts, slot_parts,
    cells_buf, answer, answered,
    ends, own_hot_y,
    slots, vals, hot, weight, where_hot, sens_t, dense, parts,
    small_sem, load_sem, store_sem, halo_send, halo_recv, lam_send, lam_recv,
    wrap_send, wrap_recv, cell_send, cell_recv, answer_send, answer_recv,
    slot_send, slot_recv, val_send, val_recv, part_send, part_recv,
):
    s = lax.axis_index("slab")
    r = lax.axis_index("row")
    c = lax.axis_index("col")
    y, zl = lax.div(s, ZL), lax.rem(s, ZL)
    x_at, zh = lax.div(c, ZH), lax.rem(c, ZH)
    group = y * NXC + x_at
    b = (zl * 2 + r) * ZH + zh

    def plane_peer(k):
        dy, dx = PLANE[k]
        return (lax.rem(y + dy, NYC) * ZL + zl, r, lax.rem(x_at + dx, NXC) * ZH + zh)

    def line_peer(k):
        other_zl = lax.rem(zl + lax.div(k, 2 * ZH), ZL)
        other_r = lax.rem(r + lax.rem(lax.div(k, ZH), 2), 2)
        other_zh = lax.rem(zh + lax.rem(k, ZH), ZH)
        return (y * ZL + other_zl, other_r, x_at * ZH + other_zh)

    plane = jnp.zeros((CY, CZ), F32)
    strip = jnp.zeros((8, CZ), F32)
    for ref in (pp, qq, lam1):
        for x in range(CX):
            ref[x, pl.ds(0, 8)] = strip
            ref[x, pl.ds(CY + 8, 8)] = strip
    for ref in (q_near, ):
        ref[0] = plane
        ref[1] = plane
    lam0[0] = plane
    lam0[CX + 1] = plane
    zrecv[...] = jnp.zeros_like(zrecv)
    lrecv[...] = jnp.zeros_like(lrecv)
    answered[...] = jnp.zeros_like(answered)

    barrier = pltpu.get_barrier_semaphore()

    def greet(device):
        pl.semaphore_signal(barrier, inc=1, device_id=device, device_id_type=MESH)

    def greet_line(k, _):
        greet(line_peer(k))
        return 0

    s_up, s_down = jnp.minimum(s + 1, ns - 1), jnp.maximum(s - 1, 0)
    r_up, r_down = jnp.minimum(r + 1, nr - 1), jnp.maximum(r - 1, 0)
    c_up, c_down = jnp.minimum(c + 1, nc - 1), jnp.maximum(c - 1, 0)
    has = {
        "xu": s < ns - 1, "xd": s > 0, "yu": r < nr - 1, "yd": r > 0, "zu": c < nc - 1, "zd": c > 0,
    }
    wrap_up = jnp.logical_and(zl == ZL - 1, has["xu"])
    wrap_down = jnp.logical_and(zl == 0, has["xd"])
    near_up = zl < ZL - 1
    near_down = zl > 0
    beyond = (
        (jnp.logical_and(zh == ZH - 1, has["zu"]), (s, r, c_up)),
        (jnp.logical_and(zh == 0, has["zd"]), (s, r, c_down)),
        (wrap_up, (s_up, r, c)),
        (wrap_down, (s_down, r, c)),
    )
    partners = NA - 1 + NB - 1
    for here, device in beyond:
        pl.when(here)(functools.partial(greet, device))
        partners = partners + here.astype(jnp.int32)
    for k in range(1, NA):
        greet(plane_peer(k))
    lax.fori_loop(1, NB, greet_line, 0)

    loads = [
        pltpu.make_async_copy(kap_in, kap, load_sem.at[0]),
        pltpu.make_async_copy(ap_in, ap, load_sem.at[1]),
        pltpu.make_async_copy(p_in, pp.at[pl.ds(0, CX), pl.ds(8, CY)], load_sem.at[2]),
        pltpu.make_async_copy(av_in, total, load_sem.at[3]),
        pltpu.make_async_copy(mask_in, mask, load_sem.at[4]),
        pltpu.make_async_copy(v_in, vel, load_sem.at[5]),
        pltpu.make_async_copy(drv_in, drv, load_sem.at[6]),
    ]
    small = [
        pltpu.make_async_copy(rows_in, rows_ref, small_sem.at[0]),
        pltpu.make_async_copy(angle_in, angle_ref, small_sem.at[1]),
        pltpu.make_async_copy(count_in, count_ref, small_sem.at[2]),
        pltpu.make_async_copy(cells_in, cells_ref, small_sem.at[3]),
        pltpu.make_async_copy(step_in, step_ref, small_sem.at[4]),
    ]
    for copy in small + loads:
        copy.start()

    lane = lax.broadcasted_iota(jnp.int32, (1, WALL), 1)
    for copy in small:
        copy.wait()
    own_rows = rows_ref[0, 0]
    live = lane < count_ref[0, 0, 0]
    bits = own_rows >> 3
    owner_group = ((bits >> 6) << 2) + ((bits >> 1) & 3)
    owner_line = (((bits >> 4) & 3) << 2) + (((bits >> 3) & 1) << 1) + (bits & 1)
    code = owner_group * WIDTH + owner_line * OWN + (own_rows & (OWN - 1))
    slots[0, 0:1] = jnp.where(live, code.astype(F32), -1.0)
    slots[0, 1:2] = angle_ref[0, 0]
    row_at = (lax.broadcasted_iota(jnp.int32, (WIDTH, WALL), 0) + group * WIDTH).astype(F32)
    knots = lax.broadcasted_iota(jnp.int32, (ANG, WALL), 0).astype(F32)

    def at_slots(k):
        return pl.ds(pl.multiple_of(k * WALL, WALL), WALL)

    def prepare(k):
        hot[:, at_slots(k)] = jnp.where(slots[k, 0:1] == row_at, 1.0, 0.0).astype(BF16)
        dist = jnp.abs(slots[k, 1:2] - knots)
        dist = jnp.minimum(dist, ANG - dist)
        outer = jnp.maximum(2.0 - dist, 0.0)
        near = jnp.maximum(1.0 - dist, 0.0)
        weight[k] = (outer * outer * outer - 4.0 * near * near * near) * (1.0 / 6.0)


    own_cells = cells_ref[0, 0]
    cells_buf[0] = own_cells
    own_xy = own_cells >> 7
    own_x = own_cells >> 14
    own_z = own_cells & (CZ - 1)

    loads[0].wait()
    loads[1].wait()
    rows_of = pl.ds(8, CY)
    for x in range(CX):
        qq[x, rows_of] = kap[x] * ap[x]
    loads[2].wait()
    for i, (ref, at) in enumerate(((pp, 0), (qq, CX))):
        for x in range(CX):
            turned = ref[x, rows_of].T
            zsend[at + x:at + x + 1] = turned[0:1]
            zsend[8 + at + x:8 + at + x + 1] = turned[CZ - 1:CZ]
            if x in (0, CX - 1):
                turned_face[x // (CX - 1), i] = turned

    def split_into(ref, first, second):
        for i, field in enumerate((first, second)):
            for j, piece in enumerate(pieces(field)):
                ref[(3 * i + j) * CZ:(3 * i + j + 1) * CZ] = piece

    def pick(ref, hot_y, at_z):
        got = jnp.dot(ref[...], hot_y, preferred_element_type=F32)
        out = []
        for i in range(2):
            field = got[3 * i * CZ:(3 * i + 1) * CZ]
            field = field + got[(3 * i + 1) * CZ:(3 * i + 2) * CZ] + got[(3 * i + 2) * CZ:(3 * i + 3) * CZ]
            out.append(jnp.sum(jnp.where(y_at == at_z, field, 0.0), axis=0, keepdims=True))
        return out

    def hot_y_of(cells):
        return jnp.where(y_at == ((cells >> 7) & (CY - 1)), 1.0, 0.0).astype(BF16)


    pl.semaphore_wait(barrier, partners)

    def slot_copy(k):
        return pltpu.make_async_remote_copy(
            src_ref=slots.at[0], dst_ref=slots.at[k],
            send_sem=slot_send, recv_sem=slot_recv.at[k],
            device_id=plane_peer(k), device_id_type=MESH,
        )

    def halo(src, dst, sem_at, send_sem, recv_sem, device):
        return pltpu.make_async_remote_copy(
            src_ref=src, dst_ref=dst, send_sem=send_sem.at[sem_at], recv_sem=recv_sem.at[sem_at],
            device_id=device, device_id_type=MESH,
        )


    inner = pl.ds(0, CX)
    q_x = {
        "xu": halo(qq.at[CX - 1, rows_of], q_near.at[0], 0, halo_send, halo_recv, (s_up, r, c)),
        "xd": halo(qq.at[0, rows_of], q_near.at[1], 1, halo_send, halo_recv, (s_down, r, c)),
    }

    def field_y(ref, base):
        return {
            "yu": halo(ref.at[inner, pl.ds(CY, 8)], ref.at[inner, pl.ds(0, 8)], base, halo_send, halo_recv, (s, r_up, c)),
            "yd": halo(ref.at[inner, pl.ds(8, 8)], ref.at[inner, pl.ds(CY + 8, 8)], base + 1, halo_send, halo_recv, (s, r_down, c)),
        }

    q_y = field_y(qq, 4)
    p_y = field_y(pp, 6)
    wrap = {
        "xu": halo(turned_face.at[1], turned_wrap, 0, wrap_send, wrap_recv, (s_up, r, c)),
        "xd": halo(turned_face.at[0], turned_wrap, 1, wrap_send, wrap_recv, (s_down, r, c)),
    }
    ask = {
        "xu": halo(cells_buf.at[0], cells_buf.at[1], 0, cell_send, cell_recv, (s_up, r, c)),
        "xd": halo(cells_buf.at[0], cells_buf.at[2], 1, cell_send, cell_recv, (s_down, r, c)),
    }
    reply = {
        "xu": halo(answer.at[1], answered.at[0], 0, answer_send, answer_recv, (s_up, r, c)),
        "xd": halo(answer.at[0], answered.at[1], 1, answer_send, answer_recv, (s_down, r, c)),
    }
    pq_z = {
        "zu": halo(zsend.at[pl.ds(8, 8)], zrecv.at[pl.ds(0, 8)], 8, halo_send, halo_recv, (s, r, c_up)),
        "zd": halo(zsend.at[pl.ds(0, 8)], zrecv.at[pl.ds(8, 8)], 9, halo_send, halo_recv, (s, r, c_down)),
    }
    lam_x = {
        "xu": halo(lam0.at[CX], lam0.at[0], 0, lam_send, lam_recv, (s_up, r, c)),
        "xd": halo(lam0.at[1], lam0.at[CX + 1], 1, lam_send, lam_recv, (s_down, r, c)),
    }
    lam_y = {
        "yu": halo(lam1.at[inner, pl.ds(CY, 8)], lam1.at[inner, pl.ds(0, 8)], 2, lam_send, lam_recv, (s, r_up, c)),
        "yd": halo(lam1.at[inner, pl.ds(8, 8)], lam1.at[inner, pl.ds(CY + 8, 8)], 3, lam_send, lam_recv, (s, r_down, c)),
    }
    lam_z = {
        "zu": halo(lsend.at[pl.ds(8, 8)], lrecv.at[pl.ds(0, 8)], 4, lam_send, lam_recv, (s, r, c_up)),
        "zd": halo(lsend.at[pl.ds(0, 8)], lrecv.at[pl.ds(8, 8)], 5, lam_send, lam_recv, (s, r, c_down)),
    }

    def start(faces):
        for side, copy in faces.items():
            pl.when(has[side])(copy.start)

    opposite = {"xu": "xd", "xd": "xu", "yu": "yd", "yd": "yu", "zu": "zd", "zd": "zu"}

    def arrive(faces):
        for side, copy in faces.items():
            pl.when(has[opposite[side]])(copy.wait_recv)

    def sent(faces):
        for side, copy in faces.items():
            pl.when(has[side])(copy.wait_send)

    start(pq_z)
    start(q_y)
    start(p_y)
    pl.when(near_up)(ask["xu"].start)
    pl.when(near_down)(ask["xd"].start)
    pl.when(wrap_up)(wrap["xu"].start)
    pl.when(wrap_down)(wrap["xd"].start)
    for k in range(NA - 1, 0, -1):
        slot_copy(k).start()

    y_at = lax.broadcasted_iota(jnp.int32, (CY, WALL), 0)
    for x in range(CX):
        where_hot[x * CY:(x + 1) * CY] = jnp.where(y_at + x * CY == own_xy, 1.0, 0.0).astype(BF16)
    own_hot_y[...] = hot_y_of(own_cells)
    for side in range(2):
        split_into(face_parts.at[side], turned_face[side, 0], turned_face[side, 1])
    prepare(0)

    phase = jnp.cos(0.5 * jnp.full((1, CZ), lax.rem(step_ref[0], 97).astype(F32), F32))
    for copy in loads[3:]:
        copy.wait()
    arrive(q_y)
    arrive(p_y)

    def along_x(ref, x):
        if x == 0:
            return ref[1, rows_of] * 0.5
        if x == CX - 1:
            return ref[CX - 2, rows_of] * -0.5
        return (ref[x + 1, rows_of] - ref[x - 1, rows_of]) * 0.5

    def along_y(ref, x):
        return (ref[x, pl.ds(9, CY)] - ref[x, pl.ds(7, CY)]) * 0.5

    at_z = lax.broadcasted_iota(jnp.int32, (CY, CZ), 1)

    def along_z(field):
        upper = jnp.where(at_z == CZ - 1, 0.0, pltpu.roll(field, CZ - 1, 1))
        lower = jnp.where(at_z == 0, 0.0, pltpu.roll(field, 1, 1))
        return (upper - lower) * 0.5

    for x in range(CX):
        here = slice(x * CY, (x + 1) * CY)
        total_0 = total[0, x] + along_x(qq, x)
        total_1 = total[1, x] + along_y(qq, x)
        total_2 = total[2, x] + along_z(qq[x, rows_of])
        total[0, x] = total_0
        total[1, x] = total_1
        total[2, x] = total_2
        moved_0 = vel[0, x] - 0.3 * along_x(pp, x) + drv[x] * phase
        moved_2 = vel[2, x] - 0.3 * along_z(pp[x, rows_of])
        sens = -(
            total_0 * moved_0 + total_1 * (vel[1, x] - 0.3 * along_y(pp, x)) + total_2 * moved_2
        )
        for i, piece in enumerate(pieces(sens.T)):
            sens_t[i * CZ:(i + 1) * CZ, here] = piece
        if x in (0, CX - 1):
            split_into(slot_parts.at[x // (CX - 1)], total_0.T, moved_0.T)
        for i, field in enumerate((total_2.T, moved_2.T)):
            ends[i:i + 1, here] = field[0:1]
            ends[2 + i:3 + i, here] = field[CZ - 1:CZ]

    def serve(side, at):
        cells = cells_buf[at]
        p_at, q_at = pick(face_parts.at[side], hot_y_of(cells), cells & (CZ - 1))
        answer[side, 0:1] = p_at
        answer[side, 1:2] = q_at

    @pl.when(near_up)
    def _():
        ask["xd"].wait_recv()
        serve(1, 2)
        reply["xu"].start()

    @pl.when(near_down)
    def _():
        ask["xu"].wait_recv()
        serve(0, 1)
        reply["xd"].start()

    pl.when(near_up)(q_x["xu"].start)
    pl.when(near_down)(q_x["xd"].start)

    on_face = [
        pick(slot_parts.at[side], where_hot[side * (CX - 1) * CY:(side * (CX - 1) + 1) * CY], own_z)
        for side in range(2)
    ]

    edge_parts = jnp.concatenate(pieces(ends[...]), axis=0)
    edge = jnp.dot(edge_parts, where_hot[...], preferred_element_type=F32)
    edge = edge[0:4] + edge[4:8] + edge[8:12]

    picked = jnp.dot(sens_t[...], where_hot[...], preferred_element_type=F32)
    picked = picked[0:CZ] + picked[CZ:2 * CZ] + picked[2 * CZ:3 * CZ]
    picked = jnp.sum(jnp.where(y_at == own_z, picked, 0.0), axis=0, keepdims=True)

    def corrected(value, side, here, total_at, moved_at, p_at, q_at):
        sign = 2.0 * side - 1.0
        more_total = jnp.where(here, q_at, 0.0) * (0.5 * sign)
        more_moved = jnp.where(here, p_at, 0.0) * (-0.15 * sign)
        return value - (more_total * (moved_at + more_moved) + total_at * more_moved)

    arrive(pq_z)
    z_parts = jnp.concatenate(pieces(zrecv[...]), axis=0)
    faces_z = jnp.dot(z_parts, own_hot_y[...], preferred_element_type=F32)
    faces_z = faces_z[0:16] + faces_z[16:32] + faces_z[32:48]
    row_x = lax.broadcasted_iota(jnp.int32, (16, WALL), 0) & (CX - 1)
    faces_z = jnp.where(row_x == own_x, faces_z, 0.0)
    for side in range(2):
        p_at = jnp.sum(faces_z[8 * side:8 * side + 4], axis=0, keepdims=True)
        q_at = jnp.sum(faces_z[8 * side + 4:8 * side + 8], axis=0, keepdims=True)
        here = own_z == side * (CZ - 1)
        picked = corrected(picked, side, here, edge[2 * side:2 * side + 1], edge[2 * side + 1:2 * side + 2], p_at, q_at)

    pl.when(near_down)(reply["xu"].wait_recv)
    pl.when(near_up)(reply["xd"].wait_recv)

    def own_answer(side):
        split_into(wrap_parts, turned_wrap[0], turned_wrap[1])
        p_at, q_at = pick(wrap_parts, own_hot_y[...], cells_buf[0] & (CZ - 1))
        answered[side, 0:1] = p_at
        answered[side, 1:2] = q_at

    @pl.when(wrap_down)
    def _():
        wrap["xu"].wait_recv()
        own_answer(0)

    @pl.when(wrap_up)
    def _():
        wrap["xd"].wait_recv()
        own_answer(1)

    for side, (total_at, moved_at) in enumerate(on_face):
        here = own_x == side * (CX - 1)
        picked = corrected(picked, side, here, total_at, moved_at, answered[side, 0:1], answered[side, 1:2])
    vals[0] = picked

    for k in range(NA - 1, 0, -1):
        pltpu.make_async_remote_copy(
            src_ref=vals.at[0], dst_ref=vals.at[k], send_sem=val_send, recv_sem=val_recv.at[k],
            device_id=plane_peer(k), device_id_type=MESH,
        ).start()

    pl.when(near_down)(q_x["xu"].wait_recv)
    pl.when(near_up)(q_x["xd"].wait_recv)

    @pl.when(wrap_down)
    def _():
        q_near[0] = turned_wrap[1].T

    @pl.when(wrap_up)
    def _():
        q_near[1] = turned_wrap[1].T

    edge_t = jnp.concatenate([zrecv[...], jnp.zeros((CZ - 16, CZ), F32)], axis=0).T

    def with_edges(field, low, high):
        field = jnp.where(at_z == CZ - 1, field + high * 0.5, field)
        return jnp.where(at_z == 0, field - low * 0.5, field)

    for x in range(CX):
        free = 1.0 - mask[x].astype(F32)
        total_0 = total[0, x]
        if x == 0:
            total_0 = total_0 - q_near[0] * 0.5
        if x == CX - 1:
            total_0 = total_0 + q_near[1] * 0.5
        lam0[x + 1] = free * total_0
        lam1[x, rows_of] = free * total[1, x]
        low, high = (edge_t[:, 8 * i + CX + x:8 * i + CX + x + 1] for i in range(2))
        lam2[x] = free * with_edges(total[2, x], low, high)

    start(lam_x)
    start(lam_y)
    for x in range(CX):
        turned = lam2[x].T
        lsend[x:x + 1] = turned[0:1]
        lsend[8 + x:9 + x] = turned[CZ - 1:CZ]
    start(lam_z)
    stores = [
        pltpu.make_async_copy(lam0.at[pl.ds(1, CX)], av_out.at[0], store_sem.at[0]),
        pltpu.make_async_copy(lam1.at[pl.ds(0, CX), rows_of], av_out.at[1], store_sem.at[1]),
        pltpu.make_async_copy(lam2, av_out.at[2], store_sem.at[2]),
    ]
    for copy in stores:
        copy.start()

    def slots_of(k, _):
        pltpu.make_async_copy(slots.at[k], slots.at[k], slot_recv.at[k]).wait()
        prepare(k)
        return 0

    rest = slots.at[pl.ds(1, NA - 1)]
    lax.fori_loop(1, NA, slots_of, 0)

    rest_vals = vals.at[pl.ds(1, NA - 1)]
    summed = None
    for low, high in zip(BATCHES[:-1], BATCHES[1:]):
        for k in range(max(low, 1), high):
            pltpu.make_async_copy(vals.at[k], vals.at[k], val_recv.at[k]).wait()
        split = [pieces(weight[k] * vals[k]) for k in range(low, high)]
        scaled = jnp.concatenate(
            [jnp.concatenate([one[i] for one in split], axis=1) for i in range(3)], axis=0
        )
        product = lax.dot_general(
            hot[:, low * WALL:high * WALL], scaled, (((1,), (1,)), ((), ())), preferred_element_type=F32
        )
        summed = product if summed is None else summed + product
    summed = summed[:, 0:ANG] + summed[:, ANG:2 * ANG] + summed[:, 2 * ANG:3 * ANG]
    dense[...] = jnp.concatenate([summed, jnp.zeros_like(summed)], axis=1).reshape(NB, OWN, 2 * ANG)

    def send_part(k, _):
        peer = line_peer(k)
        other = (lax.rem(peer[0], ZL) * 2 + peer[1]) * ZH + lax.rem(peer[2], ZH)
        pltpu.make_async_remote_copy(
            src_ref=dense.at[other], dst_ref=parts.at[k - 1], send_sem=part_send, recv_sem=part_recv,
            device_id=peer, device_id_type=MESH,
        ).start()
        return 0

    lax.fori_loop(1, NB, send_part, 0)

    for faces in (lam_x, lam_y, lam_z):
        arrive(faces)
    edge_l = jnp.concatenate([lrecv[...], jnp.zeros((CZ - 16, CZ), F32)], axis=0).T
    for x in range(CX):
        div = (
            (lam0[x + 2] - lam0[x]) * 0.5
            + (lam1[x, pl.ds(9, CY)] - lam1[x, pl.ds(7, CY)]) * 0.5
            + with_edges(along_z(lam2[x]), edge_l[:, x:x + 1], edge_l[:, 8 + x:9 + x])
        )
        apo[x] = ap[x] + 0.3 * div
    last = pltpu.make_async_copy(apo, ap_out, store_sem.at[3])
    last.start()

    pltpu.make_async_copy(parts, parts, part_recv).wait()
    grad_out[...] = (dense[b] + jnp.sum(parts[...], axis=0))[:, 0:ANG]

    for faces in (q_y, p_y, pq_z, lam_x, lam_y, lam_z):
        sent(faces)
    pl.when(wrap_up)(wrap["xu"].wait_send)
    pl.when(wrap_down)(wrap["xd"].wait_send)
    for faces in (ask, reply, q_x):
        pl.when(near_up)(faces["xu"].wait_send)
        pl.when(near_down)(faces["xd"].wait_send)
    pltpu.make_async_copy(rest, rest, slot_send).wait()
    pltpu.make_async_copy(rest_vals, rest_vals, val_send).wait()
    pltpu.make_async_copy(parts, parts, part_send).wait()
    for copy in stores + [last]:
        copy.wait()


def written(outs):
    anyspace = pl.BlockSpec(memory_space=pl.ANY)
    return pl.pallas_call(
        hand_over,
        out_shape=tuple(jax.ShapeDtypeStruct(o.shape, o.dtype) for o in outs),
        in_specs=[anyspace] * 3,
        out_specs=(anyspace,) * 3,
        scratch_shapes=[pltpu.SemaphoreType.DMA((9,))],
        compiler_params=pltpu.CompilerParams(vmem_limit_bytes=1024 * 1024),
    )(*outs)


def hand_over(adj_p, adj_v, grad, adj_p_out, adj_v_out, grad_out, sem):
    pairs = [(grad, grad_out)]
    for x in range(0, CX, 2):
        here = pl.ds(x, 2)
        pairs.append((adj_p.at[here], adj_p_out.at[here]))
        for k in range(3):
            pairs.append((adj_v.at[k, here], adj_v_out.at[k, here]))
    copies = [pltpu.make_async_copy(a, b, sem.at[i]) for i, (a, b) in enumerate(pairs)]
    for copy in copies:
        copy.start()
    for copy in copies:
        copy.wait()


def local(ns, nr, nc, *args):
    hbm = pl.BlockSpec(memory_space=pltpu.HBM)
    vmem = pl.BlockSpec(memory_space=pltpu.VMEM)
    block = (CX, CY, CZ)
    dma = pltpu.SemaphoreType.DMA
    return written(pl.pallas_call(
        functools.partial(kernel, ns, nr, nc),
        out_shape=(
            pltpu.VMEM(block, F32),
            pltpu.VMEM((3,) + block, F32),
            pltpu.VMEM((OWN, ANG), F32),
        ),
        in_specs=[hbm] * 12,
        out_specs=(pl.BlockSpec(memory_space=pl.ANY), pl.BlockSpec(memory_space=pl.ANY), vmem),
        scratch_shapes=[
            pltpu.VMEM((1, 1, 1, WALL), jnp.int32),
            pltpu.VMEM((1, 1, 1, WALL), jnp.int32),
            pltpu.VMEM((1, 1, 1, WALL), F32),
            pltpu.SMEM((1, 1, 1), jnp.int32),
            pltpu.SMEM((1,), jnp.int32),
            pltpu.VMEM((CX, CY + 16, CZ), F32),
            pltpu.VMEM((CX, CY + 16, CZ), F32),
            pltpu.VMEM(block, F32),
            pltpu.VMEM(block, F32),
            pltpu.VMEM(block, F32),
            pltpu.VMEM((3,) + block, F32),
            pltpu.VMEM((3,) + block, F32),
            pltpu.VMEM(block, jnp.int32),
            pltpu.VMEM((CX + 2, CY, CZ), F32),
            pltpu.VMEM((CX, CY + 16, CZ), F32),
            pltpu.VMEM(block, F32),
            pltpu.VMEM(block, F32),
            pltpu.VMEM((2, CY, CZ), F32),
            pltpu.VMEM((16, CY), F32),
            pltpu.VMEM((16, CY), F32),
            pltpu.VMEM((16, CY), F32),
            pltpu.VMEM((16, CY), F32),
            pltpu.VMEM((2, 2, CZ, CY), F32),
            pltpu.VMEM((2, CZ, CY), F32),
            pltpu.VMEM((2, 6 * CZ, CY), BF16),
            pltpu.VMEM((6 * CZ, CY), BF16),
            pltpu.VMEM((2, 6 * CZ, CY), BF16),
            pltpu.VMEM((3, 1, WALL), jnp.int32),
            pltpu.VMEM((2, 2, WALL), F32),
            pltpu.VMEM((2, 2, WALL), F32),
            pltpu.VMEM((4, CX * CY), F32),
            pltpu.VMEM((CY, WALL), BF16),
            pltpu.VMEM((NA, 2, WALL), F32),
            pltpu.VMEM((NA, 1, WALL), F32),
            pltpu.VMEM((WIDTH, NA * WALL), BF16),
            pltpu.VMEM((NA, ANG, WALL), F32),
            pltpu.VMEM((CX * CY, WALL), BF16),
            pltpu.VMEM((3 * CZ, CX * CY), BF16),
            pltpu.VMEM((NB, OWN, 2 * ANG), F32),
            pltpu.VMEM((NB - 1, OWN, 2 * ANG), F32),
            dma((5,)), dma((7,)), dma((4,)), dma((10,)), dma((10,)), dma((6,)), dma((6,)),
            dma((2,)), dma((2,)), dma((2,)), dma((2,)), dma((2,)), dma((2,)),
            dma, dma((NA,)), dma, dma((NA,)), dma, dma,
        ],
        compiler_params=pltpu.CompilerParams(
            collective_id=0, has_side_effects=True, vmem_limit_bytes=62 * 1024 * 1024 + 512 * 1024
        ),
        cost_estimate=pl.CostEstimate(flops=10**9, bytes_accessed=4 * 10**6, transcendentals=0),
    )(*args))


def solution(mesh):
    names = ("slab", "row", "col")
    sizes = tuple(mesh.shape[name] for name in names)
    cells = P(*names)
    vector = P(None, *names)
    slot = P(*names, None)
    in_specs = (cells, vector, cells, cells, cells, vector, cells, slot, slot, slot, cells, P())
    out_specs = (cells, vector, P(names, None))
    return jax.shard_map(
        functools.partial(local, *sizes), mesh=mesh, in_specs=in_specs, out_specs=out_specs, check_vma=False
    )
```

```python
import functools

import jax
import jax.numpy as jnp
from jax import lax
from jax.experimental import pallas as pl
from jax.experimental.pallas import tpu as pltpu
from jax.sharding import PartitionSpec as P

ANG = 64
CX = 4
CY = 128
CZ = 128
WALL = 512
OWN = 8
NXC = 4
NYC = 4
ZL = 4
ZH = 2
NA = NXC * NYC
NB = 2 * ZL * ZH
WIDTH = NB * OWN
BATCHES = (0, 5, 11, 16)
LINE = sorted(range(1, 16), key=lambda k: (-(k & 1), abs((k >> 2) - 2), k))
MESH = pl.DeviceIdType.MESH
PLANE = sorted(
    ((dy, dx) for dy in range(NYC) for dx in range(NXC)),
    key=lambda d: (min(d[0], NYC - d[0]) + min(d[1], NXC - d[1]), d),
)
F32 = jnp.float32
BF16 = jnp.bfloat16


def pieces(value):
    high = value.astype(BF16)
    rest = value - high.astype(F32)
    mid = rest.astype(BF16)
    low = (rest - mid.astype(F32)).astype(BF16)
    return high, mid, low


def kernel(
    ns, nr, nc,
    p_in, v_in, kap_in, drv_in, ap_in, av_in, mask_in, cells_in, rows_in, angle_in, count_in, step_in,
    ap_out, av_out, grad_out,
    cells_ref, rows_ref, angle_ref, count_ref, step_ref,
    pp, qq, kap, drv, ap, vel, total, mask,
    lam0, lam1, lam2, apo, q_near,
    zsend, zrecv, lsend, lrecv,
    turned_face, turned_wrap, face_parts, wrap_parts, slot_parts,
    cells_buf, answer, answered,
    ends, own_hot_y,
    slots, vals, hot, weight, where_hot, sens_t, dense, parts,
    small_sem, load_sem, store_sem, halo_send, halo_recv, lam_send, lam_recv,
    wrap_send, wrap_recv, cell_send, cell_recv, answer_send, answer_recv,
    slot_send, slot_recv, val_send, val_recv, part_send, part_recv,
):
    s = lax.axis_index("slab")
    r = lax.axis_index("row")
    c = lax.axis_index("col")
    y, zl = s >> 2, s & (ZL - 1)
    x_at, zh = c >> 1, c & (ZH - 1)
    group = y * NXC + x_at
    b = (zl * 2 + r) * ZH + zh

    def plane_peer(k):
        dy, dx = PLANE[k]
        return (((y + dy) & (NYC - 1)) * ZL + zl, r, ((x_at + dx) & (NXC - 1)) * ZH + zh)

    def line_place(k):
        return (zl + (k >> 2)) & (ZL - 1), r ^ ((k >> 1) & 1), zh ^ (k & 1)

    def line_peer(k):
        other_zl, other_r, other_zh = line_place(k)
        return (y * ZL + other_zl, other_r, x_at * ZH + other_zh)

    plane = jnp.zeros((CY, CZ), F32)
    strip = jnp.zeros((8, CZ), F32)
    for ref in (pp, qq, lam1):
        for x in range(CX):
            ref[x, pl.ds(0, 8)] = strip
            ref[x, pl.ds(CY + 8, 8)] = strip
    for ref in (q_near, ):
        ref[0] = plane
        ref[1] = plane
    lam0[0] = plane
    lam0[CX + 1] = plane
    zrecv[...] = jnp.zeros_like(zrecv)
    lrecv[...] = jnp.zeros_like(lrecv)
    answered[...] = jnp.zeros_like(answered)

    barrier = pltpu.get_barrier_semaphore()

    def greet(device):
        pl.semaphore_signal(barrier, inc=1, device_id=device, device_id_type=MESH)

    s_up, s_down = jnp.minimum(s + 1, ns - 1), jnp.maximum(s - 1, 0)
    r_up, r_down = jnp.minimum(r + 1, nr - 1), jnp.maximum(r - 1, 0)
    c_up, c_down = jnp.minimum(c + 1, nc - 1), jnp.maximum(c - 1, 0)
    has = {
        "xu": s < ns - 1, "xd": s > 0, "yu": r < nr - 1, "yd": r > 0, "zu": c < nc - 1, "zd": c > 0,
    }
    wrap_up = jnp.logical_and(zl == ZL - 1, has["xu"])
    wrap_down = jnp.logical_and(zl == 0, has["xd"])
    near_up = zl < ZL - 1
    near_down = zl > 0
    beyond = (
        (jnp.logical_and(zh == ZH - 1, has["zu"]), (s, r, c_up)),
        (jnp.logical_and(zh == 0, has["zd"]), (s, r, c_down)),
        (wrap_up, (s_up, r, c)),
        (wrap_down, (s_down, r, c)),
    )
    partners = NA - 1 + NB - 1
    for here, device in beyond:
        pl.when(here)(functools.partial(greet, device))
        partners = partners + here.astype(jnp.int32)
    for k in range(NA - 1, 0, -1):
        greet(plane_peer(k))
    for k in LINE:
        greet(line_peer(k))

    loads = [
        pltpu.make_async_copy(kap_in, kap, load_sem.at[0]),
        pltpu.make_async_copy(ap_in, ap, load_sem.at[1]),
        pltpu.make_async_copy(p_in, pp.at[pl.ds(0, CX), pl.ds(8, CY)], load_sem.at[2]),
        pltpu.make_async_copy(av_in, total, load_sem.at[3]),
        pltpu.make_async_copy(mask_in, mask, load_sem.at[4]),
        pltpu.make_async_copy(v_in, vel, load_sem.at[5]),
        pltpu.make_async_copy(drv_in, drv, load_sem.at[6]),
    ]
    small = [
        pltpu.make_async_copy(rows_in, rows_ref, small_sem.at[0]),
        pltpu.make_async_copy(angle_in, angle_ref, small_sem.at[1]),
        pltpu.make_async_copy(count_in, count_ref, small_sem.at[2]),
        pltpu.make_async_copy(cells_in, cells_ref, small_sem.at[3]),
        pltpu.make_async_copy(step_in, step_ref, small_sem.at[4]),
    ]
    for copy in small + loads:
        copy.start()

    lane = lax.broadcasted_iota(jnp.int32, (1, WALL), 1)
    for copy in small:
        copy.wait()
    own_rows = rows_ref[0, 0]
    live = lane < count_ref[0, 0, 0]
    bits = own_rows >> 3
    owner_group = ((bits >> 6) << 2) + ((bits >> 1) & 3)
    owner_line = (((bits >> 4) & 3) << 2) + (((bits >> 3) & 1) << 1) + (bits & 1)
    half = (own_rows >> 2) & 1
    code = owner_group * WIDTH + half * (WIDTH // 2) + owner_line * (OWN // 2) + (own_rows & (OWN // 2 - 1))
    slots[0, 0:1] = jnp.where(live, code.astype(F32), -1.0)
    slots[0, 1:2] = angle_ref[0, 0]
    row_at = (lax.broadcasted_iota(jnp.int32, (WIDTH, WALL), 0) + group * WIDTH).astype(F32)
    knots = lax.broadcasted_iota(jnp.int32, (ANG, WALL), 0).astype(F32)

    def at_slots(k):
        return pl.ds(pl.multiple_of(k * WALL, WALL), WALL)

    def prepare(k):
        hot[:, at_slots(k)] = jnp.where(slots[k, 0:1] == row_at, 1.0, 0.0).astype(BF16)
        dist = jnp.abs(slots[k, 1:2] - knots)
        dist = jnp.minimum(dist, ANG - dist)
        outer = jnp.maximum(2.0 - dist, 0.0)
        near = jnp.maximum(1.0 - dist, 0.0)
        weight[k] = (outer * outer * outer - 4.0 * near * near * near) * (1.0 / 6.0)


    own_cells = cells_ref[0, 0]
    cells_buf[0] = own_cells
    own_xy = own_cells >> 7
    own_x = own_cells >> 14
    own_z = own_cells & (CZ - 1)

    loads[0].wait()
    loads[1].wait()
    rows_of = pl.ds(8, CY)
    for x in range(CX):
        qq[x, rows_of] = kap[x] * ap[x]
    loads[2].wait()
    for i, (ref, at) in enumerate(((pp, 0), (qq, CX))):
        for x in range(CX):
            turned = ref[x, rows_of].T
            zsend[at + x:at + x + 1] = turned[0:1]
            zsend[8 + at + x:8 + at + x + 1] = turned[CZ - 1:CZ]
            if x in (0, CX - 1):
                turned_face[x // (CX - 1), i] = turned

    def split_into(ref, first, second):
        for i, field in enumerate((first, second)):
            for j, piece in enumerate(pieces(field)):
                ref[(3 * i + j) * CZ:(3 * i + j + 1) * CZ] = piece

    def pick(ref, hot_y, at_z):
        got = jnp.dot(ref[...], hot_y, preferred_element_type=F32)
        out = []
        for i in range(2):
            field = got[3 * i * CZ:(3 * i + 1) * CZ]
            field = field + got[(3 * i + 1) * CZ:(3 * i + 2) * CZ] + got[(3 * i + 2) * CZ:(3 * i + 3) * CZ]
            out.append(jnp.sum(jnp.where(y_at == at_z, field, 0.0), axis=0, keepdims=True))
        return out

    def hot_y_of(cells):
        return jnp.where(y_at == ((cells >> 7) & (CY - 1)), 1.0, 0.0).astype(BF16)


    pl.semaphore_wait(barrier, partners)

    def slot_copy(k):
        return pltpu.make_async_remote_copy(
            src_ref=slots.at[0], dst_ref=slots.at[k],
            send_sem=slot_send, recv_sem=slot_recv.at[k],
            device_id=plane_peer(k), device_id_type=MESH,
        )

    def halo(src, dst, sem_at, send_sem, recv_sem, device):
        return pltpu.make_async_remote_copy(
            src_ref=src, dst_ref=dst, send_sem=send_sem.at[sem_at], recv_sem=recv_sem.at[sem_at],
            device_id=device, device_id_type=MESH,
        )


    inner = pl.ds(0, CX)
    q_x = {
        "xu": halo(qq.at[CX - 1, rows_of], q_near.at[0], 0, halo_send, halo_recv, (s_up, r, c)),
        "xd": halo(qq.at[0, rows_of], q_near.at[1], 1, halo_send, halo_recv, (s_down, r, c)),
    }

    def field_y(ref, base):
        return {
            "yu": halo(ref.at[inner, pl.ds(CY, 8)], ref.at[inner, pl.ds(0, 8)], base, halo_send, halo_recv, (s, r_up, c)),
            "yd": halo(ref.at[inner, pl.ds(8, 8)], ref.at[inner, pl.ds(CY + 8, 8)], base + 1, halo_send, halo_recv, (s, r_down, c)),
        }

    q_y = field_y(qq, 4)
    p_y = field_y(pp, 6)
    wrap = {
        "xu": halo(turned_face.at[1], turned_wrap, 0, wrap_send, wrap_recv, (s_up, r, c)),
        "xd": halo(turned_face.at[0], turned_wrap, 1, wrap_send, wrap_recv, (s_down, r, c)),
    }
    ask = {
        "xu": halo(cells_buf.at[0], cells_buf.at[1], 0, cell_send, cell_recv, (s_up, r, c)),
        "xd": halo(cells_buf.at[0], cells_buf.at[2], 1, cell_send, cell_recv, (s_down, r, c)),
    }
    reply = {
        "xu": halo(answer.at[1], answered.at[0], 0, answer_send, answer_recv, (s_up, r, c)),
        "xd": halo(answer.at[0], answered.at[1], 1, answer_send, answer_recv, (s_down, r, c)),
    }
    pq_z = {
        "zu": halo(zsend.at[pl.ds(8, 8)], zrecv.at[pl.ds(0, 8)], 8, halo_send, halo_recv, (s, r, c_up)),
        "zd": halo(zsend.at[pl.ds(0, 8)], zrecv.at[pl.ds(8, 8)], 9, halo_send, halo_recv, (s, r, c_down)),
    }
    lam_x = {
        "xu": halo(lam0.at[CX], lam0.at[0], 0, lam_send, lam_recv, (s_up, r, c)),
        "xd": halo(lam0.at[1], lam0.at[CX + 1], 1, lam_send, lam_recv, (s_down, r, c)),
    }
    lam_y = {
        "yu": halo(lam1.at[inner, pl.ds(CY, 8)], lam1.at[inner, pl.ds(0, 8)], 2, lam_send, lam_recv, (s, r_up, c)),
        "yd": halo(lam1.at[inner, pl.ds(8, 8)], lam1.at[inner, pl.ds(CY + 8, 8)], 3, lam_send, lam_recv, (s, r_down, c)),
    }
    lam_z = {
        "zu": halo(lsend.at[pl.ds(8, 8)], lrecv.at[pl.ds(0, 8)], 4, lam_send, lam_recv, (s, r, c_up)),
        "zd": halo(lsend.at[pl.ds(0, 8)], lrecv.at[pl.ds(8, 8)], 5, lam_send, lam_recv, (s, r, c_down)),
    }

    def start(faces):
        for side, copy in faces.items():
            pl.when(has[side])(copy.start)

    opposite = {"xu": "xd", "xd": "xu", "yu": "yd", "yd": "yu", "zu": "zd", "zd": "zu"}

    def arrive(faces):
        for side, copy in faces.items():
            pl.when(has[opposite[side]])(copy.wait_recv)

    def sent(faces):
        for side, copy in faces.items():
            pl.when(has[side])(copy.wait_send)

    start(pq_z)
    start(q_y)
    start(p_y)
    pl.when(near_up)(ask["xu"].start)
    pl.when(near_down)(ask["xd"].start)
    pl.when(wrap_up)(wrap["xu"].start)
    pl.when(wrap_down)(wrap["xd"].start)
    for k in range(NA - 1, 0, -1):
        slot_copy(k).start()

    y_at = lax.broadcasted_iota(jnp.int32, (CY, WALL), 0)
    for x in range(CX):
        where_hot[x * CY:(x + 1) * CY] = jnp.where(y_at + x * CY == own_xy, 1.0, 0.0).astype(BF16)
    own_hot_y[...] = hot_y_of(own_cells)
    for side in range(2):
        split_into(face_parts.at[side], turned_face[side, 0], turned_face[side, 1])
    prepare(0)

    phase = jnp.cos(0.5 * jnp.full((1, CZ), lax.rem(step_ref[0], 97).astype(F32), F32))
    for copy in loads[3:]:
        copy.wait()
    arrive(q_y)
    arrive(p_y)

    def along_x(ref, x):
        if x == 0:
            return ref[1, rows_of] * 0.5
        if x == CX - 1:
            return ref[CX - 2, rows_of] * -0.5
        return (ref[x + 1, rows_of] - ref[x - 1, rows_of]) * 0.5

    def along_y(ref, x):
        return (ref[x, pl.ds(9, CY)] - ref[x, pl.ds(7, CY)]) * 0.5

    at_z = lax.broadcasted_iota(jnp.int32, (CY, CZ), 1)

    def along_z(field):
        upper = jnp.where(at_z == CZ - 1, 0.0, pltpu.roll(field, CZ - 1, 1))
        lower = jnp.where(at_z == 0, 0.0, pltpu.roll(field, 1, 1))
        return (upper - lower) * 0.5

    for x in range(CX):
        here = slice(x * CY, (x + 1) * CY)
        total_0 = total[0, x] + along_x(qq, x)
        total_1 = total[1, x] + along_y(qq, x)
        total_2 = total[2, x] + along_z(qq[x, rows_of])
        total[0, x] = total_0
        total[1, x] = total_1
        total[2, x] = total_2
        moved_0 = vel[0, x] - 0.3 * along_x(pp, x) + drv[x] * phase
        moved_2 = vel[2, x] - 0.3 * along_z(pp[x, rows_of])
        sens = -(
            total_0 * moved_0 + total_1 * (vel[1, x] - 0.3 * along_y(pp, x)) + total_2 * moved_2
        )
        for i, piece in enumerate(pieces(sens.T)):
            sens_t[i * CZ:(i + 1) * CZ, here] = piece
        if x in (0, CX - 1):
            split_into(slot_parts.at[x // (CX - 1)], total_0.T, moved_0.T)
        for i, field in enumerate((total_2.T, moved_2.T)):
            ends[i:i + 1, here] = field[0:1]
            ends[2 + i:3 + i, here] = field[CZ - 1:CZ]

    def serve(side, at):
        cells = cells_buf[at]
        p_at, q_at = pick(face_parts.at[side], hot_y_of(cells), cells & (CZ - 1))
        answer[side, 0:1] = p_at
        answer[side, 1:2] = q_at

    @pl.when(near_up)
    def _():
        ask["xd"].wait_recv()
        serve(1, 2)
        reply["xu"].start()

    @pl.when(near_down)
    def _():
        ask["xu"].wait_recv()
        serve(0, 1)
        reply["xd"].start()

    pl.when(near_up)(q_x["xu"].start)
    pl.when(near_down)(q_x["xd"].start)

    on_face = [
        pick(slot_parts.at[side], where_hot[side * (CX - 1) * CY:(side * (CX - 1) + 1) * CY], own_z)
        for side in range(2)
    ]

    edge_parts = jnp.concatenate(pieces(ends[...]), axis=0)
    edge = jnp.dot(edge_parts, where_hot[...], preferred_element_type=F32)
    edge = edge[0:4] + edge[4:8] + edge[8:12]

    picked = jnp.dot(sens_t[...], where_hot[...], preferred_element_type=F32)
    picked = picked[0:CZ] + picked[CZ:2 * CZ] + picked[2 * CZ:3 * CZ]
    picked = jnp.sum(jnp.where(y_at == own_z, picked, 0.0), axis=0, keepdims=True)

    def corrected(value, side, here, total_at, moved_at, p_at, q_at):
        sign = 2.0 * side - 1.0
        more_total = jnp.where(here, q_at, 0.0) * (0.5 * sign)
        more_moved = jnp.where(here, p_at, 0.0) * (-0.15 * sign)
        return value - (more_total * (moved_at + more_moved) + total_at * more_moved)

    arrive(pq_z)
    z_parts = jnp.concatenate(pieces(zrecv[...]), axis=0)
    faces_z = jnp.dot(z_parts, own_hot_y[...], preferred_element_type=F32)
    faces_z = faces_z[0:16] + faces_z[16:32] + faces_z[32:48]
    row_x = lax.broadcasted_iota(jnp.int32, (16, WALL), 0) & (CX - 1)
    faces_z = jnp.where(row_x == own_x, faces_z, 0.0)
    for side in range(2):
        p_at = jnp.sum(faces_z[8 * side:8 * side + 4], axis=0, keepdims=True)
        q_at = jnp.sum(faces_z[8 * side + 4:8 * side + 8], axis=0, keepdims=True)
        here = own_z == side * (CZ - 1)
        picked = corrected(picked, side, here, edge[2 * side:2 * side + 1], edge[2 * side + 1:2 * side + 2], p_at, q_at)

    pl.when(near_down)(reply["xu"].wait_recv)
    pl.when(near_up)(reply["xd"].wait_recv)

    def own_answer(side):
        split_into(wrap_parts, turned_wrap[0], turned_wrap[1])
        p_at, q_at = pick(wrap_parts, own_hot_y[...], cells_buf[0] & (CZ - 1))
        answered[side, 0:1] = p_at
        answered[side, 1:2] = q_at

    @pl.when(wrap_down)
    def _():
        wrap["xu"].wait_recv()
        own_answer(0)

    @pl.when(wrap_up)
    def _():
        wrap["xd"].wait_recv()
        own_answer(1)

    for side, (total_at, moved_at) in enumerate(on_face):
        here = own_x == side * (CX - 1)
        picked = corrected(picked, side, here, total_at, moved_at, answered[side, 0:1], answered[side, 1:2])
    vals[0] = picked

    for k in range(NA - 1, 0, -1):
        pltpu.make_async_remote_copy(
            src_ref=vals.at[0], dst_ref=vals.at[k], send_sem=val_send, recv_sem=val_recv.at[k],
            device_id=plane_peer(k), device_id_type=MESH,
        ).start()

    pl.when(near_down)(q_x["xu"].wait_recv)
    pl.when(near_up)(q_x["xd"].wait_recv)

    @pl.when(wrap_down)
    def _():
        q_near[0] = turned_wrap[1].T

    @pl.when(wrap_up)
    def _():
        q_near[1] = turned_wrap[1].T

    edge_t = jnp.concatenate([zrecv[...], jnp.zeros((CZ - 16, CZ), F32)], axis=0).T

    def with_edges(field, low, high):
        field = jnp.where(at_z == CZ - 1, field + high * 0.5, field)
        return jnp.where(at_z == 0, field - low * 0.5, field)

    for x in range(CX):
        free = 1.0 - mask[x].astype(F32)
        total_0 = total[0, x]
        if x == 0:
            total_0 = total_0 - q_near[0] * 0.5
        if x == CX - 1:
            total_0 = total_0 + q_near[1] * 0.5
        lam0[x + 1] = free * total_0
        lam1[x, rows_of] = free * total[1, x]
        low, high = (edge_t[:, 8 * i + CX + x:8 * i + CX + x + 1] for i in range(2))
        lam2[x] = free * with_edges(total[2, x], low, high)

    start(lam_x)
    start(lam_y)
    for x in range(CX):
        turned = lam2[x].T
        lsend[x:x + 1] = turned[0:1]
        lsend[8 + x:9 + x] = turned[CZ - 1:CZ]
    start(lam_z)
    stores = [
        pltpu.make_async_copy(lam0.at[pl.ds(1, CX)], av_out.at[0], store_sem.at[0]),
        pltpu.make_async_copy(lam1.at[pl.ds(0, CX), rows_of], av_out.at[1], store_sem.at[1]),
        pltpu.make_async_copy(lam2, av_out.at[2], store_sem.at[2]),
    ]
    for copy in stores:
        copy.start()

    def slots_of(k, _):
        pltpu.make_async_copy(slots.at[k], slots.at[k], slot_recv.at[k]).wait()
        prepare(k)
        return 0

    rest = slots.at[pl.ds(1, NA - 1)]
    lax.fori_loop(1, NA, slots_of, 0)

    rest_vals = vals.at[pl.ds(1, NA - 1)]
    summed = None
    for low, high in zip(BATCHES[:-1], BATCHES[1:]):
        for k in range(max(low, 1), high):
            pltpu.make_async_copy(vals.at[k], vals.at[k], val_recv.at[k]).wait()
        split = [pieces(weight[k] * vals[k]) for k in range(low, high)]
        scaled = jnp.concatenate(
            [jnp.concatenate([one[i] for one in split], axis=1) for i in range(3)], axis=0
        )
        product = lax.dot_general(
            hot[:, low * WALL:high * WALL], scaled, (((1,), (1,)), ((), ())), preferred_element_type=F32
        )
        summed = product if summed is None else summed + product
    summed = summed[:, 0:ANG] + summed[:, ANG:2 * ANG] + summed[:, 2 * ANG:3 * ANG]
    packed = jnp.concatenate([summed[0:WIDTH // 2], summed[WIDTH // 2:WIDTH]], axis=1)
    dense[...] = packed.reshape(NB, OWN // 2, 2 * ANG)

    for k in LINE:
        other_zl, other_r, other_zh = line_place(k)
        pltpu.make_async_remote_copy(
            src_ref=dense.at[(other_zl * 2 + other_r) * ZH + other_zh], dst_ref=parts.at[k - 1],
            send_sem=part_send, recv_sem=part_recv, device_id=line_peer(k), device_id_type=MESH,
        ).start()

    for faces in (lam_x, lam_y, lam_z):
        arrive(faces)
    edge_l = jnp.concatenate([lrecv[...], jnp.zeros((CZ - 16, CZ), F32)], axis=0).T
    for x in range(CX):
        div = (
            (lam0[x + 2] - lam0[x]) * 0.5
            + (lam1[x, pl.ds(9, CY)] - lam1[x, pl.ds(7, CY)]) * 0.5
            + with_edges(along_z(lam2[x]), edge_l[:, x:x + 1], edge_l[:, 8 + x:9 + x])
        )
        apo[x] = ap[x] + 0.3 * div
    last = pltpu.make_async_copy(apo, ap_out, store_sem.at[3])
    last.start()

    pltpu.make_async_copy(parts, parts, part_recv).wait()
    own = dense[b] + jnp.sum(parts[...], axis=0)
    grad_out[...] = jnp.concatenate([own[:, 0:ANG], own[:, ANG:2 * ANG]], axis=0)

    for faces in (q_y, p_y, pq_z, lam_x, lam_y, lam_z):
        sent(faces)
    pl.when(wrap_up)(wrap["xu"].wait_send)
    pl.when(wrap_down)(wrap["xd"].wait_send)
    for faces in (ask, reply, q_x):
        pl.when(near_up)(faces["xu"].wait_send)
        pl.when(near_down)(faces["xd"].wait_send)
    pltpu.make_async_copy(rest, rest, slot_send).wait()
    pltpu.make_async_copy(rest_vals, rest_vals, val_send).wait()
    pltpu.make_async_copy(parts, parts, part_send).wait()
    for copy in stores + [last]:
        copy.wait()


def written(outs):
    anyspace = pl.BlockSpec(memory_space=pl.ANY)
    return pl.pallas_call(
        hand_over,
        out_shape=tuple(jax.ShapeDtypeStruct(o.shape, o.dtype) for o in outs),
        in_specs=[anyspace] * 3,
        out_specs=(anyspace,) * 3,
        scratch_shapes=[pltpu.SemaphoreType.DMA((9,))],
        compiler_params=pltpu.CompilerParams(vmem_limit_bytes=1024 * 1024),
    )(*outs)


def hand_over(adj_p, adj_v, grad, adj_p_out, adj_v_out, grad_out, sem):
    pairs = [(grad, grad_out)]
    for x in range(0, CX, 2):
        here = pl.ds(x, 2)
        pairs.append((adj_p.at[here], adj_p_out.at[here]))
        for k in range(3):
            pairs.append((adj_v.at[k, here], adj_v_out.at[k, here]))
    copies = [pltpu.make_async_copy(a, b, sem.at[i]) for i, (a, b) in enumerate(pairs)]
    for copy in copies:
        copy.start()
    for copy in copies:
        copy.wait()


def local(ns, nr, nc, *args):
    hbm = pl.BlockSpec(memory_space=pltpu.HBM)
    vmem = pl.BlockSpec(memory_space=pltpu.VMEM)
    block = (CX, CY, CZ)
    dma = pltpu.SemaphoreType.DMA
    return written(pl.pallas_call(
        functools.partial(kernel, ns, nr, nc),
        out_shape=(
            pltpu.VMEM(block, F32),
            pltpu.VMEM((3,) + block, F32),
            pltpu.VMEM((OWN, ANG), F32),
        ),
        in_specs=[hbm] * 12,
        out_specs=(pl.BlockSpec(memory_space=pl.ANY), pl.BlockSpec(memory_space=pl.ANY), vmem),
        scratch_shapes=[
            pltpu.VMEM((1, 1, 1, WALL), jnp.int32),
            pltpu.VMEM((1, 1, 1, WALL), jnp.int32),
            pltpu.VMEM((1, 1, 1, WALL), F32),
            pltpu.SMEM((1, 1, 1), jnp.int32),
            pltpu.SMEM((1,), jnp.int32),
            pltpu.VMEM((CX, CY + 16, CZ), F32),
            pltpu.VMEM((CX, CY + 16, CZ), F32),
            pltpu.VMEM(block, F32),
            pltpu.VMEM(block, F32),
            pltpu.VMEM(block, F32),
            pltpu.VMEM((3,) + block, F32),
            pltpu.VMEM((3,) + block, F32),
            pltpu.VMEM(block, jnp.int32),
            pltpu.VMEM((CX + 2, CY, CZ), F32),
            pltpu.VMEM((CX, CY + 16, CZ), F32),
            pltpu.VMEM(block, F32),
            pltpu.VMEM(block, F32),
            pltpu.VMEM((2, CY, CZ), F32),
            pltpu.VMEM((16, CY), F32),
            pltpu.VMEM((16, CY), F32),
            pltpu.VMEM((16, CY), F32),
            pltpu.VMEM((16, CY), F32),
            pltpu.VMEM((2, 2, CZ, CY), F32),
            pltpu.VMEM((2, CZ, CY), F32),
            pltpu.VMEM((2, 6 * CZ, CY), BF16),
            pltpu.VMEM((6 * CZ, CY), BF16),
            pltpu.VMEM((2, 6 * CZ, CY), BF16),
            pltpu.VMEM((3, 1, WALL), jnp.int32),
            pltpu.VMEM((2, 2, WALL), F32),
            pltpu.VMEM((2, 2, WALL), F32),
            pltpu.VMEM((4, CX * CY), F32),
            pltpu.VMEM((CY, WALL), BF16),
            pltpu.VMEM((NA, 2, WALL), F32),
            pltpu.VMEM((NA, 1, WALL), F32),
            pltpu.VMEM((WIDTH, NA * WALL), BF16),
            pltpu.VMEM((NA, ANG, WALL), F32),
            pltpu.VMEM((CX * CY, WALL), BF16),
            pltpu.VMEM((3 * CZ, CX * CY), BF16),
            pltpu.VMEM((NB, OWN // 2, 2 * ANG), F32),
            pltpu.VMEM((NB - 1, OWN // 2, 2 * ANG), F32),
            dma((5,)), dma((7,)), dma((4,)), dma((10,)), dma((10,)), dma((6,)), dma((6,)),
            dma((2,)), dma((2,)), dma((2,)), dma((2,)), dma((2,)), dma((2,)),
            dma, dma((NA,)), dma, dma((NA,)), dma, dma,
        ],
        compiler_params=pltpu.CompilerParams(
            collective_id=0, has_side_effects=True, vmem_limit_bytes=62 * 1024 * 1024 + 512 * 1024
        ),
        cost_estimate=pl.CostEstimate(flops=10**9, bytes_accessed=4 * 10**6, transcendentals=0),
    )(*args))


def solution(mesh):
    names = ("slab", "row", "col")
    sizes = tuple(mesh.shape[name] for name in names)
    cells = P(*names)
    vector = P(None, *names)
    slot = P(*names, None)
    in_specs = (cells, vector, cells, cells, cells, vector, cells, slot, slot, slot, cells, P())
    out_specs = (cells, vector, P(names, None))
    return jax.shard_map(
        functools.partial(local, *sizes), mesh=mesh, in_specs=in_specs, out_specs=out_specs, check_vma=False
    )
```

```python
import functools

import jax
import jax.numpy as jnp
from jax import lax
from jax.experimental import pallas as pl
from jax.experimental.pallas import tpu as pltpu
from jax.sharding import PartitionSpec as P

ANG = 64
CX = 4
CY = 128
CZ = 128
WALL = 512
OWN = 8
NXC = 4
NYC = 4
ZL = 4
ZH = 2
NA = NXC * NYC
NB = 2 * ZL * ZH
WIDTH = NB * OWN
BATCHES = (0, 5, 11, 16)
LINE = sorted(range(1, 16), key=lambda k: (-(k & 1), abs((k >> 2) - 2), k))
MESH = pl.DeviceIdType.MESH
PLANE = sorted(
    ((dy, dx) for dy in range(NYC) for dx in range(NXC)),
    key=lambda d: (min(d[0], NYC - d[0]) + min(d[1], NXC - d[1]), d),
)
F32 = jnp.float32
BF16 = jnp.bfloat16


def pieces(value):
    high = value.astype(BF16)
    rest = value - high.astype(F32)
    mid = rest.astype(BF16)
    low = (rest - mid.astype(F32)).astype(BF16)
    return high, mid, low


def kernel(
    ns, nr, nc,
    p_in, v_in, kap_in, drv_in, ap_in, av_in, mask_in, cells_in, rows_in, angle_in, count_in, step_in,
    ap_out, av_out, grad_out,
    cells_ref, rows_ref, angle_ref, count_ref, step_ref,
    pp, qq, kap, drv, ap, vel, total, mask,
    lam0, lam1, lam2, apo, q_near,
    zsend, zrecv, lsend, lrecv,
    turned_face, turned_wrap, face_parts, wrap_parts, slot_parts,
    cells_buf, answer, answered,
    ends, own_hot_y,
    slots, vals, hot, weight, where_hot, sens_t, dense, parts,
    small_sem, load_sem, store_sem, halo_send, halo_recv, lam_send, lam_recv,
    wrap_send, wrap_recv, cell_send, cell_recv, answer_send, answer_recv,
    slot_send, slot_recv, val_send, val_recv, part_send, part_recv,
):
    s = lax.axis_index("slab")
    r = lax.axis_index("row")
    c = lax.axis_index("col")
    y, zl = s >> 2, s & (ZL - 1)
    x_at, zh = c >> 1, c & (ZH - 1)
    group = y * NXC + x_at
    b = (zl * 2 + r) * ZH + zh

    def plane_peer(k):
        dy, dx = PLANE[k]
        return (((y + dy) & (NYC - 1)) * ZL + zl, r, ((x_at + dx) & (NXC - 1)) * ZH + zh)

    def line_place(k):
        return (zl + (k >> 2)) & (ZL - 1), r ^ ((k >> 1) & 1), zh ^ (k & 1)

    def line_peer(k):
        other_zl, other_r, other_zh = line_place(k)
        return (y * ZL + other_zl, other_r, x_at * ZH + other_zh)

    plane = jnp.zeros((CY, CZ), F32)
    strip = jnp.zeros((8, CZ), F32)
    for ref in (pp, qq, lam1):
        for x in range(CX):
            ref[x, pl.ds(0, 8)] = strip
            ref[x, pl.ds(CY + 8, 8)] = strip
    for ref in (q_near, ):
        ref[0] = plane
        ref[1] = plane
    lam0[0] = plane
    lam0[CX + 1] = plane
    zrecv[...] = jnp.zeros_like(zrecv)
    lrecv[...] = jnp.zeros_like(lrecv)
    answered[...] = jnp.zeros_like(answered)

    barrier = pltpu.get_barrier_semaphore()

    def greet(device):
        pl.semaphore_signal(barrier, inc=1, device_id=device, device_id_type=MESH)

    s_up, s_down = jnp.minimum(s + 1, ns - 1), jnp.maximum(s - 1, 0)
    r_up, r_down = jnp.minimum(r + 1, nr - 1), jnp.maximum(r - 1, 0)
    c_up, c_down = jnp.minimum(c + 1, nc - 1), jnp.maximum(c - 1, 0)
    has = {
        "xu": s < ns - 1, "xd": s > 0, "yu": r < nr - 1, "yd": r > 0, "zu": c < nc - 1, "zd": c > 0,
    }
    wrap_up = jnp.logical_and(zl == ZL - 1, has["xu"])
    wrap_down = jnp.logical_and(zl == 0, has["xd"])
    near_up = zl < ZL - 1
    near_down = zl > 0
    beyond = (
        (jnp.logical_and(zh == ZH - 1, has["zu"]), (s, r, c_up)),
        (jnp.logical_and(zh == 0, has["zd"]), (s, r, c_down)),
        (wrap_up, (s_up, r, c)),
        (wrap_down, (s_down, r, c)),
    )
    partners = NA - 1 + NB - 1
    for here, device in beyond:
        pl.when(here)(functools.partial(greet, device))
        partners = partners + here.astype(jnp.int32)
    for k in range(NA - 1, 0, -1):
        greet(plane_peer(k))
    for k in LINE:
        greet(line_peer(k))

    loads = [
        pltpu.make_async_copy(kap_in, kap, load_sem.at[0]),
        pltpu.make_async_copy(ap_in, ap, load_sem.at[1]),
        pltpu.make_async_copy(p_in, pp.at[pl.ds(0, CX), pl.ds(8, CY)], load_sem.at[2]),
        pltpu.make_async_copy(av_in, total, load_sem.at[3]),
        pltpu.make_async_copy(mask_in, mask, load_sem.at[4]),
        pltpu.make_async_copy(v_in, vel, load_sem.at[5]),
        pltpu.make_async_copy(drv_in, drv, load_sem.at[6]),
    ]
    small = [
        pltpu.make_async_copy(rows_in, rows_ref, small_sem.at[0]),
        pltpu.make_async_copy(angle_in, angle_ref, small_sem.at[1]),
        pltpu.make_async_copy(count_in, count_ref, small_sem.at[2]),
        pltpu.make_async_copy(cells_in, cells_ref, small_sem.at[3]),
        pltpu.make_async_copy(step_in, step_ref, small_sem.at[4]),
    ]
    for copy in small + loads:
        copy.start()

    lane = lax.broadcasted_iota(jnp.int32, (1, WALL), 1)
    for copy in small:
        copy.wait()
    own_rows = rows_ref[0, 0]
    live = lane < count_ref[0, 0, 0]
    bits = own_rows >> 3
    owner_group = ((bits >> 6) << 2) + ((bits >> 1) & 3)
    owner_line = (((bits >> 4) & 3) << 2) + (((bits >> 3) & 1) << 1) + (bits & 1)
    half = (own_rows >> 2) & 1
    code = owner_group * WIDTH + half * (WIDTH // 2) + owner_line * (OWN // 2) + (own_rows & (OWN // 2 - 1))
    slots[0, 0:1] = jnp.where(live, code.astype(F32), -1.0)
    slots[0, 1:2] = angle_ref[0, 0]
    row_at = (lax.broadcasted_iota(jnp.int32, (WIDTH, WALL), 0) + group * WIDTH).astype(F32)
    knots = lax.broadcasted_iota(jnp.int32, (ANG, WALL), 0).astype(F32)

    def at_slots(k):
        return pl.ds(pl.multiple_of(k * WALL, WALL), WALL)

    def prepare(k):
        hot[:, at_slots(k)] = jnp.where(slots[k, 0:1] == row_at, 1.0, 0.0).astype(BF16)
        dist = jnp.abs(slots[k, 1:2] - knots)
        dist = jnp.minimum(dist, ANG - dist)
        outer = jnp.maximum(2.0 - dist, 0.0)
        near = jnp.maximum(1.0 - dist, 0.0)
        weight[k] = (outer * outer * outer - 4.0 * near * near * near) * (1.0 / 6.0)


    own_cells = cells_ref[0, 0]
    cells_buf[0] = own_cells
    own_xy = own_cells >> 7
    own_x = own_cells >> 14
    own_z = own_cells & (CZ - 1)

    loads[0].wait()
    loads[1].wait()
    rows_of = pl.ds(8, CY)
    for x in range(CX):
        qq[x, rows_of] = kap[x] * ap[x]
    loads[2].wait()
    for i, (ref, at) in enumerate(((pp, 0), (qq, CX))):
        for x in range(CX):
            turned = ref[x, rows_of].T
            zsend[at + x:at + x + 1] = turned[0:1]
            zsend[8 + at + x:8 + at + x + 1] = turned[CZ - 1:CZ]
            if x in (0, CX - 1):
                turned_face[x // (CX - 1), i] = turned

    picks = 2

    def split_into(ref, first, second):
        for i, field in enumerate((first, second)):
            for j, piece in enumerate(pieces(field)[:picks]):
                ref[(picks * i + j) * CZ:(picks * i + j + 1) * CZ] = piece

    def pick(ref, hot_y, at_z):
        got = jnp.dot(ref[0:2 * picks * CZ], hot_y, preferred_element_type=F32)
        out = []
        for i in range(2):
            field = got[picks * i * CZ:(picks * i + 1) * CZ]
            for j in range(1, picks):
                field = field + got[(picks * i + j) * CZ:(picks * i + j + 1) * CZ]
            out.append(jnp.sum(jnp.where(y_at == at_z, field, 0.0), axis=0, keepdims=True))
        return out

    def hot_y_of(cells):
        return jnp.where(y_at == ((cells >> 7) & (CY - 1)), 1.0, 0.0).astype(BF16)


    pl.semaphore_wait(barrier, partners)

    def slot_copy(k):
        return pltpu.make_async_remote_copy(
            src_ref=slots.at[0], dst_ref=slots.at[k],
            send_sem=slot_send, recv_sem=slot_recv.at[k],
            device_id=plane_peer(k), device_id_type=MESH,
        )

    def halo(src, dst, sem_at, send_sem, recv_sem, device):
        return pltpu.make_async_remote_copy(
            src_ref=src, dst_ref=dst, send_sem=send_sem.at[sem_at], recv_sem=recv_sem.at[sem_at],
            device_id=device, device_id_type=MESH,
        )


    inner = pl.ds(0, CX)
    q_x = {
        "xu": halo(qq.at[CX - 1, rows_of], q_near.at[0], 0, halo_send, halo_recv, (s_up, r, c)),
        "xd": halo(qq.at[0, rows_of], q_near.at[1], 1, halo_send, halo_recv, (s_down, r, c)),
    }

    def field_y(ref, base):
        return {
            "yu": halo(ref.at[inner, pl.ds(CY, 8)], ref.at[inner, pl.ds(0, 8)], base, halo_send, halo_recv, (s, r_up, c)),
            "yd": halo(ref.at[inner, pl.ds(8, 8)], ref.at[inner, pl.ds(CY + 8, 8)], base + 1, halo_send, halo_recv, (s, r_down, c)),
        }

    q_y = field_y(qq, 4)
    p_y = field_y(pp, 6)
    wrap = {
        "xu": halo(turned_face.at[1], turned_wrap, 0, wrap_send, wrap_recv, (s_up, r, c)),
        "xd": halo(turned_face.at[0], turned_wrap, 1, wrap_send, wrap_recv, (s_down, r, c)),
    }
    ask = {
        "xu": halo(cells_buf.at[0], cells_buf.at[1], 0, cell_send, cell_recv, (s_up, r, c)),
        "xd": halo(cells_buf.at[0], cells_buf.at[2], 1, cell_send, cell_recv, (s_down, r, c)),
    }
    reply = {
        "xu": halo(answer.at[1], answered.at[0], 0, answer_send, answer_recv, (s_up, r, c)),
        "xd": halo(answer.at[0], answered.at[1], 1, answer_send, answer_recv, (s_down, r, c)),
    }
    pq_z = {
        "zu": halo(zsend.at[pl.ds(8, 8)], zrecv.at[pl.ds(0, 8)], 8, halo_send, halo_recv, (s, r, c_up)),
        "zd": halo(zsend.at[pl.ds(0, 8)], zrecv.at[pl.ds(8, 8)], 9, halo_send, halo_recv, (s, r, c_down)),
    }
    lam_x = {
        "xu": halo(lam0.at[CX], lam0.at[0], 0, lam_send, lam_recv, (s_up, r, c)),
        "xd": halo(lam0.at[1], lam0.at[CX + 1], 1, lam_send, lam_recv, (s_down, r, c)),
    }
    lam_y = {
        "yu": halo(lam1.at[inner, pl.ds(CY, 8)], lam1.at[inner, pl.ds(0, 8)], 2, lam_send, lam_recv, (s, r_up, c)),
        "yd": halo(lam1.at[inner, pl.ds(8, 8)], lam1.at[inner, pl.ds(CY + 8, 8)], 3, lam_send, lam_recv, (s, r_down, c)),
    }
    lam_z = {
        "zu": halo(lsend.at[pl.ds(8, 8)], lrecv.at[pl.ds(0, 8)], 4, lam_send, lam_recv, (s, r, c_up)),
        "zd": halo(lsend.at[pl.ds(0, 8)], lrecv.at[pl.ds(8, 8)], 5, lam_send, lam_recv, (s, r, c_down)),
    }

    def start(faces):
        for side, copy in faces.items():
            pl.when(has[side])(copy.start)

    opposite = {"xu": "xd", "xd": "xu", "yu": "yd", "yd": "yu", "zu": "zd", "zd": "zu"}

    def arrive(faces):
        for side, copy in faces.items():
            pl.when(has[opposite[side]])(copy.wait_recv)

    def sent(faces):
        for side, copy in faces.items():
            pl.when(has[side])(copy.wait_send)

    start(pq_z)
    start(q_y)
    start(p_y)
    pl.when(near_up)(ask["xu"].start)
    pl.when(near_down)(ask["xd"].start)
    pl.when(wrap_up)(wrap["xu"].start)
    pl.when(wrap_down)(wrap["xd"].start)
    for k in range(NA - 1, 0, -1):
        slot_copy(k).start()

    y_at = lax.broadcasted_iota(jnp.int32, (CY, WALL), 0)
    for x in range(CX):
        where_hot[x * CY:(x + 1) * CY] = jnp.where(y_at + x * CY == own_xy, 1.0, 0.0).astype(BF16)
    own_hot_y[...] = hot_y_of(own_cells)
    for side in range(2):
        split_into(face_parts.at[side], turned_face[side, 0], turned_face[side, 1])
    prepare(0)

    phase = jnp.cos(0.5 * jnp.full((1, CZ), lax.rem(step_ref[0], 97).astype(F32), F32))
    for copy in loads[3:]:
        copy.wait()
    arrive(q_y)
    arrive(p_y)

    def along_x(ref, x):
        if x == 0:
            return ref[1, rows_of] * 0.5
        if x == CX - 1:
            return ref[CX - 2, rows_of] * -0.5
        return (ref[x + 1, rows_of] - ref[x - 1, rows_of]) * 0.5

    def along_y(ref, x):
        return (ref[x, pl.ds(9, CY)] - ref[x, pl.ds(7, CY)]) * 0.5

    at_z = lax.broadcasted_iota(jnp.int32, (CY, CZ), 1)

    def along_z(field):
        upper = jnp.where(at_z == CZ - 1, 0.0, pltpu.roll(field, CZ - 1, 1))
        lower = jnp.where(at_z == 0, 0.0, pltpu.roll(field, 1, 1))
        return (upper - lower) * 0.5

    for x in range(CX):
        here = slice(x * CY, (x + 1) * CY)
        total_0 = total[0, x] + along_x(qq, x)
        total_1 = total[1, x] + along_y(qq, x)
        total_2 = total[2, x] + along_z(qq[x, rows_of])
        total[0, x] = total_0
        total[1, x] = total_1
        total[2, x] = total_2
        moved_0 = vel[0, x] - 0.3 * along_x(pp, x) + drv[x] * phase
        moved_2 = vel[2, x] - 0.3 * along_z(pp[x, rows_of])
        sens = -(
            total_0 * moved_0 + total_1 * (vel[1, x] - 0.3 * along_y(pp, x)) + total_2 * moved_2
        )
        for i, piece in enumerate(pieces(sens.T)):
            sens_t[i * CZ:(i + 1) * CZ, here] = piece
        if x in (0, CX - 1):
            split_into(slot_parts.at[x // (CX - 1)], total_0.T, moved_0.T)
        for i, field in enumerate((total_2.T, moved_2.T)):
            ends[i:i + 1, here] = field[0:1]
            ends[2 + i:3 + i, here] = field[CZ - 1:CZ]

    def serve(side, at):
        cells = cells_buf[at]
        p_at, q_at = pick(face_parts.at[side], hot_y_of(cells), cells & (CZ - 1))
        answer[side, 0:1] = p_at
        answer[side, 1:2] = q_at

    @pl.when(near_up)
    def _():
        ask["xd"].wait_recv()
        serve(1, 2)
        reply["xu"].start()

    @pl.when(near_down)
    def _():
        ask["xu"].wait_recv()
        serve(0, 1)
        reply["xd"].start()

    pl.when(near_up)(q_x["xu"].start)
    pl.when(near_down)(q_x["xd"].start)

    on_face = [
        pick(slot_parts.at[side], where_hot[side * (CX - 1) * CY:(side * (CX - 1) + 1) * CY], own_z)
        for side in range(2)
    ]

    edge_parts = jnp.concatenate(pieces(ends[...]), axis=0)
    edge = jnp.dot(edge_parts, where_hot[...], preferred_element_type=F32)
    edge = edge[0:4] + edge[4:8] + edge[8:12]

    picked = jnp.dot(sens_t[...], where_hot[...], preferred_element_type=F32)
    picked = picked[0:CZ] + picked[CZ:2 * CZ] + picked[2 * CZ:3 * CZ]
    picked = jnp.sum(jnp.where(y_at == own_z, picked, 0.0), axis=0, keepdims=True)

    def corrected(value, side, here, total_at, moved_at, p_at, q_at):
        sign = 2.0 * side - 1.0
        more_total = jnp.where(here, q_at, 0.0) * (0.5 * sign)
        more_moved = jnp.where(here, p_at, 0.0) * (-0.15 * sign)
        return value - (more_total * (moved_at + more_moved) + total_at * more_moved)

    arrive(pq_z)
    z_parts = jnp.concatenate(pieces(zrecv[...]), axis=0)
    faces_z = jnp.dot(z_parts, own_hot_y[...], preferred_element_type=F32)
    faces_z = faces_z[0:16] + faces_z[16:32] + faces_z[32:48]
    row_x = lax.broadcasted_iota(jnp.int32, (16, WALL), 0) & (CX - 1)
    faces_z = jnp.where(row_x == own_x, faces_z, 0.0)
    for side in range(2):
        p_at = jnp.sum(faces_z[8 * side:8 * side + 4], axis=0, keepdims=True)
        q_at = jnp.sum(faces_z[8 * side + 4:8 * side + 8], axis=0, keepdims=True)
        here = own_z == side * (CZ - 1)
        picked = corrected(picked, side, here, edge[2 * side:2 * side + 1], edge[2 * side + 1:2 * side + 2], p_at, q_at)

    pl.when(near_down)(reply["xu"].wait_recv)
    pl.when(near_up)(reply["xd"].wait_recv)

    def own_answer(side):
        split_into(wrap_parts, turned_wrap[0], turned_wrap[1])
        p_at, q_at = pick(wrap_parts, own_hot_y[...], cells_buf[0] & (CZ - 1))
        answered[side, 0:1] = p_at
        answered[side, 1:2] = q_at

    @pl.when(wrap_down)
    def _():
        wrap["xu"].wait_recv()
        own_answer(0)

    @pl.when(wrap_up)
    def _():
        wrap["xd"].wait_recv()
        own_answer(1)

    for side, (total_at, moved_at) in enumerate(on_face):
        here = own_x == side * (CX - 1)
        picked = corrected(picked, side, here, total_at, moved_at, answered[side, 0:1], answered[side, 1:2])
    vals[0] = picked

    for k in range(NA - 1, 0, -1):
        pltpu.make_async_remote_copy(
            src_ref=vals.at[0], dst_ref=vals.at[k], send_sem=val_send, recv_sem=val_recv.at[k],
            device_id=plane_peer(k), device_id_type=MESH,
        ).start()

    pl.when(near_down)(q_x["xu"].wait_recv)
    pl.when(near_up)(q_x["xd"].wait_recv)

    @pl.when(wrap_down)
    def _():
        q_near[0] = turned_wrap[1].T

    @pl.when(wrap_up)
    def _():
        q_near[1] = turned_wrap[1].T

    edge_t = jnp.concatenate([zrecv[...], jnp.zeros((CZ - 16, CZ), F32)], axis=0).T

    def with_edges(field, low, high):
        field = jnp.where(at_z == CZ - 1, field + high * 0.5, field)
        return jnp.where(at_z == 0, field - low * 0.5, field)

    for x in range(CX):
        free = 1.0 - mask[x].astype(F32)
        total_0 = total[0, x]
        if x == 0:
            total_0 = total_0 - q_near[0] * 0.5
        if x == CX - 1:
            total_0 = total_0 + q_near[1] * 0.5
        lam0[x + 1] = free * total_0
        lam1[x, rows_of] = free * total[1, x]
        low, high = (edge_t[:, 8 * i + CX + x:8 * i + CX + x + 1] for i in range(2))
        lam2[x] = free * with_edges(total[2, x], low, high)

    start(lam_x)
    start(lam_y)
    for x in range(CX):
        turned = lam2[x].T
        lsend[x:x + 1] = turned[0:1]
        lsend[8 + x:9 + x] = turned[CZ - 1:CZ]
    start(lam_z)
    stores = [
        pltpu.make_async_copy(lam0.at[pl.ds(1, CX)], av_out.at[0], store_sem.at[0]),
        pltpu.make_async_copy(lam1.at[pl.ds(0, CX), rows_of], av_out.at[1], store_sem.at[1]),
        pltpu.make_async_copy(lam2, av_out.at[2], store_sem.at[2]),
    ]
    for copy in stores:
        copy.start()

    def slots_of(k, _):
        pltpu.make_async_copy(slots.at[k], slots.at[k], slot_recv.at[k]).wait()
        prepare(k)
        return 0

    rest = slots.at[pl.ds(1, NA - 1)]
    lax.fori_loop(1, NA, slots_of, 0)

    rest_vals = vals.at[pl.ds(1, NA - 1)]
    summed = None
    for low, high in zip(BATCHES[:-1], BATCHES[1:]):
        for k in range(max(low, 1), high):
            pltpu.make_async_copy(vals.at[k], vals.at[k], val_recv.at[k]).wait()
        split = [pieces(weight[k] * vals[k])[:2] for k in range(low, high)]
        scaled = jnp.concatenate(
            [jnp.concatenate([one[i] for one in split], axis=1) for i in range(2)], axis=0
        )
        product = lax.dot_general(
            hot[:, low * WALL:high * WALL], scaled, (((1,), (1,)), ((), ())), preferred_element_type=F32
        )
        summed = product if summed is None else summed + product
    summed = sum(summed[:, i * ANG:(i + 1) * ANG] for i in range(1, 2)) + summed[:, 0:ANG]
    packed = jnp.concatenate([summed[0:WIDTH // 2], summed[WIDTH // 2:WIDTH]], axis=1)
    dense[...] = packed.reshape(NB, OWN // 2, 2 * ANG)

    for k in LINE:
        other_zl, other_r, other_zh = line_place(k)
        pltpu.make_async_remote_copy(
            src_ref=dense.at[(other_zl * 2 + other_r) * ZH + other_zh], dst_ref=parts.at[k - 1],
            send_sem=part_send, recv_sem=part_recv, device_id=line_peer(k), device_id_type=MESH,
        ).start()

    for faces in (lam_x, lam_y, lam_z):
        arrive(faces)
    edge_l = jnp.concatenate([lrecv[...], jnp.zeros((CZ - 16, CZ), F32)], axis=0).T
    for x in range(CX):
        div = (
            (lam0[x + 2] - lam0[x]) * 0.5
            + (lam1[x, pl.ds(9, CY)] - lam1[x, pl.ds(7, CY)]) * 0.5
            + with_edges(along_z(lam2[x]), edge_l[:, x:x + 1], edge_l[:, 8 + x:9 + x])
        )
        apo[x] = ap[x] + 0.3 * div
    last = pltpu.make_async_copy(apo, ap_out, store_sem.at[3])
    last.start()

    pltpu.make_async_copy(parts, parts, part_recv).wait()
    own = dense[b] + jnp.sum(parts[...], axis=0)
    grad_out[...] = jnp.concatenate([own[:, 0:ANG], own[:, ANG:2 * ANG]], axis=0)

    for faces in (q_y, p_y, pq_z, lam_x, lam_y, lam_z):
        sent(faces)
    pl.when(wrap_up)(wrap["xu"].wait_send)
    pl.when(wrap_down)(wrap["xd"].wait_send)
    for faces in (ask, reply, q_x):
        pl.when(near_up)(faces["xu"].wait_send)
        pl.when(near_down)(faces["xd"].wait_send)
    pltpu.make_async_copy(rest, rest, slot_send).wait()
    pltpu.make_async_copy(rest_vals, rest_vals, val_send).wait()
    pltpu.make_async_copy(parts, parts, part_send).wait()
    for copy in stores + [last]:
        copy.wait()


def written(outs):
    anyspace = pl.BlockSpec(memory_space=pl.ANY)
    return pl.pallas_call(
        hand_over,
        out_shape=tuple(jax.ShapeDtypeStruct(o.shape, o.dtype) for o in outs),
        in_specs=[anyspace] * 3,
        out_specs=(anyspace,) * 3,
        scratch_shapes=[pltpu.SemaphoreType.DMA((3,))],
        compiler_params=pltpu.CompilerParams(vmem_limit_bytes=1024 * 1024),
    )(*outs)


def hand_over(adj_p, adj_v, grad, adj_p_out, adj_v_out, grad_out, sem):
    pairs = ((adj_v, adj_v_out), (adj_p, adj_p_out), (grad, grad_out))
    copies = [pltpu.make_async_copy(a, b, sem.at[i]) for i, (a, b) in enumerate(pairs)]
    for copy in copies:
        copy.start()
    for copy in copies:
        copy.wait()


def local(ns, nr, nc, *args):
    hbm = pl.BlockSpec(memory_space=pltpu.HBM)
    vmem = pl.BlockSpec(memory_space=pltpu.VMEM)
    block = (CX, CY, CZ)
    dma = pltpu.SemaphoreType.DMA
    return written(pl.pallas_call(
        functools.partial(kernel, ns, nr, nc),
        out_shape=(
            pltpu.VMEM(block, F32),
            pltpu.VMEM((3,) + block, F32),
            pltpu.VMEM((OWN, ANG), F32),
        ),
        in_specs=[hbm] * 12,
        out_specs=(pl.BlockSpec(memory_space=pl.ANY), pl.BlockSpec(memory_space=pl.ANY), vmem),
        scratch_shapes=[
            pltpu.VMEM((1, 1, 1, WALL), jnp.int32),
            pltpu.VMEM((1, 1, 1, WALL), jnp.int32),
            pltpu.VMEM((1, 1, 1, WALL), F32),
            pltpu.SMEM((1, 1, 1), jnp.int32),
            pltpu.SMEM((1,), jnp.int32),
            pltpu.VMEM((CX, CY + 16, CZ), F32),
            pltpu.VMEM((CX, CY + 16, CZ), F32),
            pltpu.VMEM(block, F32),
            pltpu.VMEM(block, F32),
            pltpu.VMEM(block, F32),
            pltpu.VMEM((3,) + block, F32),
            pltpu.VMEM((3,) + block, F32),
            pltpu.VMEM(block, jnp.int32),
            pltpu.VMEM((CX + 2, CY, CZ), F32),
            pltpu.VMEM((CX, CY + 16, CZ), F32),
            pltpu.VMEM(block, F32),
            pltpu.VMEM(block, F32),
            pltpu.VMEM((2, CY, CZ), F32),
            pltpu.VMEM((16, CY), F32),
            pltpu.VMEM((16, CY), F32),
            pltpu.VMEM((16, CY), F32),
            pltpu.VMEM((16, CY), F32),
            pltpu.VMEM((2, 2, CZ, CY), F32),
            pltpu.VMEM((2, CZ, CY), F32),
            pltpu.VMEM((2, 6 * CZ, CY), BF16),
            pltpu.VMEM((6 * CZ, CY), BF16),
            pltpu.VMEM((2, 6 * CZ, CY), BF16),
            pltpu.VMEM((3, 1, WALL), jnp.int32),
            pltpu.VMEM((2, 2, WALL), F32),
            pltpu.VMEM((2, 2, WALL), F32),
            pltpu.VMEM((4, CX * CY), F32),
            pltpu.VMEM((CY, WALL), BF16),
            pltpu.VMEM((NA, 2, WALL), F32),
            pltpu.VMEM((NA, 1, WALL), F32),
            pltpu.VMEM((WIDTH, NA * WALL), BF16),
            pltpu.VMEM((NA, ANG, WALL), F32),
            pltpu.VMEM((CX * CY, WALL), BF16),
            pltpu.VMEM((3 * CZ, CX * CY), BF16),
            pltpu.VMEM((NB, OWN // 2, 2 * ANG), F32),
            pltpu.VMEM((NB - 1, OWN // 2, 2 * ANG), F32),
            dma((5,)), dma((7,)), dma((4,)), dma((10,)), dma((10,)), dma((6,)), dma((6,)),
            dma((2,)), dma((2,)), dma((2,)), dma((2,)), dma((2,)), dma((2,)),
            dma, dma((NA,)), dma, dma((NA,)), dma, dma,
        ],
        compiler_params=pltpu.CompilerParams(
            collective_id=0, has_side_effects=True, vmem_limit_bytes=62 * 1024 * 1024 + 512 * 1024
        ),
        cost_estimate=pl.CostEstimate(flops=10**9, bytes_accessed=4 * 10**6, transcendentals=0),
    )(*args))


def solution(mesh):
    names = ("slab", "row", "col")
    sizes = tuple(mesh.shape[name] for name in names)
    cells = P(*names)
    vector = P(None, *names)
    slot = P(*names, None)
    in_specs = (cells, vector, cells, cells, cells, vector, cells, slot, slot, slot, cells, P())
    out_specs = (cells, vector, P(names, None))
    return jax.shard_map(
        functools.partial(local, *sizes), mesh=mesh, in_specs=in_specs, out_specs=out_specs, check_vma=False
    )
```

```python
import functools

import jax
import jax.numpy as jnp
from jax import lax
from jax.experimental import pallas as pl
from jax.experimental.pallas import tpu as pltpu
from jax.sharding import PartitionSpec as P

ANG = 64
CX = 4
CY = 128
CZ = 128
WALL = 512
OWN = 8
NXC = 4
NYC = 4
ZL = 4
ZH = 2
NA = NXC * NYC
NB = 2 * ZL * ZH
WIDTH = NB * OWN
LINE = sorted(range(1, 16), key=lambda k: (-(k & 1), abs((k >> 2) - 2), k))
MESH = pl.DeviceIdType.MESH


def hops(dy, dx):
    dy, dx = dy % NYC, dx % NXC
    return min(dy, NYC - dy) + min(dx, NXC - dx)


PLANE = sorted(
    ((dy, dx) for dy in range(NYC) for dx in range(NXC)),
    key=lambda d: (d != (0, 0), max(hops(d[0], d[1] + i) for i in (-1, 0, 1)), hops(*d), d),
)
BESIDE = [
    tuple(PLANE.index((dy, (dx + i) % NXC)) for i in (1, -1)) for dy, dx in PLANE
]
BATCHES = (0, 6, 13, 16)
F32 = jnp.float32
BF16 = jnp.bfloat16


def pieces(value):
    high = value.astype(BF16)
    rest = value - high.astype(F32)
    mid = rest.astype(BF16)
    low = (rest - mid.astype(F32)).astype(BF16)
    return high, mid, low


def kernel(
    ns, nr, nc,
    p_in, v_in, kap_in, drv_in, ap_in, av_in, mask_in, cells_in, rows_in, angle_in, count_in, step_in,
    ap_out, av_out, grad_out,
    cells_ref, rows_ref, angle_ref, count_ref, step_ref,
    pp, qq, kap, drv, ap, vel, total, mask,
    lam0, lam1, lam2, apo, q_near,
    zsend, zrecv, lsend, lrecv, z_far, l_far, asking, asked,
    turned_face, turned_wrap, face_parts, wrap_parts, slot_parts,
    cells_buf, answer, answered,
    ends, own_hot_y,
    slots, vals, hot, weight, where_hot, sens_t, dense, parts,
    small_sem, load_sem, store_sem, halo_send, halo_recv, lam_send, lam_recv,
    info_send, info_recv, wrap_send, wrap_recv, cell_send, cell_recv, answer_send, answer_recv,
    slot_send, slot_recv, val_send, val_recv, part_send, part_recv,
):
    s = lax.axis_index("slab")
    r = lax.axis_index("row")
    c = lax.axis_index("col")
    y, zl = s >> 2, s & (ZL - 1)
    x_at, zh = c >> 1, c & (ZH - 1)
    group = y * NXC + x_at
    b = (zl * 2 + r) * ZH + zh

    def plane_peer(k):
        dy, dx = PLANE[k]
        return (((y + dy) & (NYC - 1)) * ZL + zl, r, ((x_at + dx) & (NXC - 1)) * ZH + zh)

    def line_place(k):
        return (zl + (k >> 2)) & (ZL - 1), r ^ ((k >> 1) & 1), zh ^ (k & 1)

    def line_peer(k):
        other_zl, other_r, other_zh = line_place(k)
        return (y * ZL + other_zl, other_r, x_at * ZH + other_zh)

    plane = jnp.zeros((CY, CZ), F32)
    strip = jnp.zeros((8, CZ), F32)
    for ref in (pp, qq, lam1):
        for x in range(CX):
            ref[x, pl.ds(0, 8)] = strip
            ref[x, pl.ds(CY + 8, 8)] = strip
    for ref in (q_near, ):
        ref[0] = plane
        ref[1] = plane
    lam0[0] = plane
    lam0[CX + 1] = plane
    z_far[...] = jnp.zeros_like(z_far)
    l_far[...] = jnp.zeros_like(l_far)
    asked[...] = jnp.zeros_like(asked)
    answered[...] = jnp.zeros_like(answered)

    barrier = pltpu.get_barrier_semaphore()

    def greet(device):
        pl.semaphore_signal(barrier, inc=1, device_id=device, device_id_type=MESH)

    s_up, s_down = jnp.minimum(s + 1, ns - 1), jnp.maximum(s - 1, 0)
    r_up, r_down = jnp.minimum(r + 1, nr - 1), jnp.maximum(r - 1, 0)
    has = {
        "xu": s < ns - 1, "xd": s > 0, "yu": r < nr - 1, "yd": r > 0,
    }
    wrap_up = jnp.logical_and(zl == ZL - 1, has["xu"])
    wrap_down = jnp.logical_and(zl == 0, has["xd"])
    c_pair = c ^ 1
    aside = 1 - 2 * zh
    has_served = jnp.logical_and(x_at + aside >= 0, x_at + aside < NXC)
    has_server = jnp.logical_and(x_at - aside >= 0, x_at - aside < NXC)
    c_served = jnp.clip(x_at + aside, 0, NXC - 1) * ZH + zh
    c_server = jnp.clip(x_at - aside, 0, NXC - 1) * ZH + zh
    near_up = zl < ZL - 1
    near_down = zl > 0
    beyond = (
        (wrap_up, (s_up, r, c)),
        (wrap_down, (s_down, r, c)),
    )
    partners = NA - 1 + NB - 1
    for here, device in beyond:
        pl.when(here)(functools.partial(greet, device))
        partners = partners + here.astype(jnp.int32)
    for k in range(NA - 1, 0, -1):
        greet(plane_peer(k))
    for k in LINE:
        greet(line_peer(k))

    loads = [
        pltpu.make_async_copy(kap_in, kap, load_sem.at[0]),
        pltpu.make_async_copy(ap_in, ap, load_sem.at[1]),
        pltpu.make_async_copy(p_in, pp.at[pl.ds(0, CX), pl.ds(8, CY)], load_sem.at[2]),
        pltpu.make_async_copy(av_in, total, load_sem.at[3]),
        pltpu.make_async_copy(mask_in, mask, load_sem.at[4]),
        pltpu.make_async_copy(v_in, vel, load_sem.at[5]),
        pltpu.make_async_copy(drv_in, drv, load_sem.at[6]),
    ]
    small = [
        pltpu.make_async_copy(rows_in, rows_ref, small_sem.at[0]),
        pltpu.make_async_copy(angle_in, angle_ref, small_sem.at[1]),
        pltpu.make_async_copy(count_in, count_ref, small_sem.at[2]),
        pltpu.make_async_copy(cells_in, cells_ref, small_sem.at[3]),
        pltpu.make_async_copy(step_in, step_ref, small_sem.at[4]),
    ]
    for copy in small + loads:
        copy.start()

    lane = lax.broadcasted_iota(jnp.int32, (1, WALL), 1)
    for copy in small:
        copy.wait()
    own_rows = rows_ref[0, 0]
    live = lane < count_ref[0, 0, 0]
    bits = own_rows >> 3
    owner_group = ((bits >> 6) << 2) + ((bits >> 1) & 3)
    owner_line = (((bits >> 4) & 3) << 2) + (((bits >> 3) & 1) << 1) + (bits & 1)
    half = (own_rows >> 2) & 1
    code = owner_group * WIDTH + half * (WIDTH // 2) + owner_line * (OWN // 2) + (own_rows & (OWN // 2 - 1))
    slots[0, 0:1] = jnp.where(live, code.astype(F32), -1.0)
    slots[0, 1:2] = angle_ref[0, 0]
    row_at = (lax.broadcasted_iota(jnp.int32, (WIDTH, WALL), 0) + group * WIDTH).astype(F32)
    knots = lax.broadcasted_iota(jnp.int32, (ANG, WALL), 0).astype(F32)

    def at_slots(k):
        return pl.ds(pl.multiple_of(k * WALL, WALL), WALL)

    def prepare(k):
        hot[:, at_slots(k)] = jnp.where(slots[k, 0:1] == row_at, 1.0, 0.0).astype(BF16)
        dist = jnp.abs(slots[k, 1:2] - knots)
        dist = jnp.minimum(dist, ANG - dist)
        outer = jnp.maximum(2.0 - dist, 0.0)
        near = jnp.maximum(1.0 - dist, 0.0)
        weight[k] = (outer * outer * outer - 4.0 * near * near * near) * (1.0 / 6.0)


    own_cells = cells_ref[0, 0]
    cells_buf[0] = own_cells
    own_xy = own_cells >> 7
    own_x = own_cells >> 14
    own_z = own_cells & (CZ - 1)

    loads[0].wait()
    loads[1].wait()
    rows_of = pl.ds(8, CY)
    for x in range(CX):
        qq[x, rows_of] = kap[x] * ap[x]
    loads[2].wait()
    for i, (ref, at) in enumerate(((pp, 0), (qq, CX))):
        for x in range(CX):
            turned = ref[x, rows_of].T
            zsend[at + x:at + x + 1] = turned[0:1]
            zsend[8 + at + x:8 + at + x + 1] = turned[CZ - 1:CZ]
            if x in (0, CX - 1):
                turned_face[x // (CX - 1), i] = turned

    picks = 2

    def split_into(ref, first, second):
        for i, field in enumerate((first, second)):
            for j, piece in enumerate(pieces(field)[:picks]):
                ref[(picks * i + j) * CZ:(picks * i + j + 1) * CZ] = piece

    def pick(ref, hot_y, at_z):
        got = jnp.dot(ref[0:2 * picks * CZ], hot_y, preferred_element_type=F32)
        out = []
        for i in range(2):
            field = got[picks * i * CZ:(picks * i + 1) * CZ]
            for j in range(1, picks):
                field = field + got[(picks * i + j) * CZ:(picks * i + j + 1) * CZ]
            out.append(jnp.sum(jnp.where(y_at == at_z, field, 0.0), axis=0, keepdims=True))
        return out

    def hot_y_of(cells):
        return jnp.where(y_at == ((cells >> 7) & (CY - 1)), 1.0, 0.0).astype(BF16)


    pl.semaphore_wait(barrier, partners)

    def slot_copy(k):
        return pltpu.make_async_remote_copy(
            src_ref=slots.at[0], dst_ref=slots.at[k],
            send_sem=slot_send, recv_sem=slot_recv.at[k],
            device_id=plane_peer(k), device_id_type=MESH,
        )

    def halo(src, dst, sem_at, send_sem, recv_sem, device):
        return pltpu.make_async_remote_copy(
            src_ref=src, dst_ref=dst, send_sem=send_sem.at[sem_at], recv_sem=recv_sem.at[sem_at],
            device_id=device, device_id_type=MESH,
        )


    inner = pl.ds(0, CX)
    q_x = {
        "xu": halo(qq.at[CX - 1, rows_of], q_near.at[0], 0, halo_send, halo_recv, (s_up, r, c)),
        "xd": halo(qq.at[0, rows_of], q_near.at[1], 1, halo_send, halo_recv, (s_down, r, c)),
    }

    def field_y(ref, base):
        return {
            "yu": halo(ref.at[inner, pl.ds(CY, 8)], ref.at[inner, pl.ds(0, 8)], base, halo_send, halo_recv, (s, r_up, c)),
            "yd": halo(ref.at[inner, pl.ds(8, 8)], ref.at[inner, pl.ds(CY + 8, 8)], base + 1, halo_send, halo_recv, (s, r_down, c)),
        }

    q_y = field_y(qq, 4)
    p_y = field_y(pp, 6)
    wrap = {
        "xu": halo(turned_face.at[1], turned_wrap, 0, wrap_send, wrap_recv, (s_up, r, c)),
        "xd": halo(turned_face.at[0], turned_wrap, 1, wrap_send, wrap_recv, (s_down, r, c)),
    }
    ask = {
        "xu": halo(cells_buf.at[0], cells_buf.at[1], 0, cell_send, cell_recv, (s_up, r, c)),
        "xd": halo(cells_buf.at[0], cells_buf.at[2], 1, cell_send, cell_recv, (s_down, r, c)),
    }
    reply = {
        "xu": halo(answer.at[1], answered.at[0], 0, answer_send, answer_recv, (s_up, r, c)),
        "xd": halo(answer.at[0], answered.at[1], 1, answer_send, answer_recv, (s_down, r, c)),
    }
    pq_z = halo(zsend, zrecv, 8, halo_send, halo_recv, (s, r, c_pair))
    lam_z = halo(lsend, lrecv, 4, lam_send, lam_recv, (s, r, c_pair))
    info = halo(asking, asked, 0, info_send, info_recv, (s, r, c_server))

    def onward(src, dst, at):
        return [halo(src.at[pl.ds(8 * (1 - h), 8)], dst, at, info_send, info_recv, (s, r, c_served)) for h in range(ZH)]

    z_on = onward(zrecv, z_far, 1)
    l_on = onward(lrecv, l_far, 2)

    def start_on(copies):
        for h in range(ZH):
            pl.when(jnp.logical_and(has_served, zh == h))(copies[h].start)

    lam_x = {
        "xu": halo(lam0.at[CX], lam0.at[0], 0, lam_send, lam_recv, (s_up, r, c)),
        "xd": halo(lam0.at[1], lam0.at[CX + 1], 1, lam_send, lam_recv, (s_down, r, c)),
    }
    lam_y = {
        "yu": halo(lam1.at[inner, pl.ds(CY, 8)], lam1.at[inner, pl.ds(0, 8)], 2, lam_send, lam_recv, (s, r_up, c)),
        "yd": halo(lam1.at[inner, pl.ds(8, 8)], lam1.at[inner, pl.ds(CY + 8, 8)], 3, lam_send, lam_recv, (s, r_down, c)),
    }

    def start(faces):
        for side, copy in faces.items():
            pl.when(has[side])(copy.start)

    opposite = {"xu": "xd", "xd": "xu", "yu": "yd", "yd": "yu"}

    def arrive(faces):
        for side, copy in faces.items():
            pl.when(has[opposite[side]])(copy.wait_recv)

    def sent(faces):
        for side, copy in faces.items():
            pl.when(has[side])(copy.wait_send)

    pq_z.start()
    start(q_y)
    start(p_y)
    pl.when(near_up)(ask["xu"].start)
    pl.when(near_down)(ask["xd"].start)
    pl.when(wrap_up)(wrap["xu"].start)
    pl.when(wrap_down)(wrap["xd"].start)
    for k in range(NA - 1, 0, -1):
        slot_copy(k).start()

    y_at = lax.broadcasted_iota(jnp.int32, (CY, WALL), 0)
    for x in range(CX):
        where_hot[x * CY:(x + 1) * CY] = jnp.where(y_at + x * CY == own_xy, 1.0, 0.0).astype(BF16)
    own_hot_y[...] = hot_y_of(own_cells)
    for side in range(2):
        split_into(face_parts.at[side], turned_face[side, 0], turned_face[side, 1])
    prepare(0)

    phase = jnp.cos(0.5 * jnp.full((1, CZ), lax.rem(step_ref[0], 97).astype(F32), F32))
    for copy in loads[3:]:
        copy.wait()
    at_z = lax.broadcasted_iota(jnp.int32, (CY, CZ), 1)

    def along_z(field):
        upper = jnp.where(at_z == CZ - 1, 0.0, pltpu.roll(field, CZ - 1, 1))
        lower = jnp.where(at_z == 0, 0.0, pltpu.roll(field, 1, 1))
        return (upper - lower) * 0.5

    for x in range(CX):
        here = slice(x * CY, (x + 1) * CY)
        total_2 = total[2, x] + along_z(qq[x, rows_of])
        moved_2 = vel[2, x] - 0.3 * along_z(pp[x, rows_of])
        total[2, x] = total_2
        apo[x] = total_2 * moved_2
        for i, field in enumerate((total_2.T, moved_2.T)):
            ends[i:i + 1, here] = field[0:1]
            ends[2 + i:3 + i, here] = field[CZ - 1:CZ]
    edge_parts = jnp.concatenate(pieces(ends[...]), axis=0)
    edge = jnp.dot(edge_parts, where_hot[...], preferred_element_type=F32)
    edge = edge[0:4] + edge[4:8] + edge[8:12]
    far_edge = jnp.where(zh == 0, edge[0:2], edge[2:4])
    near_edge = jnp.where(zh == 0, edge[2:4], edge[0:2])
    asking[0:2] = far_edge
    asking[2:3] = own_cells.astype(F32)
    asking[3:4] = own_cells.astype(F32)
    pl.when(has_server)(info.start)

    arrive(q_y)
    arrive(p_y)

    def along_x(ref, x):
        if x == 0:
            return ref[1, rows_of] * 0.5
        if x == CX - 1:
            return ref[CX - 2, rows_of] * -0.5
        return (ref[x + 1, rows_of] - ref[x - 1, rows_of]) * 0.5

    def along_y(ref, x):
        return (ref[x, pl.ds(9, CY)] - ref[x, pl.ds(7, CY)]) * 0.5

    for x in range(CX):
        here = slice(x * CY, (x + 1) * CY)
        total_0 = total[0, x] + along_x(qq, x)
        total_1 = total[1, x] + along_y(qq, x)
        total[0, x] = total_0
        total[1, x] = total_1
        moved_0 = vel[0, x] - 0.3 * along_x(pp, x) + drv[x] * phase
        sens = -(total_0 * moved_0 + total_1 * (vel[1, x] - 0.3 * along_y(pp, x)) + apo[x])
        for i, piece in enumerate(pieces(sens.T)):
            sens_t[i * CZ:(i + 1) * CZ, here] = piece
        if x in (0, CX - 1):
            split_into(slot_parts.at[x // (CX - 1)], total_0.T, moved_0.T)

    def serve(side, at):
        cells = cells_buf[at]
        p_at, q_at = pick(face_parts.at[side], hot_y_of(cells), cells & (CZ - 1))
        answer[side, 0:1] = p_at
        answer[side, 1:2] = q_at

    @pl.when(near_up)
    def _():
        ask["xd"].wait_recv()
        serve(1, 2)
        reply["xu"].start()

    @pl.when(near_down)
    def _():
        ask["xu"].wait_recv()
        serve(0, 1)
        reply["xd"].start()

    pl.when(near_up)(q_x["xu"].start)
    pl.when(near_down)(q_x["xd"].start)

    on_face = [
        pick(slot_parts.at[side], where_hot[side * (CX - 1) * CY:(side * (CX - 1) + 1) * CY], own_z)
        for side in range(2)
    ]

    picked = jnp.dot(sens_t[...], where_hot[...], preferred_element_type=F32)
    picked = picked[0:CZ] + picked[CZ:2 * CZ] + picked[2 * CZ:3 * CZ]
    picked = jnp.sum(jnp.where(y_at == own_z, picked, 0.0), axis=0, keepdims=True)

    def correction(sign, here, total_at, moved_at, p_at, q_at):
        more_total = jnp.where(here, q_at, 0.0) * (0.5 * sign)
        more_moved = jnp.where(here, p_at, 0.0) * (-0.15 * sign)
        return -(more_total * (moved_at + more_moved) + total_at * more_moved)

    row_x = lax.broadcasted_iota(jnp.int32, (8, WALL), 0) & (CX - 1)

    def face_at(rows, hot_y, at_x):
        got = jnp.dot(jnp.concatenate(pieces(rows), axis=0), hot_y, preferred_element_type=F32)
        got = jnp.where(row_x == at_x, got[0:8] + got[8:16] + got[16:24], 0.0)
        return jnp.sum(got[0:4], axis=0, keepdims=True), jnp.sum(got[4:8], axis=0, keepdims=True)

    pl.when(has_served)(info.wait_recv)
    served_cells = asked[2:3].astype(jnp.int32)
    served_hot = hot_y_of(served_cells)
    pq_z.wait_recv()
    start_on(z_on)
    near_face = jnp.where(zh == 0, zrecv[0:8], zrecv[8:16])
    far_face = jnp.where(zh == 0, zrecv[8:16], zrecv[0:8])
    sign = aside.astype(F32)
    near_end = (CZ - 1) * (1 - zh)
    far_end = (CZ - 1) * zh
    p_at, q_at = face_at(near_face, own_hot_y[...], own_x)
    picked = picked + correction(sign, own_z == near_end, near_edge[0:1], near_edge[1:2], p_at, q_at)
    p_at, q_at = face_at(far_face, served_hot, served_cells >> 14)
    on_edge = jnp.logical_and((served_cells & (CZ - 1)) == far_end, has_served)
    vals[0, 1:2] = jnp.where(
        on_edge, correction(-sign, on_edge, asked[0:1], asked[1:2], p_at, q_at), 0.0
    )

    pl.when(near_down)(reply["xu"].wait_recv)
    pl.when(near_up)(reply["xd"].wait_recv)

    def own_answer(side):
        split_into(wrap_parts, turned_wrap[0], turned_wrap[1])
        p_at, q_at = pick(wrap_parts, own_hot_y[...], cells_buf[0] & (CZ - 1))
        answered[side, 0:1] = p_at
        answered[side, 1:2] = q_at

    @pl.when(wrap_down)
    def _():
        wrap["xu"].wait_recv()
        own_answer(0)

    @pl.when(wrap_up)
    def _():
        wrap["xd"].wait_recv()
        own_answer(1)

    for side, (total_at, moved_at) in enumerate(on_face):
        here = own_x == side * (CX - 1)
        picked = picked + correction(2.0 * side - 1.0, here, total_at, moved_at, answered[side, 0:1], answered[side, 1:2])
    vals[0, 0:1] = picked

    for k in range(NA - 1, 0, -1):
        pltpu.make_async_remote_copy(
            src_ref=vals.at[0], dst_ref=vals.at[k], send_sem=val_send, recv_sem=val_recv.at[k],
            device_id=plane_peer(k), device_id_type=MESH,
        ).start()

    pl.when(near_down)(q_x["xu"].wait_recv)
    pl.when(near_up)(q_x["xd"].wait_recv)

    @pl.when(wrap_down)
    def _():
        q_near[0] = turned_wrap[1].T

    @pl.when(wrap_up)
    def _():
        q_near[1] = turned_wrap[1].T

    def both_edges(pair, far):
        lower = jnp.where(zh == 0, far[...], pair[8:16])
        upper = jnp.where(zh == 0, pair[0:8], far[...])
        return jnp.concatenate([lower, upper, jnp.zeros((CZ - 16, CZ), F32)], axis=0).T

    pl.when(has_server)(z_on[0].wait_recv)
    edge_t = both_edges(zrecv, z_far)

    def with_edges(field, low, high):
        field = jnp.where(at_z == CZ - 1, field + high * 0.5, field)
        return jnp.where(at_z == 0, field - low * 0.5, field)

    for x in range(CX):
        free = 1.0 - mask[x].astype(F32)
        total_0 = total[0, x]
        if x == 0:
            total_0 = total_0 - q_near[0] * 0.5
        if x == CX - 1:
            total_0 = total_0 + q_near[1] * 0.5
        lam0[x + 1] = free * total_0
        lam1[x, rows_of] = free * total[1, x]
        low, high = (edge_t[:, 8 * i + CX + x:8 * i + CX + x + 1] for i in range(2))
        lam2[x] = free * with_edges(total[2, x], low, high)

    start(lam_x)
    start(lam_y)
    for x in range(CX):
        turned = lam2[x].T
        lsend[x:x + 1] = turned[0:1]
        lsend[8 + x:9 + x] = turned[CZ - 1:CZ]
    lam_z.start()
    stores = [
        pltpu.make_async_copy(lam0.at[pl.ds(1, CX)], av_out.at[0], store_sem.at[0]),
        pltpu.make_async_copy(lam1.at[pl.ds(0, CX), rows_of], av_out.at[1], store_sem.at[1]),
        pltpu.make_async_copy(lam2, av_out.at[2], store_sem.at[2]),
    ]
    for copy in stores:
        copy.start()

    def slots_of(k, _):
        pltpu.make_async_copy(slots.at[k], slots.at[k], slot_recv.at[k]).wait()
        prepare(k)
        return 0

    rest = slots.at[pl.ds(1, NA - 1)]
    lax.fori_loop(1, NA, slots_of, 0)

    rest_vals = vals.at[pl.ds(1, NA - 1)]
    summed = None
    seen = {0}
    for low, high in zip(BATCHES[:-1], BATCHES[1:]):
        for k in sorted({k for j in range(low, high) for k in (j,) + BESIDE[j]} - seen):
            pltpu.make_async_copy(vals.at[k], vals.at[k], val_recv.at[k]).wait()
            seen.add(k)
        value = [
            vals[k, 0:1] + jnp.where(zh == 0, vals[BESIDE[k][0], 1:2], vals[BESIDE[k][1], 1:2])
            for k in range(low, high)
        ]
        split = [pieces(weight[k] * value[k - low])[:2] for k in range(low, high)]
        scaled = jnp.concatenate(
            [jnp.concatenate([one[i] for one in split], axis=1) for i in range(2)], axis=0
        )
        product = lax.dot_general(
            hot[:, low * WALL:high * WALL], scaled, (((1,), (1,)), ((), ())), preferred_element_type=F32
        )
        summed = product if summed is None else summed + product
    summed = sum(summed[:, i * ANG:(i + 1) * ANG] for i in range(1, 2)) + summed[:, 0:ANG]
    packed = jnp.concatenate([summed[0:WIDTH // 2], summed[WIDTH // 2:WIDTH]], axis=1)
    dense[...] = packed.reshape(NB, OWN // 2, 2 * ANG)

    for k in LINE:
        other_zl, other_r, other_zh = line_place(k)
        pltpu.make_async_remote_copy(
            src_ref=dense.at[(other_zl * 2 + other_r) * ZH + other_zh], dst_ref=parts.at[k - 1],
            send_sem=part_send, recv_sem=part_recv, device_id=line_peer(k), device_id_type=MESH,
        ).start()

    lam_z.wait_recv()
    start_on(l_on)
    arrive(lam_x)
    arrive(lam_y)
    pl.when(has_server)(l_on[0].wait_recv)
    edge_l = both_edges(lrecv, l_far)
    for x in range(CX):
        div = (
            (lam0[x + 2] - lam0[x]) * 0.5
            + (lam1[x, pl.ds(9, CY)] - lam1[x, pl.ds(7, CY)]) * 0.5
            + with_edges(along_z(lam2[x]), edge_l[:, x:x + 1], edge_l[:, 8 + x:9 + x])
        )
        apo[x] = ap[x] + 0.3 * div
    last = pltpu.make_async_copy(apo, ap_out, store_sem.at[3])
    last.start()

    pltpu.make_async_copy(parts, parts, part_recv).wait()
    own = dense[b] + jnp.sum(parts[...], axis=0)
    grad_out[...] = jnp.concatenate([own[:, 0:ANG], own[:, ANG:2 * ANG]], axis=0)

    for faces in (q_y, p_y, lam_x, lam_y):
        sent(faces)
    pq_z.wait_send()
    lam_z.wait_send()
    pl.when(has_server)(info.wait_send)
    pl.when(has_served)(z_on[0].wait_send)
    pl.when(has_served)(l_on[0].wait_send)
    pl.when(wrap_up)(wrap["xu"].wait_send)
    pl.when(wrap_down)(wrap["xd"].wait_send)
    for faces in (ask, reply, q_x):
        pl.when(near_up)(faces["xu"].wait_send)
        pl.when(near_down)(faces["xd"].wait_send)
    pltpu.make_async_copy(rest, rest, slot_send).wait()
    pltpu.make_async_copy(rest_vals, rest_vals, val_send).wait()
    pltpu.make_async_copy(parts, parts, part_send).wait()
    for copy in stores + [last]:
        copy.wait()


def written(outs):
    anyspace = pl.BlockSpec(memory_space=pl.ANY)
    return pl.pallas_call(
        hand_over,
        out_shape=tuple(jax.ShapeDtypeStruct(o.shape, o.dtype) for o in outs),
        in_specs=[anyspace] * 3,
        out_specs=(anyspace,) * 3,
        scratch_shapes=[pltpu.SemaphoreType.DMA((3,))],
        compiler_params=pltpu.CompilerParams(vmem_limit_bytes=1024 * 1024),
    )(*outs)


def hand_over(adj_p, adj_v, grad, adj_p_out, adj_v_out, grad_out, sem):
    pairs = ((adj_v, adj_v_out), (adj_p, adj_p_out), (grad, grad_out))
    copies = [pltpu.make_async_copy(a, b, sem.at[i]) for i, (a, b) in enumerate(pairs)]
    for copy in copies:
        copy.start()
    for copy in copies:
        copy.wait()


def local(ns, nr, nc, *args):
    hbm = pl.BlockSpec(memory_space=pltpu.HBM)
    vmem = pl.BlockSpec(memory_space=pltpu.VMEM)
    block = (CX, CY, CZ)
    dma = pltpu.SemaphoreType.DMA
    return written(pl.pallas_call(
        functools.partial(kernel, ns, nr, nc),
        out_shape=(
            pltpu.VMEM(block, F32),
            pltpu.VMEM((3,) + block, F32),
            pltpu.VMEM((OWN, ANG), F32),
        ),
        in_specs=[hbm] * 12,
        out_specs=(pl.BlockSpec(memory_space=pl.ANY), pl.BlockSpec(memory_space=pl.ANY), vmem),
        scratch_shapes=[
            pltpu.VMEM((1, 1, 1, WALL), jnp.int32),
            pltpu.VMEM((1, 1, 1, WALL), jnp.int32),
            pltpu.VMEM((1, 1, 1, WALL), F32),
            pltpu.SMEM((1, 1, 1), jnp.int32),
            pltpu.SMEM((1,), jnp.int32),
            pltpu.VMEM((CX, CY + 16, CZ), F32),
            pltpu.VMEM((CX, CY + 16, CZ), F32),
            pltpu.VMEM(block, F32),
            pltpu.VMEM(block, F32),
            pltpu.VMEM(block, F32),
            pltpu.VMEM((3,) + block, F32),
            pltpu.VMEM((3,) + block, F32),
            pltpu.VMEM(block, jnp.int32),
            pltpu.VMEM((CX + 2, CY, CZ), F32),
            pltpu.VMEM((CX, CY + 16, CZ), F32),
            pltpu.VMEM(block, F32),
            pltpu.VMEM(block, F32),
            pltpu.VMEM((2, CY, CZ), F32),
            pltpu.VMEM((16, CY), F32),
            pltpu.VMEM((16, CY), F32),
            pltpu.VMEM((16, CY), F32),
            pltpu.VMEM((16, CY), F32),
            pltpu.VMEM((8, CY), F32),
            pltpu.VMEM((8, CY), F32),
            pltpu.VMEM((4, WALL), F32),
            pltpu.VMEM((4, WALL), F32),
            pltpu.VMEM((2, 2, CZ, CY), F32),
            pltpu.VMEM((2, CZ, CY), F32),
            pltpu.VMEM((2, 6 * CZ, CY), BF16),
            pltpu.VMEM((6 * CZ, CY), BF16),
            pltpu.VMEM((2, 6 * CZ, CY), BF16),
            pltpu.VMEM((3, 1, WALL), jnp.int32),
            pltpu.VMEM((2, 2, WALL), F32),
            pltpu.VMEM((2, 2, WALL), F32),
            pltpu.VMEM((4, CX * CY), F32),
            pltpu.VMEM((CY, WALL), BF16),
            pltpu.VMEM((NA, 2, WALL), F32),
            pltpu.VMEM((NA, 2, WALL), F32),
            pltpu.VMEM((WIDTH, NA * WALL), BF16),
            pltpu.VMEM((NA, ANG, WALL), F32),
            pltpu.VMEM((CX * CY, WALL), BF16),
            pltpu.VMEM((3 * CZ, CX * CY), BF16),
            pltpu.VMEM((NB, OWN // 2, 2 * ANG), F32),
            pltpu.VMEM((NB - 1, OWN // 2, 2 * ANG), F32),
            dma((5,)), dma((7,)), dma((4,)), dma((10,)), dma((10,)), dma((6,)), dma((6,)), dma((3,)), dma((3,)),
            dma((2,)), dma((2,)), dma((2,)), dma((2,)), dma((2,)), dma((2,)),
            dma, dma((NA,)), dma, dma((NA,)), dma, dma,
        ],
        compiler_params=pltpu.CompilerParams(
            collective_id=0, has_side_effects=True, vmem_limit_bytes=62 * 1024 * 1024 + 512 * 1024
        ),
        cost_estimate=pl.CostEstimate(flops=10**9, bytes_accessed=4 * 10**6, transcendentals=0),
    )(*args))


def solution(mesh):
    names = ("slab", "row", "col")
    sizes = tuple(mesh.shape[name] for name in names)
    cells = P(*names)
    vector = P(None, *names)
    slot = P(*names, None)
    in_specs = (cells, vector, cells, cells, cells, vector, cells, slot, slot, slot, cells, P())
    out_specs = (cells, vector, P(names, None))
    return jax.shard_map(
        functools.partial(local, *sizes), mesh=mesh, in_specs=in_specs, out_specs=out_specs, check_vma=False
    )
```

```python
import functools

import jax
import jax.numpy as jnp
from jax import lax
from jax.experimental import pallas as pl
from jax.experimental.pallas import tpu as pltpu
from jax.sharding import PartitionSpec as P

ANG = 64
CX = 4
CY = 128
CZ = 128
WALL = 512
OWN = 8
NXC = 4
NYC = 4
ZL = 4
ZH = 2
NA = NXC * NYC
NB = 2 * ZL * ZH
WIDTH = NB * OWN
BATCHES = (0, 5, 11, 16)
LINE = sorted(range(1, 16), key=lambda k: (-(k & 1), abs((k >> 2) - 2), k))
MESH = pl.DeviceIdType.MESH
PLANE = sorted(
    ((dy, dx) for dy in range(NYC) for dx in range(NXC)),
    key=lambda d: (min(d[0], NYC - d[0]) + min(d[1], NXC - d[1]), d),
)
F32 = jnp.float32
BF16 = jnp.bfloat16


def pieces(value):
    high = value.astype(BF16)
    rest = value - high.astype(F32)
    mid = rest.astype(BF16)
    low = (rest - mid.astype(F32)).astype(BF16)
    return high, mid, low


def kernel(
    ns, nr, nc,
    p_in, v_in, kap_in, drv_in, ap_in, av_in, mask_in, cells_in, rows_in, angle_in, count_in, step_in,
    ap_out, av_out, grad_out,
    cells_ref, rows_ref, angle_ref, count_ref, step_ref,
    pp, qq, kap, drv, ap, vel, total, mask,
    lam0, lam1, lam2, apo, q_near,
    zsend, zrecv, lsend, lrecv,
    turned_face, turned_wrap, face_parts, wrap_parts, slot_parts,
    cells_buf, answer, answered,
    ends, own_hot_y,
    slots, vals, hot, weight, where_hot, sens_t, dense, parts,
    small_sem, load_sem, store_sem, halo_send, halo_recv, lam_send, lam_recv,
    wrap_send, wrap_recv, cell_send, cell_recv, answer_send, answer_recv,
    slot_send, slot_recv, val_send, val_recv, part_send, part_recv,
):
    s = lax.axis_index("slab")
    r = lax.axis_index("row")
    c = lax.axis_index("col")
    y, zl = s >> 2, s & (ZL - 1)
    x_at, zh = c >> 1, c & (ZH - 1)
    group = y * NXC + x_at
    b = (zl * 2 + r) * ZH + zh

    def plane_peer(k):
        dy, dx = PLANE[k]
        return (((y + dy) & (NYC - 1)) * ZL + zl, r, ((x_at + dx) & (NXC - 1)) * ZH + zh)

    def line_place(k):
        return (zl + (k >> 2)) & (ZL - 1), r ^ ((k >> 1) & 1), zh ^ (k & 1)

    def line_peer(k):
        other_zl, other_r, other_zh = line_place(k)
        return (y * ZL + other_zl, other_r, x_at * ZH + other_zh)

    plane = jnp.zeros((CY, CZ), F32)
    strip = jnp.zeros((8, CZ), F32)
    for ref in (pp, qq, lam1):
        for x in range(CX):
            ref[x, pl.ds(0, 8)] = strip
            ref[x, pl.ds(CY + 8, 8)] = strip
    for ref in (q_near, ):
        ref[0] = plane
        ref[1] = plane
    lam0[0] = plane
    lam0[CX + 1] = plane
    zrecv[...] = jnp.zeros_like(zrecv)
    lrecv[...] = jnp.zeros_like(lrecv)
    answered[...] = jnp.zeros_like(answered)

    barrier = pltpu.get_barrier_semaphore()

    def greet(device):
        pl.semaphore_signal(barrier, inc=1, device_id=device, device_id_type=MESH)

    s_up, s_down = jnp.minimum(s + 1, ns - 1), jnp.maximum(s - 1, 0)
    r_up, r_down = jnp.minimum(r + 1, nr - 1), jnp.maximum(r - 1, 0)
    c_up, c_down = jnp.minimum(c + 1, nc - 1), jnp.maximum(c - 1, 0)
    has = {
        "xu": s < ns - 1, "xd": s > 0, "yu": r < nr - 1, "yd": r > 0, "zu": c < nc - 1, "zd": c > 0,
    }
    wrap_up = jnp.logical_and(zl == ZL - 1, has["xu"])
    wrap_down = jnp.logical_and(zl == 0, has["xd"])
    near_up = zl < ZL - 1
    near_down = zl > 0
    beyond = (
        (jnp.logical_and(zh == ZH - 1, has["zu"]), (s, r, c_up)),
        (jnp.logical_and(zh == 0, has["zd"]), (s, r, c_down)),
        (wrap_up, (s_up, r, c)),
        (wrap_down, (s_down, r, c)),
    )
    partners = NA - 1 + NB - 1
    for here, device in beyond:
        pl.when(here)(functools.partial(greet, device))
        partners = partners + here.astype(jnp.int32)
    for k in range(NA - 1, 0, -1):
        greet(plane_peer(k))
    for k in LINE:
        greet(line_peer(k))

    loads = [
        pltpu.make_async_copy(kap_in, kap, load_sem.at[0]),
        pltpu.make_async_copy(ap_in, ap, load_sem.at[1]),
        pltpu.make_async_copy(p_in, pp.at[pl.ds(0, CX), pl.ds(8, CY)], load_sem.at[2]),
        pltpu.make_async_copy(av_in, total, load_sem.at[3]),
        pltpu.make_async_copy(mask_in, mask, load_sem.at[4]),
        pltpu.make_async_copy(v_in, vel, load_sem.at[5]),
        pltpu.make_async_copy(drv_in, drv, load_sem.at[6]),
    ]
    small = [
        pltpu.make_async_copy(rows_in, rows_ref, small_sem.at[0]),
        pltpu.make_async_copy(angle_in, angle_ref, small_sem.at[1]),
        pltpu.make_async_copy(count_in, count_ref, small_sem.at[2]),
        pltpu.make_async_copy(cells_in, cells_ref, small_sem.at[3]),
        pltpu.make_async_copy(step_in, step_ref, small_sem.at[4]),
    ]
    for copy in small + loads:
        copy.start()

    lane = lax.broadcasted_iota(jnp.int32, (1, WALL), 1)
    for copy in small:
        copy.wait()
    own_rows = rows_ref[0, 0]
    live = lane < count_ref[0, 0, 0]
    bits = own_rows >> 3
    owner_group = ((bits >> 6) << 2) + ((bits >> 1) & 3)
    owner_line = (((bits >> 4) & 3) << 2) + (((bits >> 3) & 1) << 1) + (bits & 1)
    half = (own_rows >> 2) & 1
    code = owner_group * WIDTH + half * (WIDTH // 2) + owner_line * (OWN // 2) + (own_rows & (OWN // 2 - 1))
    slots[0, 0:1] = jnp.where(live, code.astype(F32), -1.0)
    slots[0, 1:2] = angle_ref[0, 0]
    row_at = (lax.broadcasted_iota(jnp.int32, (WIDTH, WALL), 0) + group * WIDTH).astype(F32)
    knots = lax.broadcasted_iota(jnp.int32, (ANG, WALL), 0).astype(F32)

    def at_slots(k):
        return pl.ds(pl.multiple_of(k * WALL, WALL), WALL)

    def prepare(k):
        hot[:, at_slots(k)] = jnp.where(slots[k, 0:1] == row_at, 1.0, 0.0).astype(BF16)
        dist = jnp.abs(slots[k, 1:2] - knots)
        dist = jnp.minimum(dist, ANG - dist)
        outer = jnp.maximum(2.0 - dist, 0.0)
        near = jnp.maximum(1.0 - dist, 0.0)
        weight[k] = (outer * outer * outer - 4.0 * near * near * near) * (1.0 / 6.0)


    own_cells = cells_ref[0, 0]
    cells_buf[0] = own_cells
    own_xy = own_cells >> 7
    own_x = own_cells >> 14
    own_z = own_cells & (CZ - 1)

    loads[0].wait()
    loads[1].wait()
    rows_of = pl.ds(8, CY)
    for x in range(CX):
        qq[x, rows_of] = kap[x] * ap[x]
    loads[2].wait()
    for i, (ref, at) in enumerate(((pp, 0), (qq, CX))):
        for x in range(CX):
            turned = ref[x, rows_of].T
            zsend[at + x:at + x + 1] = turned[0:1]
            zsend[8 + at + x:8 + at + x + 1] = turned[CZ - 1:CZ]
            if x in (0, CX - 1):
                turned_face[x // (CX - 1), i] = turned

    picks = 2

    def split_into(ref, first, second):
        for i, field in enumerate((first, second)):
            for j, piece in enumerate(pieces(field)[:picks]):
                ref[(picks * i + j) * CZ:(picks * i + j + 1) * CZ] = piece

    def pick(ref, hot_y, at_z):
        got = jnp.dot(ref[0:2 * picks * CZ], hot_y, preferred_element_type=F32)
        out = []
        for i in range(2):
            field = got[picks * i * CZ:(picks * i + 1) * CZ]
            for j in range(1, picks):
                field = field + got[(picks * i + j) * CZ:(picks * i + j + 1) * CZ]
            out.append(jnp.sum(jnp.where(y_at == at_z, field, 0.0), axis=0, keepdims=True))
        return out

    def hot_y_of(cells):
        return jnp.where(y_at == ((cells >> 7) & (CY - 1)), 1.0, 0.0).astype(BF16)


    pl.semaphore_wait(barrier, partners)

    def slot_copy(k):
        return pltpu.make_async_remote_copy(
            src_ref=slots.at[0], dst_ref=slots.at[k],
            send_sem=slot_send, recv_sem=slot_recv.at[k],
            device_id=plane_peer(k), device_id_type=MESH,
        )

    def halo(src, dst, sem_at, send_sem, recv_sem, device):
        return pltpu.make_async_remote_copy(
            src_ref=src, dst_ref=dst, send_sem=send_sem.at[sem_at], recv_sem=recv_sem.at[sem_at],
            device_id=device, device_id_type=MESH,
        )


    inner = pl.ds(0, CX)
    q_x = {
        "xu": halo(qq.at[CX - 1, rows_of], q_near.at[0], 0, halo_send, halo_recv, (s_up, r, c)),
        "xd": halo(qq.at[0, rows_of], q_near.at[1], 1, halo_send, halo_recv, (s_down, r, c)),
    }

    def field_y(ref, base):
        return {
            "yu": halo(ref.at[inner, pl.ds(CY, 8)], ref.at[inner, pl.ds(0, 8)], base, halo_send, halo_recv, (s, r_up, c)),
            "yd": halo(ref.at[inner, pl.ds(8, 8)], ref.at[inner, pl.ds(CY + 8, 8)], base + 1, halo_send, halo_recv, (s, r_down, c)),
        }

    q_y = field_y(qq, 4)
    p_y = field_y(pp, 6)
    wrap = {
        "xu": halo(turned_face.at[1], turned_wrap, 0, wrap_send, wrap_recv, (s_up, r, c)),
        "xd": halo(turned_face.at[0], turned_wrap, 1, wrap_send, wrap_recv, (s_down, r, c)),
    }
    ask = {
        "xu": halo(cells_buf.at[0], cells_buf.at[1], 0, cell_send, cell_recv, (s_up, r, c)),
        "xd": halo(cells_buf.at[0], cells_buf.at[2], 1, cell_send, cell_recv, (s_down, r, c)),
    }
    reply = {
        "xu": halo(answer.at[1], answered.at[0], 0, answer_send, answer_recv, (s_up, r, c)),
        "xd": halo(answer.at[0], answered.at[1], 1, answer_send, answer_recv, (s_down, r, c)),
    }
    pq_z = {
        "zu": halo(zsend.at[pl.ds(8, 8)], zrecv.at[pl.ds(0, 8)], 8, halo_send, halo_recv, (s, r, c_up)),
        "zd": halo(zsend.at[pl.ds(0, 8)], zrecv.at[pl.ds(8, 8)], 9, halo_send, halo_recv, (s, r, c_down)),
    }
    lam_x = {
        "xu": halo(lam0.at[CX], lam0.at[0], 0, lam_send, lam_recv, (s_up, r, c)),
        "xd": halo(lam0.at[1], lam0.at[CX + 1], 1, lam_send, lam_recv, (s_down, r, c)),
    }
    lam_y = {
        "yu": halo(lam1.at[inner, pl.ds(CY, 8)], lam1.at[inner, pl.ds(0, 8)], 2, lam_send, lam_recv, (s, r_up, c)),
        "yd": halo(lam1.at[inner, pl.ds(8, 8)], lam1.at[inner, pl.ds(CY + 8, 8)], 3, lam_send, lam_recv, (s, r_down, c)),
    }
    lam_z = {
        "zu": halo(lsend.at[pl.ds(8, 8)], lrecv.at[pl.ds(0, 8)], 4, lam_send, lam_recv, (s, r, c_up)),
        "zd": halo(lsend.at[pl.ds(0, 8)], lrecv.at[pl.ds(8, 8)], 5, lam_send, lam_recv, (s, r, c_down)),
    }

    def start(faces):
        for side, copy in faces.items():
            pl.when(has[side])(copy.start)

    opposite = {"xu": "xd", "xd": "xu", "yu": "yd", "yd": "yu", "zu": "zd", "zd": "zu"}

    def arrive(faces):
        for side, copy in faces.items():
            pl.when(has[opposite[side]])(copy.wait_recv)

    def sent(faces):
        for side, copy in faces.items():
            pl.when(has[side])(copy.wait_send)

    start(pq_z)
    start(q_y)
    start(p_y)
    pl.when(near_up)(ask["xu"].start)
    pl.when(near_down)(ask["xd"].start)
    pl.when(wrap_up)(wrap["xu"].start)
    pl.when(wrap_down)(wrap["xd"].start)
    for k in range(NA - 1, 0, -1):
        slot_copy(k).start()

    y_at = lax.broadcasted_iota(jnp.int32, (CY, WALL), 0)
    for x in range(CX):
        where_hot[x * CY:(x + 1) * CY] = jnp.where(y_at + x * CY == own_xy, 1.0, 0.0).astype(BF16)
    own_hot_y[...] = hot_y_of(own_cells)
    for side in range(2):
        split_into(face_parts.at[side], turned_face[side, 0], turned_face[side, 1])
    prepare(0)

    phase = jnp.cos(0.5 * jnp.full((1, CZ), lax.rem(step_ref[0], 97).astype(F32), F32))
    for copy in loads[3:]:
        copy.wait()
    arrive(q_y)
    arrive(p_y)

    def along_x(ref, x):
        if x == 0:
            return ref[1, rows_of] * 0.5
        if x == CX - 1:
            return ref[CX - 2, rows_of] * -0.5
        return (ref[x + 1, rows_of] - ref[x - 1, rows_of]) * 0.5

    def along_y(ref, x):
        return (ref[x, pl.ds(9, CY)] - ref[x, pl.ds(7, CY)]) * 0.5

    at_z = lax.broadcasted_iota(jnp.int32, (CY, CZ), 1)

    def along_z(field):
        upper = jnp.where(at_z == CZ - 1, 0.0, pltpu.roll(field, CZ - 1, 1))
        lower = jnp.where(at_z == 0, 0.0, pltpu.roll(field, 1, 1))
        return (upper - lower) * 0.5

    for x in range(CX):
        here = slice(x * CY, (x + 1) * CY)
        total_0 = total[0, x] + along_x(qq, x)
        total_1 = total[1, x] + along_y(qq, x)
        total_2 = total[2, x] + along_z(qq[x, rows_of])
        total[0, x] = total_0
        total[1, x] = total_1
        total[2, x] = total_2
        moved_0 = vel[0, x] - 0.3 * along_x(pp, x) + drv[x] * phase
        moved_2 = vel[2, x] - 0.3 * along_z(pp[x, rows_of])
        sens = -(
            total_0 * moved_0 + total_1 * (vel[1, x] - 0.3 * along_y(pp, x)) + total_2 * moved_2
        )
        for i, piece in enumerate(pieces(sens.T)):
            sens_t[i * CZ:(i + 1) * CZ, here] = piece
        if x in (0, CX - 1):
            split_into(slot_parts.at[x // (CX - 1)], total_0.T, moved_0.T)
        for i, field in enumerate((total_2.T, moved_2.T)):
            ends[i:i + 1, here] = field[0:1]
            ends[2 + i:3 + i, here] = field[CZ - 1:CZ]

    def serve(side, at):
        cells = cells_buf[at]
        p_at, q_at = pick(face_parts.at[side], hot_y_of(cells), cells & (CZ - 1))
        answer[side, 0:1] = p_at
        answer[side, 1:2] = q_at

    @pl.when(near_up)
    def _():
        ask["xd"].wait_recv()
        serve(1, 2)
        reply["xu"].start()

    @pl.when(near_down)
    def _():
        ask["xu"].wait_recv()
        serve(0, 1)
        reply["xd"].start()

    pl.when(near_up)(q_x["xu"].start)
    pl.when(near_down)(q_x["xd"].start)

    on_face = [
        pick(slot_parts.at[side], where_hot[side * (CX - 1) * CY:(side * (CX - 1) + 1) * CY], own_z)
        for side in range(2)
    ]

    edge_parts = jnp.concatenate(pieces(ends[...]), axis=0)
    edge = jnp.dot(edge_parts, where_hot[...], preferred_element_type=F32)
    edge = edge[0:4] + edge[4:8] + edge[8:12]

    picked = jnp.dot(sens_t[...], where_hot[...], preferred_element_type=F32)
    picked = picked[0:CZ] + picked[CZ:2 * CZ] + picked[2 * CZ:3 * CZ]
    picked = jnp.sum(jnp.where(y_at == own_z, picked, 0.0), axis=0, keepdims=True)

    def corrected(value, side, here, total_at, moved_at, p_at, q_at):
        sign = 2.0 * side - 1.0
        more_total = jnp.where(here, q_at, 0.0) * (0.5 * sign)
        more_moved = jnp.where(here, p_at, 0.0) * (-0.15 * sign)
        return value - (more_total * (moved_at + more_moved) + total_at * more_moved)

    pl.when(near_down)(reply["xu"].wait_recv)
    pl.when(near_up)(reply["xd"].wait_recv)

    def own_answer(side):
        split_into(wrap_parts, turned_wrap[0], turned_wrap[1])
        p_at, q_at = pick(wrap_parts, own_hot_y[...], cells_buf[0] & (CZ - 1))
        answered[side, 0:1] = p_at
        answered[side, 1:2] = q_at

    @pl.when(wrap_down)
    def _():
        wrap["xu"].wait_recv()
        own_answer(0)

    @pl.when(wrap_up)
    def _():
        wrap["xd"].wait_recv()
        own_answer(1)

    for side, (total_at, moved_at) in enumerate(on_face):
        here = own_x == side * (CX - 1)
        picked = corrected(picked, side, here, total_at, moved_at, answered[side, 0:1], answered[side, 1:2])

    arrive(pq_z)
    z_parts = jnp.concatenate(pieces(zrecv[...]), axis=0)
    faces_z = jnp.dot(z_parts, own_hot_y[...], preferred_element_type=F32)
    faces_z = faces_z[0:16] + faces_z[16:32] + faces_z[32:48]
    row_x = lax.broadcasted_iota(jnp.int32, (16, WALL), 0) & (CX - 1)
    faces_z = jnp.where(row_x == own_x, faces_z, 0.0)
    for side in range(2):
        p_at = jnp.sum(faces_z[8 * side:8 * side + 4], axis=0, keepdims=True)
        q_at = jnp.sum(faces_z[8 * side + 4:8 * side + 8], axis=0, keepdims=True)
        here = own_z == side * (CZ - 1)
        picked = corrected(picked, side, here, edge[2 * side:2 * side + 1], edge[2 * side + 1:2 * side + 2], p_at, q_at)
    vals[0] = picked

    for k in range(NA - 1, 0, -1):
        pltpu.make_async_remote_copy(
            src_ref=vals.at[0], dst_ref=vals.at[k], send_sem=val_send, recv_sem=val_recv.at[k],
            device_id=plane_peer(k), device_id_type=MESH,
        ).start()

    pl.when(near_down)(q_x["xu"].wait_recv)
    pl.when(near_up)(q_x["xd"].wait_recv)

    @pl.when(wrap_down)
    def _():
        q_near[0] = turned_wrap[1].T

    @pl.when(wrap_up)
    def _():
        q_near[1] = turned_wrap[1].T

    edge_t = jnp.concatenate([zrecv[...], jnp.zeros((CZ - 16, CZ), F32)], axis=0).T

    def with_edges(field, low, high):
        field = jnp.where(at_z == CZ - 1, field + high * 0.5, field)
        return jnp.where(at_z == 0, field - low * 0.5, field)

    for x in range(CX):
        free = 1.0 - mask[x].astype(F32)
        total_0 = total[0, x]
        if x == 0:
            total_0 = total_0 - q_near[0] * 0.5
        if x == CX - 1:
            total_0 = total_0 + q_near[1] * 0.5
        lam0[x + 1] = free * total_0
        lam1[x, rows_of] = free * total[1, x]
        low, high = (edge_t[:, 8 * i + CX + x:8 * i + CX + x + 1] for i in range(2))
        lam2[x] = free * with_edges(total[2, x], low, high)

    start(lam_x)
    start(lam_y)
    for x in range(CX):
        turned = lam2[x].T
        lsend[x:x + 1] = turned[0:1]
        lsend[8 + x:9 + x] = turned[CZ - 1:CZ]
    start(lam_z)
    stores = [
        pltpu.make_async_copy(lam0.at[pl.ds(1, CX)], av_out.at[0], store_sem.at[0]),
        pltpu.make_async_copy(lam1.at[pl.ds(0, CX), rows_of], av_out.at[1], store_sem.at[1]),
        pltpu.make_async_copy(lam2, av_out.at[2], store_sem.at[2]),
    ]
    for copy in stores:
        copy.start()

    def slots_of(k, _):
        pltpu.make_async_copy(slots.at[k], slots.at[k], slot_recv.at[k]).wait()
        prepare(k)
        return 0

    rest = slots.at[pl.ds(1, NA - 1)]
    lax.fori_loop(1, NA, slots_of, 0)

    rest_vals = vals.at[pl.ds(1, NA - 1)]
    summed = None
    for low, high in zip(BATCHES[:-1], BATCHES[1:]):
        for k in range(max(low, 1), high):
            pltpu.make_async_copy(vals.at[k], vals.at[k], val_recv.at[k]).wait()
        split = [pieces(weight[k] * vals[k])[:2] for k in range(low, high)]
        scaled = jnp.concatenate(
            [jnp.concatenate([one[i] for one in split], axis=1) for i in range(2)], axis=0
        )
        product = lax.dot_general(
            hot[:, low * WALL:high * WALL], scaled, (((1,), (1,)), ((), ())), preferred_element_type=F32
        )
        summed = product if summed is None else summed + product
    summed = sum(summed[:, i * ANG:(i + 1) * ANG] for i in range(1, 2)) + summed[:, 0:ANG]
    packed = jnp.concatenate([summed[0:WIDTH // 2], summed[WIDTH // 2:WIDTH]], axis=1)
    dense[...] = packed.reshape(NB, OWN // 2, 2 * ANG)

    for k in LINE:
        other_zl, other_r, other_zh = line_place(k)
        pltpu.make_async_remote_copy(
            src_ref=dense.at[(other_zl * 2 + other_r) * ZH + other_zh], dst_ref=parts.at[k - 1],
            send_sem=part_send, recv_sem=part_recv, device_id=line_peer(k), device_id_type=MESH,
        ).start()

    for faces in (lam_x, lam_y, lam_z):
        arrive(faces)
    edge_l = jnp.concatenate([lrecv[...], jnp.zeros((CZ - 16, CZ), F32)], axis=0).T
    for x in range(CX):
        div = (
            (lam0[x + 2] - lam0[x]) * 0.5
            + (lam1[x, pl.ds(9, CY)] - lam1[x, pl.ds(7, CY)]) * 0.5
            + with_edges(along_z(lam2[x]), edge_l[:, x:x + 1], edge_l[:, 8 + x:9 + x])
        )
        apo[x] = ap[x] + 0.3 * div
    last = pltpu.make_async_copy(apo, ap_out, store_sem.at[3])
    last.start()

    pltpu.make_async_copy(parts, parts, part_recv).wait()
    own = dense[b] + jnp.sum(parts[...], axis=0)
    grad_out[...] = jnp.concatenate([own[:, 0:ANG], own[:, ANG:2 * ANG]], axis=0)

    for faces in (q_y, p_y, pq_z, lam_x, lam_y, lam_z):
        sent(faces)
    pl.when(wrap_up)(wrap["xu"].wait_send)
    pl.when(wrap_down)(wrap["xd"].wait_send)
    for faces in (ask, reply, q_x):
        pl.when(near_up)(faces["xu"].wait_send)
        pl.when(near_down)(faces["xd"].wait_send)
    pltpu.make_async_copy(rest, rest, slot_send).wait()
    pltpu.make_async_copy(rest_vals, rest_vals, val_send).wait()
    pltpu.make_async_copy(parts, parts, part_send).wait()
    for copy in stores + [last]:
        copy.wait()


def written(outs):
    anyspace = pl.BlockSpec(memory_space=pl.ANY)
    return pl.pallas_call(
        hand_over,
        out_shape=tuple(jax.ShapeDtypeStruct(o.shape, o.dtype) for o in outs),
        in_specs=[anyspace] * 3,
        out_specs=(anyspace,) * 3,
        scratch_shapes=[pltpu.SemaphoreType.DMA((3,))],
        compiler_params=pltpu.CompilerParams(vmem_limit_bytes=1024 * 1024),
    )(*outs)


def hand_over(adj_p, adj_v, grad, adj_p_out, adj_v_out, grad_out, sem):
    pairs = ((adj_v, adj_v_out), (adj_p, adj_p_out), (grad, grad_out))
    copies = [pltpu.make_async_copy(a, b, sem.at[i]) for i, (a, b) in enumerate(pairs)]
    for copy in copies:
        copy.start()
    for copy in copies:
        copy.wait()


def local(ns, nr, nc, *args):
    hbm = pl.BlockSpec(memory_space=pltpu.HBM)
    vmem = pl.BlockSpec(memory_space=pltpu.VMEM)
    block = (CX, CY, CZ)
    dma = pltpu.SemaphoreType.DMA
    return written(pl.pallas_call(
        functools.partial(kernel, ns, nr, nc),
        out_shape=(
            pltpu.VMEM(block, F32),
            pltpu.VMEM((3,) + block, F32),
            pltpu.VMEM((OWN, ANG), F32),
        ),
        in_specs=[hbm] * 12,
        out_specs=(pl.BlockSpec(memory_space=pl.ANY), pl.BlockSpec(memory_space=pl.ANY), vmem),
        scratch_shapes=[
            pltpu.VMEM((1, 1, 1, WALL), jnp.int32),
            pltpu.VMEM((1, 1, 1, WALL), jnp.int32),
            pltpu.VMEM((1, 1, 1, WALL), F32),
            pltpu.SMEM((1, 1, 1), jnp.int32),
            pltpu.SMEM((1,), jnp.int32),
            pltpu.VMEM((CX, CY + 16, CZ), F32),
            pltpu.VMEM((CX, CY + 16, CZ), F32),
            pltpu.VMEM(block, F32),
            pltpu.VMEM(block, F32),
            pltpu.VMEM(block, F32),
            pltpu.VMEM((3,) + block, F32),
            pltpu.VMEM((3,) + block, F32),
            pltpu.VMEM(block, jnp.int32),
            pltpu.VMEM((CX + 2, CY, CZ), F32),
            pltpu.VMEM((CX, CY + 16, CZ), F32),
            pltpu.VMEM(block, F32),
            pltpu.VMEM(block, F32),
            pltpu.VMEM((2, CY, CZ), F32),
            pltpu.VMEM((16, CY), F32),
            pltpu.VMEM((16, CY), F32),
            pltpu.VMEM((16, CY), F32),
            pltpu.VMEM((16, CY), F32),
            pltpu.VMEM((2, 2, CZ, CY), F32),
            pltpu.VMEM((2, CZ, CY), F32),
            pltpu.VMEM((2, 6 * CZ, CY), BF16),
            pltpu.VMEM((6 * CZ, CY), BF16),
            pltpu.VMEM((2, 6 * CZ, CY), BF16),
            pltpu.VMEM((3, 1, WALL), jnp.int32),
            pltpu.VMEM((2, 2, WALL), F32),
            pltpu.VMEM((2, 2, WALL), F32),
            pltpu.VMEM((4, CX * CY), F32),
            pltpu.VMEM((CY, WALL), BF16),
            pltpu.VMEM((NA, 2, WALL), F32),
            pltpu.VMEM((NA, 1, WALL), F32),
            pltpu.VMEM((WIDTH, NA * WALL), BF16),
            pltpu.VMEM((NA, ANG, WALL), F32),
            pltpu.VMEM((CX * CY, WALL), BF16),
            pltpu.VMEM((3 * CZ, CX * CY), BF16),
            pltpu.VMEM((NB, OWN // 2, 2 * ANG), F32),
            pltpu.VMEM((NB - 1, OWN // 2, 2 * ANG), F32),
            dma((5,)), dma((7,)), dma((4,)), dma((10,)), dma((10,)), dma((6,)), dma((6,)),
            dma((2,)), dma((2,)), dma((2,)), dma((2,)), dma((2,)), dma((2,)),
            dma, dma((NA,)), dma, dma((NA,)), dma, dma,
        ],
        compiler_params=pltpu.CompilerParams(
            collective_id=0, has_side_effects=True, vmem_limit_bytes=62 * 1024 * 1024 + 512 * 1024
        ),
        cost_estimate=pl.CostEstimate(flops=10**9, bytes_accessed=4 * 10**6, transcendentals=0),
    )(*args))


def solution(mesh):
    names = ("slab", "row", "col")
    sizes = tuple(mesh.shape[name] for name in names)
    cells = P(*names)
    vector = P(None, *names)
    slot = P(*names, None)
    in_specs = (cells, vector, cells, cells, cells, vector, cells, slot, slot, slot, cells, P())
    out_specs = (cells, vector, P(names, None))
    return jax.shard_map(
        functools.partial(local, *sizes), mesh=mesh, in_specs=in_specs, out_specs=out_specs, check_vma=False
    )
```

```python
import functools

import jax
import jax.numpy as jnp
from jax import lax
from jax.experimental import pallas as pl
from jax.experimental.pallas import tpu as pltpu
from jax.sharding import PartitionSpec as P

ANG = 64
CX = 4
CY = 128
CZ = 128
WALL = 512
OWN = 8
NXC = 4
NYC = 4
ZL = 4
ZH = 2
NA = NXC * NYC
NB = 2 * ZL * ZH
WIDTH = NB * OWN
BATCHES = (0, 5, 11, 16)
LINE = sorted(range(1, 16), key=lambda k: (-(k & 1), abs((k >> 2) - 2), k))
MESH = pl.DeviceIdType.MESH
PLANE = sorted(
    ((dy, dx) for dy in range(NYC) for dx in range(NXC)),
    key=lambda d: (min(d[0], NYC - d[0]) + min(d[1], NXC - d[1]), d),
)
F32 = jnp.float32
BF16 = jnp.bfloat16


def pieces(value):
    high = value.astype(BF16)
    rest = value - high.astype(F32)
    mid = rest.astype(BF16)
    low = (rest - mid.astype(F32)).astype(BF16)
    return high, mid, low


def kernel(
    ns, nr, nc,
    p_in, v_in, kap_in, drv_in, ap_in, av_in, mask_in, cells_in, rows_in, angle_in, count_in, step_in,
    ap_out, av_out, grad_out,
    cells_ref, rows_ref, angle_ref, count_ref, step_ref,
    pp, qq, kap, drv, ap, vel, total, mask,
    lam0, lam1, lam2, apo, q_near,
    zsend, zrecv, lsend, lrecv,
    turned_face, turned_wrap, face_parts, wrap_parts, slot_parts,
    cells_buf, answer, answered,
    ends, own_hot_y,
    slots, vals, hot, weight, where_hot, sens_t, dense, parts,
    small_sem, load_sem, store_sem, halo_send, halo_recv, lam_send, lam_recv,
    wrap_send, wrap_recv, cell_send, cell_recv, answer_send, answer_recv,
    slot_send, slot_recv, val_send, val_recv, part_send, part_recv,
):
    s = lax.axis_index("slab")
    r = lax.axis_index("row")
    c = lax.axis_index("col")
    y, zl = s >> 2, s & (ZL - 1)
    x_at, zh = c >> 1, c & (ZH - 1)
    group = y * NXC + x_at
    b = (zl * 2 + r) * ZH + zh

    def plane_peer(k):
        dy, dx = PLANE[k]
        return (((y + dy) & (NYC - 1)) * ZL + zl, r, ((x_at + dx) & (NXC - 1)) * ZH + zh)

    def line_place(k):
        return (zl + (k >> 2)) & (ZL - 1), r ^ ((k >> 1) & 1), zh ^ (k & 1)

    def line_peer(k):
        other_zl, other_r, other_zh = line_place(k)
        return (y * ZL + other_zl, other_r, x_at * ZH + other_zh)

    plane = jnp.zeros((CY, CZ), F32)
    strip = jnp.zeros((8, CZ), F32)
    for ref in (pp, qq, lam1):
        for x in range(CX):
            ref[x, pl.ds(0, 8)] = strip
            ref[x, pl.ds(CY + 8, 8)] = strip
    for ref in (q_near, ):
        ref[0] = plane
        ref[1] = plane
    lam0[0] = plane
    lam0[CX + 1] = plane
    zrecv[...] = jnp.zeros_like(zrecv)
    lrecv[...] = jnp.zeros_like(lrecv)
    answered[...] = jnp.zeros_like(answered)

    barrier = pltpu.get_barrier_semaphore()

    def greet(device):
        pl.semaphore_signal(barrier, inc=1, device_id=device, device_id_type=MESH)

    s_up, s_down = jnp.minimum(s + 1, ns - 1), jnp.maximum(s - 1, 0)
    r_up, r_down = jnp.minimum(r + 1, nr - 1), jnp.maximum(r - 1, 0)
    c_up, c_down = jnp.minimum(c + 1, nc - 1), jnp.maximum(c - 1, 0)
    has = {
        "xu": s < ns - 1, "xd": s > 0, "yu": r < nr - 1, "yd": r > 0, "zu": c < nc - 1, "zd": c > 0,
    }
    wrap_up = jnp.logical_and(zl == ZL - 1, has["xu"])
    wrap_down = jnp.logical_and(zl == 0, has["xd"])
    near_up = zl < ZL - 1
    near_down = zl > 0
    beyond = (
        (jnp.logical_and(zh == ZH - 1, has["zu"]), (s, r, c_up)),
        (jnp.logical_and(zh == 0, has["zd"]), (s, r, c_down)),
        (wrap_up, (s_up, r, c)),
        (wrap_down, (s_down, r, c)),
    )
    partners = NA - 1 + NB - 1
    for here, device in beyond:
        pl.when(here)(functools.partial(greet, device))
        partners = partners + here.astype(jnp.int32)
    for k in range(NA - 1, 0, -1):
        greet(plane_peer(k))
    for k in LINE:
        greet(line_peer(k))

    loads = [
        pltpu.make_async_copy(kap_in, kap, load_sem.at[0]),
        pltpu.make_async_copy(ap_in, ap, load_sem.at[1]),
        pltpu.make_async_copy(p_in, pp.at[pl.ds(0, CX), pl.ds(8, CY)], load_sem.at[2]),
        pltpu.make_async_copy(av_in, total, load_sem.at[3]),
        pltpu.make_async_copy(mask_in, mask, load_sem.at[4]),
        pltpu.make_async_copy(v_in, vel, load_sem.at[5]),
        pltpu.make_async_copy(drv_in, drv, load_sem.at[6]),
    ]
    small = [
        pltpu.make_async_copy(rows_in, rows_ref, small_sem.at[0]),
        pltpu.make_async_copy(angle_in, angle_ref, small_sem.at[1]),
        pltpu.make_async_copy(count_in, count_ref, small_sem.at[2]),
        pltpu.make_async_copy(cells_in, cells_ref, small_sem.at[3]),
        pltpu.make_async_copy(step_in, step_ref, small_sem.at[4]),
    ]
    for copy in small + loads:
        copy.start()

    lane = lax.broadcasted_iota(jnp.int32, (1, WALL), 1)
    for copy in small:
        copy.wait()
    own_rows = rows_ref[0, 0]
    live = lane < count_ref[0, 0, 0]
    bits = own_rows >> 3
    owner_group = ((bits >> 6) << 2) + ((bits >> 1) & 3)
    owner_line = (((bits >> 4) & 3) << 2) + (((bits >> 3) & 1) << 1) + (bits & 1)
    half = (own_rows >> 2) & 1
    code = owner_group * WIDTH + half * (WIDTH // 2) + owner_line * (OWN // 2) + (own_rows & (OWN // 2 - 1))
    slots[0, 0:1] = jnp.where(live, code.astype(F32), -1.0)
    slots[0, 1:2] = angle_ref[0, 0]
    row_at = (lax.broadcasted_iota(jnp.int32, (WIDTH, WALL), 0) + group * WIDTH).astype(F32)
    knots = lax.broadcasted_iota(jnp.int32, (ANG, WALL), 0).astype(F32)

    def at_slots(k):
        return pl.ds(pl.multiple_of(k * WALL, WALL), WALL)

    def prepare(k):
        hot[:, at_slots(k)] = jnp.where(slots[k, 0:1] == row_at, 1.0, 0.0).astype(BF16)
        dist = jnp.abs(slots[k, 1:2] - knots)
        dist = jnp.minimum(dist, ANG - dist)
        outer = jnp.maximum(2.0 - dist, 0.0)
        near = jnp.maximum(1.0 - dist, 0.0)
        weight[k] = (outer * outer * outer - 4.0 * near * near * near) * (1.0 / 6.0)


    own_cells = cells_ref[0, 0]
    cells_buf[0] = own_cells
    own_xy = own_cells >> 7
    own_x = own_cells >> 14
    own_z = own_cells & (CZ - 1)

    loads[0].wait()
    loads[1].wait()
    rows_of = pl.ds(8, CY)
    for x in range(CX):
        qq[x, rows_of] = kap[x] * ap[x]
    loads[2].wait()
    for i, (ref, at) in enumerate(((pp, 0), (qq, CX))):
        for x in range(CX):
            turned = ref[x, rows_of].T
            zsend[at + x:at + x + 1] = turned[0:1]
            zsend[8 + at + x:8 + at + x + 1] = turned[CZ - 1:CZ]
            if x in (0, CX - 1):
                turned_face[x // (CX - 1), i] = turned

    picks = 2

    def split_into(ref, first, second):
        for i, field in enumerate((first, second)):
            for j, piece in enumerate(pieces(field)[:picks]):
                ref[(picks * i + j) * CZ:(picks * i + j + 1) * CZ] = piece

    y_at = lax.broadcasted_iota(jnp.int32, (CY, WALL), 0)

    def pick(ref, hot_y, at_z):
        got = jnp.dot(ref[0:2 * picks * CZ], hot_y, preferred_element_type=F32)
        out = []
        for i in range(2):
            field = got[picks * i * CZ:(picks * i + 1) * CZ]
            for j in range(1, picks):
                field = field + got[(picks * i + j) * CZ:(picks * i + j + 1) * CZ]
            out.append(jnp.sum(jnp.where(y_at == at_z, field, 0.0), axis=0, keepdims=True))
        return out

    def hot_y_of(cells):
        return jnp.where(y_at == ((cells >> 7) & (CY - 1)), 1.0, 0.0).astype(BF16)


    for x in range(CX):
        where_hot[x * CY:(x + 1) * CY] = jnp.where(y_at + x * CY == own_xy, 1.0, 0.0).astype(BF16)
    own_hot_y[...] = hot_y_of(own_cells)
    for side in range(2):
        split_into(face_parts.at[side], turned_face[side, 0], turned_face[side, 1])
    prepare(0)

    pl.semaphore_wait(barrier, partners)

    def slot_copy(k):
        return pltpu.make_async_remote_copy(
            src_ref=slots.at[0], dst_ref=slots.at[k],
            send_sem=slot_send, recv_sem=slot_recv.at[k],
            device_id=plane_peer(k), device_id_type=MESH,
        )

    def halo(src, dst, sem_at, send_sem, recv_sem, device):
        return pltpu.make_async_remote_copy(
            src_ref=src, dst_ref=dst, send_sem=send_sem.at[sem_at], recv_sem=recv_sem.at[sem_at],
            device_id=device, device_id_type=MESH,
        )


    inner = pl.ds(0, CX)
    q_x = {
        "xu": halo(qq.at[CX - 1, rows_of], q_near.at[0], 0, halo_send, halo_recv, (s_up, r, c)),
        "xd": halo(qq.at[0, rows_of], q_near.at[1], 1, halo_send, halo_recv, (s_down, r, c)),
    }

    def field_y(ref, base):
        return {
            "yu": halo(ref.at[inner, pl.ds(CY, 8)], ref.at[inner, pl.ds(0, 8)], base, halo_send, halo_recv, (s, r_up, c)),
            "yd": halo(ref.at[inner, pl.ds(8, 8)], ref.at[inner, pl.ds(CY + 8, 8)], base + 1, halo_send, halo_recv, (s, r_down, c)),
        }

    q_y = field_y(qq, 4)
    p_y = field_y(pp, 6)
    wrap = {
        "xu": halo(turned_face.at[1], turned_wrap, 0, wrap_send, wrap_recv, (s_up, r, c)),
        "xd": halo(turned_face.at[0], turned_wrap, 1, wrap_send, wrap_recv, (s_down, r, c)),
    }
    ask = {
        "xu": halo(cells_buf.at[0], cells_buf.at[1], 0, cell_send, cell_recv, (s_up, r, c)),
        "xd": halo(cells_buf.at[0], cells_buf.at[2], 1, cell_send, cell_recv, (s_down, r, c)),
    }
    reply = {
        "xu": halo(answer.at[1], answered.at[0], 0, answer_send, answer_recv, (s_up, r, c)),
        "xd": halo(answer.at[0], answered.at[1], 1, answer_send, answer_recv, (s_down, r, c)),
    }
    pq_z = {
        "zu": halo(zsend.at[pl.ds(8, 8)], zrecv.at[pl.ds(0, 8)], 8, halo_send, halo_recv, (s, r, c_up)),
        "zd": halo(zsend.at[pl.ds(0, 8)], zrecv.at[pl.ds(8, 8)], 9, halo_send, halo_recv, (s, r, c_down)),
    }
    lam_x = {
        "xu": halo(lam0.at[CX], lam0.at[0], 0, lam_send, lam_recv, (s_up, r, c)),
        "xd": halo(lam0.at[1], lam0.at[CX + 1], 1, lam_send, lam_recv, (s_down, r, c)),
    }
    lam_y = {
        "yu": halo(lam1.at[inner, pl.ds(CY, 8)], lam1.at[inner, pl.ds(0, 8)], 2, lam_send, lam_recv, (s, r_up, c)),
        "yd": halo(lam1.at[inner, pl.ds(8, 8)], lam1.at[inner, pl.ds(CY + 8, 8)], 3, lam_send, lam_recv, (s, r_down, c)),
    }
    lam_z = {
        "zu": halo(lsend.at[pl.ds(8, 8)], lrecv.at[pl.ds(0, 8)], 4, lam_send, lam_recv, (s, r, c_up)),
        "zd": halo(lsend.at[pl.ds(0, 8)], lrecv.at[pl.ds(8, 8)], 5, lam_send, lam_recv, (s, r, c_down)),
    }

    def start(faces):
        for side, copy in faces.items():
            pl.when(has[side])(copy.start)

    opposite = {"xu": "xd", "xd": "xu", "yu": "yd", "yd": "yu", "zu": "zd", "zd": "zu"}

    def arrive(faces):
        for side, copy in faces.items():
            pl.when(has[opposite[side]])(copy.wait_recv)

    def sent(faces):
        for side, copy in faces.items():
            pl.when(has[side])(copy.wait_send)

    start(pq_z)
    start(q_y)
    start(p_y)
    pl.when(near_up)(ask["xu"].start)
    pl.when(near_down)(ask["xd"].start)
    pl.when(wrap_up)(wrap["xu"].start)
    pl.when(wrap_down)(wrap["xd"].start)
    for k in range(NA - 1, 0, -1):
        slot_copy(k).start()


    phase = jnp.cos(0.5 * jnp.full((1, CZ), lax.rem(step_ref[0], 97).astype(F32), F32))
    for copy in loads[3:]:
        copy.wait()
    arrive(q_y)
    arrive(p_y)

    def along_x(ref, x):
        if x == 0:
            return ref[1, rows_of] * 0.5
        if x == CX - 1:
            return ref[CX - 2, rows_of] * -0.5
        return (ref[x + 1, rows_of] - ref[x - 1, rows_of]) * 0.5

    def along_y(ref, x):
        return (ref[x, pl.ds(9, CY)] - ref[x, pl.ds(7, CY)]) * 0.5

    at_z = lax.broadcasted_iota(jnp.int32, (CY, CZ), 1)

    def along_z(field):
        upper = jnp.where(at_z == CZ - 1, 0.0, pltpu.roll(field, CZ - 1, 1))
        lower = jnp.where(at_z == 0, 0.0, pltpu.roll(field, 1, 1))
        return (upper - lower) * 0.5

    for x in range(CX):
        here = slice(x * CY, (x + 1) * CY)
        total_0 = total[0, x] + along_x(qq, x)
        total_1 = total[1, x] + along_y(qq, x)
        total_2 = total[2, x] + along_z(qq[x, rows_of])
        total[0, x] = total_0
        total[1, x] = total_1
        total[2, x] = total_2
        moved_0 = vel[0, x] - 0.3 * along_x(pp, x) + drv[x] * phase
        moved_2 = vel[2, x] - 0.3 * along_z(pp[x, rows_of])
        sens = -(
            total_0 * moved_0 + total_1 * (vel[1, x] - 0.3 * along_y(pp, x)) + total_2 * moved_2
        )
        for i, piece in enumerate(pieces(sens.T)):
            sens_t[i * CZ:(i + 1) * CZ, here] = piece
        if x in (0, CX - 1):
            split_into(slot_parts.at[x // (CX - 1)], total_0.T, moved_0.T)
        for i, field in enumerate((total_2.T, moved_2.T)):
            ends[i:i + 1, here] = field[0:1]
            ends[2 + i:3 + i, here] = field[CZ - 1:CZ]

    def serve(side, at):
        cells = cells_buf[at]
        p_at, q_at = pick(face_parts.at[side], hot_y_of(cells), cells & (CZ - 1))
        answer[side, 0:1] = p_at
        answer[side, 1:2] = q_at

    @pl.when(near_up)
    def _():
        ask["xd"].wait_recv()
        serve(1, 2)
        reply["xu"].start()

    @pl.when(near_down)
    def _():
        ask["xu"].wait_recv()
        serve(0, 1)
        reply["xd"].start()

    pl.when(near_up)(q_x["xu"].start)
    pl.when(near_down)(q_x["xd"].start)

    on_face = [
        pick(slot_parts.at[side], where_hot[side * (CX - 1) * CY:(side * (CX - 1) + 1) * CY], own_z)
        for side in range(2)
    ]

    edge_parts = jnp.concatenate(pieces(ends[...]), axis=0)
    edge = jnp.dot(edge_parts, where_hot[...], preferred_element_type=F32)
    edge = edge[0:4] + edge[4:8] + edge[8:12]

    def slots_of(k, _):
        pltpu.make_async_copy(slots.at[k], slots.at[k], slot_recv.at[k]).wait()
        prepare(k)
        return 0

    lax.fori_loop(1, BATCHES[1], slots_of, 0)

    picked = jnp.dot(sens_t[...], where_hot[...], preferred_element_type=F32)
    picked = picked[0:CZ] + picked[CZ:2 * CZ] + picked[2 * CZ:3 * CZ]
    picked = jnp.sum(jnp.where(y_at == own_z, picked, 0.0), axis=0, keepdims=True)

    def corrected(value, side, here, total_at, moved_at, p_at, q_at):
        sign = 2.0 * side - 1.0
        more_total = jnp.where(here, q_at, 0.0) * (0.5 * sign)
        more_moved = jnp.where(here, p_at, 0.0) * (-0.15 * sign)
        return value - (more_total * (moved_at + more_moved) + total_at * more_moved)

    pl.when(near_down)(reply["xu"].wait_recv)
    pl.when(near_up)(reply["xd"].wait_recv)

    def own_answer(side):
        split_into(wrap_parts, turned_wrap[0], turned_wrap[1])
        p_at, q_at = pick(wrap_parts, own_hot_y[...], cells_buf[0] & (CZ - 1))
        answered[side, 0:1] = p_at
        answered[side, 1:2] = q_at

    @pl.when(wrap_down)
    def _():
        wrap["xu"].wait_recv()
        own_answer(0)

    @pl.when(wrap_up)
    def _():
        wrap["xd"].wait_recv()
        own_answer(1)

    for side, (total_at, moved_at) in enumerate(on_face):
        here = own_x == side * (CX - 1)
        picked = corrected(picked, side, here, total_at, moved_at, answered[side, 0:1], answered[side, 1:2])

    arrive(pq_z)
    z_parts = jnp.concatenate(pieces(zrecv[...]), axis=0)
    faces_z = jnp.dot(z_parts, own_hot_y[...], preferred_element_type=F32)
    faces_z = faces_z[0:16] + faces_z[16:32] + faces_z[32:48]
    row_x = lax.broadcasted_iota(jnp.int32, (16, WALL), 0) & (CX - 1)
    faces_z = jnp.where(row_x == own_x, faces_z, 0.0)
    for side in range(2):
        p_at = jnp.sum(faces_z[8 * side:8 * side + 4], axis=0, keepdims=True)
        q_at = jnp.sum(faces_z[8 * side + 4:8 * side + 8], axis=0, keepdims=True)
        here = own_z == side * (CZ - 1)
        picked = corrected(picked, side, here, edge[2 * side:2 * side + 1], edge[2 * side + 1:2 * side + 2], p_at, q_at)
    vals[0] = picked

    for k in range(NA - 1, 0, -1):
        pltpu.make_async_remote_copy(
            src_ref=vals.at[0], dst_ref=vals.at[k], send_sem=val_send, recv_sem=val_recv.at[k],
            device_id=plane_peer(k), device_id_type=MESH,
        ).start()

    pl.when(near_down)(q_x["xu"].wait_recv)
    pl.when(near_up)(q_x["xd"].wait_recv)

    @pl.when(wrap_down)
    def _():
        q_near[0] = turned_wrap[1].T

    @pl.when(wrap_up)
    def _():
        q_near[1] = turned_wrap[1].T

    edge_t = jnp.concatenate([zrecv[...], jnp.zeros((CZ - 16, CZ), F32)], axis=0).T

    def with_edges(field, low, high):
        field = jnp.where(at_z == CZ - 1, field + high * 0.5, field)
        return jnp.where(at_z == 0, field - low * 0.5, field)

    for x in range(CX):
        free = 1.0 - mask[x].astype(F32)
        total_0 = total[0, x]
        if x == 0:
            total_0 = total_0 - q_near[0] * 0.5
        if x == CX - 1:
            total_0 = total_0 + q_near[1] * 0.5
        lam0[x + 1] = free * total_0
        lam1[x, rows_of] = free * total[1, x]
        low, high = (edge_t[:, 8 * i + CX + x:8 * i + CX + x + 1] for i in range(2))
        lam2[x] = free * with_edges(total[2, x], low, high)

    start(lam_x)
    start(lam_y)
    for x in range(CX):
        turned = lam2[x].T
        lsend[x:x + 1] = turned[0:1]
        lsend[8 + x:9 + x] = turned[CZ - 1:CZ]
    start(lam_z)
    stores = [
        pltpu.make_async_copy(lam0.at[pl.ds(1, CX)], av_out.at[0], store_sem.at[0]),
        pltpu.make_async_copy(lam1.at[pl.ds(0, CX), rows_of], av_out.at[1], store_sem.at[1]),
        pltpu.make_async_copy(lam2, av_out.at[2], store_sem.at[2]),
    ]
    for copy in stores:
        copy.start()

    rest = slots.at[pl.ds(1, NA - 1)]
    lax.fori_loop(BATCHES[1], NA, slots_of, 0)

    rest_vals = vals.at[pl.ds(1, NA - 1)]
    summed = None
    for low, high in zip(BATCHES[:-1], BATCHES[1:]):
        for k in range(max(low, 1), high):
            pltpu.make_async_copy(vals.at[k], vals.at[k], val_recv.at[k]).wait()
        split = [pieces(weight[k] * vals[k])[:2] for k in range(low, high)]
        scaled = jnp.concatenate(
            [jnp.concatenate([one[i] for one in split], axis=1) for i in range(2)], axis=0
        )
        product = lax.dot_general(
            hot[:, low * WALL:high * WALL], scaled, (((1,), (1,)), ((), ())), preferred_element_type=F32
        )
        summed = product if summed is None else summed + product
    summed = sum(summed[:, i * ANG:(i + 1) * ANG] for i in range(1, 2)) + summed[:, 0:ANG]
    packed = jnp.concatenate([summed[0:WIDTH // 2], summed[WIDTH // 2:WIDTH]], axis=1)
    dense[...] = packed.reshape(NB, OWN // 2, 2 * ANG)

    for k in LINE:
        other_zl, other_r, other_zh = line_place(k)
        pltpu.make_async_remote_copy(
            src_ref=dense.at[(other_zl * 2 + other_r) * ZH + other_zh], dst_ref=parts.at[k - 1],
            send_sem=part_send, recv_sem=part_recv, device_id=line_peer(k), device_id_type=MESH,
        ).start()

    for faces in (lam_x, lam_y, lam_z):
        arrive(faces)
    edge_l = jnp.concatenate([lrecv[...], jnp.zeros((CZ - 16, CZ), F32)], axis=0).T
    for x in range(CX):
        div = (
            (lam0[x + 2] - lam0[x]) * 0.5
            + (lam1[x, pl.ds(9, CY)] - lam1[x, pl.ds(7, CY)]) * 0.5
            + with_edges(along_z(lam2[x]), edge_l[:, x:x + 1], edge_l[:, 8 + x:9 + x])
        )
        apo[x] = ap[x] + 0.3 * div
    last = pltpu.make_async_copy(apo, ap_out, store_sem.at[3])
    last.start()

    pltpu.make_async_copy(parts, parts, part_recv).wait()
    own = dense[b] + jnp.sum(parts[...], axis=0)
    grad_out[...] = jnp.concatenate([own[:, 0:ANG], own[:, ANG:2 * ANG]], axis=0)

    for faces in (q_y, p_y, pq_z, lam_x, lam_y, lam_z):
        sent(faces)
    pl.when(wrap_up)(wrap["xu"].wait_send)
    pl.when(wrap_down)(wrap["xd"].wait_send)
    for faces in (ask, reply, q_x):
        pl.when(near_up)(faces["xu"].wait_send)
        pl.when(near_down)(faces["xd"].wait_send)
    pltpu.make_async_copy(rest, rest, slot_send).wait()
    pltpu.make_async_copy(rest_vals, rest_vals, val_send).wait()
    pltpu.make_async_copy(parts, parts, part_send).wait()
    for copy in stores + [last]:
        copy.wait()


def written(outs):
    anyspace = pl.BlockSpec(memory_space=pl.ANY)
    return pl.pallas_call(
        hand_over,
        out_shape=tuple(jax.ShapeDtypeStruct(o.shape, o.dtype) for o in outs),
        in_specs=[anyspace] * 3,
        out_specs=(anyspace,) * 3,
        scratch_shapes=[pltpu.SemaphoreType.DMA((3,))],
        compiler_params=pltpu.CompilerParams(vmem_limit_bytes=1024 * 1024),
    )(*outs)


def hand_over(adj_p, adj_v, grad, adj_p_out, adj_v_out, grad_out, sem):
    pairs = ((adj_v, adj_v_out), (adj_p, adj_p_out), (grad, grad_out))
    copies = [pltpu.make_async_copy(a, b, sem.at[i]) for i, (a, b) in enumerate(pairs)]
    for copy in copies:
        copy.start()
    for copy in copies:
        copy.wait()


def local(ns, nr, nc, *args):
    hbm = pl.BlockSpec(memory_space=pltpu.HBM)
    vmem = pl.BlockSpec(memory_space=pltpu.VMEM)
    block = (CX, CY, CZ)
    dma = pltpu.SemaphoreType.DMA
    return written(pl.pallas_call(
        functools.partial(kernel, ns, nr, nc),
        out_shape=(
            pltpu.VMEM(block, F32),
            pltpu.VMEM((3,) + block, F32),
            pltpu.VMEM((OWN, ANG), F32),
        ),
        in_specs=[hbm] * 12,
        out_specs=(pl.BlockSpec(memory_space=pl.ANY), pl.BlockSpec(memory_space=pl.ANY), vmem),
        scratch_shapes=[
            pltpu.VMEM((1, 1, 1, WALL), jnp.int32),
            pltpu.VMEM((1, 1, 1, WALL), jnp.int32),
            pltpu.VMEM((1, 1, 1, WALL), F32),
            pltpu.SMEM((1, 1, 1), jnp.int32),
            pltpu.SMEM((1,), jnp.int32),
            pltpu.VMEM((CX, CY + 16, CZ), F32),
            pltpu.VMEM((CX, CY + 16, CZ), F32),
            pltpu.VMEM(block, F32),
            pltpu.VMEM(block, F32),
            pltpu.VMEM(block, F32),
            pltpu.VMEM((3,) + block, F32),
            pltpu.VMEM((3,) + block, F32),
            pltpu.VMEM(block, jnp.int32),
            pltpu.VMEM((CX + 2, CY, CZ), F32),
            pltpu.VMEM((CX, CY + 16, CZ), F32),
            pltpu.VMEM(block, F32),
            pltpu.VMEM(block, F32),
            pltpu.VMEM((2, CY, CZ), F32),
            pltpu.VMEM((16, CY), F32),
            pltpu.VMEM((16, CY), F32),
            pltpu.VMEM((16, CY), F32),
            pltpu.VMEM((16, CY), F32),
            pltpu.VMEM((2, 2, CZ, CY), F32),
            pltpu.VMEM((2, CZ, CY), F32),
            pltpu.VMEM((2, 6 * CZ, CY), BF16),
            pltpu.VMEM((6 * CZ, CY), BF16),
            pltpu.VMEM((2, 6 * CZ, CY), BF16),
            pltpu.VMEM((3, 1, WALL), jnp.int32),
            pltpu.VMEM((2, 2, WALL), F32),
            pltpu.VMEM((2, 2, WALL), F32),
            pltpu.VMEM((4, CX * CY), F32),
            pltpu.VMEM((CY, WALL), BF16),
            pltpu.VMEM((NA, 2, WALL), F32),
            pltpu.VMEM((NA, 1, WALL), F32),
            pltpu.VMEM((WIDTH, NA * WALL), BF16),
            pltpu.VMEM((NA, ANG, WALL), F32),
            pltpu.VMEM((CX * CY, WALL), BF16),
            pltpu.VMEM((3 * CZ, CX * CY), BF16),
            pltpu.VMEM((NB, OWN // 2, 2 * ANG), F32),
            pltpu.VMEM((NB - 1, OWN // 2, 2 * ANG), F32),
            dma((5,)), dma((7,)), dma((4,)), dma((10,)), dma((10,)), dma((6,)), dma((6,)),
            dma((2,)), dma((2,)), dma((2,)), dma((2,)), dma((2,)), dma((2,)),
            dma, dma((NA,)), dma, dma((NA,)), dma, dma,
        ],
        compiler_params=pltpu.CompilerParams(
            collective_id=0, has_side_effects=True, vmem_limit_bytes=62 * 1024 * 1024 + 512 * 1024
        ),
        cost_estimate=pl.CostEstimate(flops=10**9, bytes_accessed=4 * 10**6, transcendentals=0),
    )(*args))


def solution(mesh):
    names = ("slab", "row", "col")
    sizes = tuple(mesh.shape[name] for name in names)
    cells = P(*names)
    vector = P(None, *names)
    slot = P(*names, None)
    in_specs = (cells, vector, cells, cells, cells, vector, cells, slot, slot, slot, cells, P())
    out_specs = (cells, vector, P(names, None))
    return jax.shard_map(
        functools.partial(local, *sizes), mesh=mesh, in_specs=in_specs, out_specs=out_specs, check_vma=False
    )
```
